256 devices in a mesh: tensor: 4 (over y), prompt: 16 (over x_lo, z), cand: 4 (over x_hi, core).
Axes of the slice: x: 4 (x_hi: 2, x_lo: 2; x = x_hi * 2 + x_lo), y: 4, z: 8, core: 2. Of those that a mesh axis runs over, the one named last changes fastest.
Arguments:
- q_step: bfloat16 [512, 2, 4096], P(('prompt', 'cand'), None, 'tensor')
- step_k: bfloat16 [512, 2, 512], P(('prompt', 'cand'), None, 'tensor')
- step_values: bfloat16 [512, 2, 512], P(('prompt', 'cand'), None, 'tensor'), may hold values from -6 to 6
- prefix_k: bfloat16 [32, 4096, 512], P('prompt', 'cand', 'tensor'), may hold values from -13 to 13
- prefix_v: bfloat16 [32, 4096, 512], P('prompt', 'cand', 'tensor'), may hold values from -6 to 6
- suffix_k: bfloat16 [512, 2048, 512], P(('prompt', 'cand'), None, 'tensor')
- suffix_values: bfloat16 [512, 2048, 512], P(('prompt', 'cand'), None, 'tensor'), may hold values from -6 to 6
- lengths: int32 [512], P(('prompt', 'cand')), may hold values from 256 to 2048, as said below
- placement: int32 [16, 32], P('prompt'), may hold values from 0 to 31, each once within a row
- output_weight: bfloat16 [4096, 8192], P(('tensor', 'cand')), may hold values from -0.5 to 0.5
Outputs:
- projected: bfloat16 [512, 2, 8192], P('prompt', None, ('tensor', 'cand'))
The draws below stay inside these ranges and needn't reach their ends.
Inputs may be any that keep to these rules, and one draw needn't show every extreme that they name: Each row is a permutation; the slot in column r of row p holds a candidate of prompt placement[p, r], so every prompt index holds 1 candidates of every prompt. `lengths`: some slot has exactly 2048 live positions and some slot exactly 256.
All inputs are finite; a program needn't handle non-finite values.
Results may differ from the reference program's by a relative error of at most 0.019.
Values may be sent and summed in bfloat16 or wider, within the bound.
No kernel may reach another device: no remote copies, remote signals or barrier semaphores. Data moves between devices by JAX's collectives and lax.ppermute only.
A program may use at most 128 MiB of HBM per device.

```python
import math
import jax
import jax.numpy as jnp
from jax import lax

MODEL_WIDTH = 8192
HEAD_WIDTH = 128
QUERY_HEADS = 32
KEY_VALUE_HEADS = 4
PREFIX = 4096
SUFFIX_LENGTH = 2048
LEAST_LIVE = 256
STEP_TOKENS = 2
PROMPTS = 32
CANDIDATE_SPREAD = 1
SLOTS_P = 32
SLOT_TOTAL = 512
N_PROMPT = 16


def shared_queries(key):
    return jax.random.normal(jax.random.fold_in(key, 101), (SLOT_TOTAL, STEP_TOKENS, QUERY_HEADS, HEAD_WIDTH), jnp.float32)


def shared_leading(key):
    return 2.2 * jax.random.normal(jax.random.fold_in(key, 102), (SLOT_TOTAL, 2, KEY_VALUE_HEADS, HEAD_WIDTH), jnp.float32)


def draw_q_step(key, part):
    query_rows = shared_queries(key)
    return query_rows.reshape(SLOT_TOTAL, STEP_TOKENS, QUERY_HEADS * HEAD_WIDTH).astype(jnp.bfloat16)


def draw_step_k(key, part):
    query_rows = shared_queries(key)
    key = jax.random.fold_in(key, 4)
    grouped_queries = jnp.mean(query_rows.reshape(SLOT_TOTAL, STEP_TOKENS, KEY_VALUE_HEADS, QUERY_HEADS // KEY_VALUE_HEADS, HEAD_WIDTH), axis=3)
    attract_scale = 8.5 * (QUERY_HEADS // KEY_VALUE_HEADS) / math.sqrt(HEAD_WIDTH)
    random_noise = jax.random.normal(key, (SLOT_TOTAL, STEP_TOKENS, KEY_VALUE_HEADS, HEAD_WIDTH), jnp.float32)
    return (attract_scale * grouped_queries + random_noise).reshape(SLOT_TOTAL, STEP_TOKENS, KEY_VALUE_HEADS * HEAD_WIDTH).astype(jnp.bfloat16)


def draw_suffix_k(key, part):
    leading_rows = shared_leading(key)
    key = jax.random.fold_in(key, 3)
    remaining_rows = 2.2 * jax.random.normal(key, (SLOT_TOTAL, SUFFIX_LENGTH - 2, KEY_VALUE_HEADS, HEAD_WIDTH), jnp.float32)
    return jnp.concatenate([leading_rows, remaining_rows], 1).reshape(SLOT_TOTAL, SUFFIX_LENGTH, KEY_VALUE_HEADS * HEAD_WIDTH).astype(jnp.bfloat16)


def draw_lengths(key, part):
    key = jax.random.fold_in(key, 21)
    random_key_first, random_key_second, random_key_third, random_key_fourth = jax.random.split(key, 4)
    spanned_length = jax.random.randint(random_key_first, (SLOT_TOTAL,), 0, SUFFIX_LENGTH - LEAST_LIVE + 1)
    softmax_divisor = jax.random.randint(random_key_second, (SLOT_TOTAL,), 1, 5)
    counts = LEAST_LIVE + spanned_length // softmax_divisor
    longest_length = jax.random.randint(random_key_third, (), 0, SLOT_TOTAL)
    shortest_length = (longest_length + 1 + jax.random.randint(random_key_fourth, (), 0, SLOT_TOTAL - 1)) % SLOT_TOTAL
    counts = counts.at[longest_length].set(SUFFIX_LENGTH).at[shortest_length].set(LEAST_LIVE)
    return counts.astype(jnp.int32)


def with_spikes(result, rng, source, target, shards_of, factor):
    owner, partner = [(jnp.arange(result.shape[dim]) // (result.shape[dim] // shards_of)).reshape([-1 if axis == dim else 1 for axis in range(result.ndim)]) for dim in (source, target)]
    chosen = jax.random.permutation(rng, shards_of)[partner]
    strong = (owner == chosen) | (owner == (partner + shards_of // 2) % shards_of)
    return jnp.where(strong, factor * result, result)


def block_scale(own_key, extent, shards, low, high):
    loudness, own = 1.0, jax.random.fold_in(own_key, 6)
    for axis_at, shards_of in shards:
        heights = jnp.exp(jax.random.uniform(jax.random.fold_in(own, axis_at), (shards_of,), jnp.float32, low / len(shards), high / len(shards)))
        loudness = loudness * jnp.repeat(heights, extent[axis_at] // shards_of).reshape([-1 if axis == axis_at else 1 for axis in range(len(extent))])
    return loudness


def normal_values(key, extent, width, most, pieces=(), kind=jnp.bfloat16):
    gain = block_scale(key, extent, pieces, -0.22, 0.18) if pieces else 1.0
    entries = jax.random.normal(key, extent, jnp.float32) * width * gain
    return jnp.minimum(jnp.maximum(entries, -most), most).astype(kind)


def gaussian_with(own_key, shape, spread, limit, pieces, heavy, kind=jnp.bfloat16):
    result = spread * jax.random.normal(own_key, shape, jnp.float32)
    if pieces:
        result = result * block_scale(own_key, shape, pieces, -0.22, 0.18)
    return jnp.clip(with_spikes(result, jax.random.fold_in(own_key, 3), *heavy), -limit, limit).astype(kind)


def setup_inputs(seed: int = 0) -> dict:
    key_of = jax.random.split(jax.random.key(seed), 11)
    return {
        "q_step": draw_q_step(jax.random.fold_in(key_of[10], 71), 0),
        "step_k": draw_step_k(jax.random.fold_in(key_of[10], 71), 0),
        "step_values": normal_values(key_of[2], (SLOT_TOTAL, STEP_TOKENS, KEY_VALUE_HEADS * HEAD_WIDTH), 1.0, 6.0, ((0, 64), (2, 4))),
        "prefix_k": normal_values(key_of[3], (PROMPTS, PREFIX, KEY_VALUE_HEADS * HEAD_WIDTH), 2.2, 13.0, ((0, 16), (1, 4), (2, 4))),
        "prefix_v": normal_values(key_of[4], (PROMPTS, PREFIX, KEY_VALUE_HEADS * HEAD_WIDTH), 1.0, 6.0, ((0, 16), (1, 4), (2, 4))),
        "suffix_k": draw_suffix_k(jax.random.fold_in(key_of[10], 71), 0),
        "suffix_values": normal_values(key_of[6], (SLOT_TOTAL, SUFFIX_LENGTH, KEY_VALUE_HEADS * HEAD_WIDTH), 1.0, 6.0, ((0, 64), (2, 4))),
        "lengths": draw_lengths(jax.random.fold_in(key_of[10], 71), 0),
        "placement": jax.vmap(lambda own: jax.random.permutation(own, SLOTS_P))(jax.random.split(key_of[8], N_PROMPT)).reshape((N_PROMPT, SLOTS_P)).astype(jnp.int32),
        "output_weight": gaussian_with(key_of[9], (QUERY_HEADS * HEAD_WIDTH, MODEL_WIDTH), (QUERY_HEADS * HEAD_WIDTH // 16) ** -0.5, 0.5, ((0, 16),), (0, 1, 16, 2.0)),
    }


def reference(q_step, step_k, step_values, prefix_k, prefix_v, suffix_k, suffix_values, lengths, placement, output_weight):
    group_size = QUERY_HEADS // KEY_VALUE_HEADS
    score_scale = 1.0 / math.sqrt(HEAD_WIDTH)
    prompt_for_slot = (placement.reshape(SLOT_TOTAL) // CANDIDATE_SPREAD).astype(jnp.int32)
    positions = jnp.arange(PREFIX + SUFFIX_LENGTH + STEP_TOKENS, dtype=jnp.int32)
    tokens_at = jnp.arange(STEP_TOKENS, dtype=jnp.int32)

    def attend(slot_items):
        query_rows, own_keys, own_values, tail_keys, tail_values, length, prompt_id = slot_items
        head_keys = lax.dynamic_index_in_dim(prefix_k, prompt_id, 0, keepdims=False)
        head_values = lax.dynamic_index_in_dim(prefix_v, prompt_id, 0, keepdims=False)
        key_rows = jnp.concatenate([head_keys, tail_keys, own_keys], 0).astype(jnp.float32).reshape(-1, KEY_VALUE_HEADS, HEAD_WIDTH)
        value_rows = jnp.concatenate([head_values, tail_values, own_values], 0).astype(jnp.float32).reshape(-1, KEY_VALUE_HEADS, HEAD_WIDTH)
        shaped = query_rows.astype(jnp.float32).reshape(STEP_TOKENS, KEY_VALUE_HEADS, group_size, HEAD_WIDTH)
        scores = jnp.einsum('tkgd,lkd->tkgl', shaped, key_rows, precision=lax.Precision.HIGHEST) * score_scale
        own_part = positions[None, :] - (PREFIX + SUFFIX_LENGTH)
        visible = (positions[None, :] < PREFIX + length) | (own_part >= 0) & (own_part <= tokens_at[:, None])
        scores = jnp.where(visible[:, None, None, :], scores, -jnp.inf)
        maxima = lax.optimization_barrier(jnp.max(scores, axis=-1, keepdims=True))
        weights = jnp.exp(scores - maxima)
        totals = lax.optimization_barrier(jnp.sum(weights, axis=-1, keepdims=True))
        shares = lax.optimization_barrier(weights.astype(jnp.bfloat16)).astype(jnp.float32)
        numerators = jnp.einsum('tkgl,lkd->tkgd', shares, value_rows, precision=lax.Precision.HIGHEST)
        return (numerators / totals).reshape(STEP_TOKENS, QUERY_HEADS * HEAD_WIDTH).astype(jnp.bfloat16)
    attention_output = lax.map(attend, (q_step, step_k, step_values, suffix_k, suffix_values, lengths, prompt_for_slot))
    projected = jnp.dot(attention_output.reshape(SLOT_TOTAL * STEP_TOKENS, QUERY_HEADS * HEAD_WIDTH), output_weight, preferred_element_type=jnp.float32)
    return projected.reshape(SLOT_TOTAL, STEP_TOKENS, MODEL_WIDTH).astype(jnp.bfloat16)
```

```python
import math

import jax
import jax.numpy as jnp
from jax import lax
from jax.experimental import pallas as pl
from jax.experimental.pallas import tpu as pltpu
from jax.sharding import PartitionSpec as P

D = 128
LOG2E = 1.4426950408889634
SCALE2 = LOG2E / math.sqrt(D)
HIDDEN = -1e30
F32 = jnp.float32
BF16 = jnp.bfloat16
VMEM_LIMIT = 48 * 1024 * 1024


def split_stat(level, rows):
    high = level.astype(BF16).astype(F32)
    rest = level - high
    middle = rest.astype(BF16).astype(F32)
    low = rest - middle
    lane = lax.broadcasted_iota(jnp.int32, (rows, D), 1)
    return jnp.where(lane == 0, high, jnp.where(lane == 1, middle, jnp.where(lane == 2, low, 0.0)))


def join_stat(block):
    return block[..., 0:1] + block[..., 1:2] + block[..., 2:3]


def dot_t(a, b):
    return lax.dot_general(a, b, (((1,), (1,)), ((), ())), preferred_element_type=F32)


def dot(a, b):
    return lax.dot_general(a, b, (((1,), (0,)), ((), ())), preferred_element_type=F32)


def suffix_kernel(slots, tokens, heads, len_ref, q_ref, sk_ref, sv_ref, k_ref, v_ref, out_ref, q_rows):
    step = pl.program_id(0)
    rows = tokens * heads
    span = k_ref.shape[1]
    row_token = lax.broadcasted_iota(jnp.int32, (rows, tokens), 0) % tokens
    key_token = lax.broadcasted_iota(jnp.int32, (rows, tokens), 1)
    causal = key_token <= row_token
    position = lax.broadcasted_iota(jnp.int32, (rows, span), 1)
    for i in range(slots):
        length = len_ref[step * slots + i]
        wide = q_ref[i].astype(F32)
        for h in range(heads):
            q_rows[i, h * tokens : (h + 1) * tokens, :] = wide[:, h * D : (h + 1) * D]
        q = q_rows[i].astype(BF16)
        scores = dot_t(q, k_ref[i]) * SCALE2
        scores = jnp.where(position < length, scores, HIDDEN)
        step_scores = dot_t(q, sk_ref[i]) * SCALE2
        step_scores = jnp.where(causal, step_scores, HIDDEN)
        top = jnp.maximum(
            jnp.max(scores, axis=1, keepdims=True), jnp.max(step_scores, axis=1, keepdims=True)
        )
        weights = jnp.exp2(scores - top)
        step_weights = jnp.exp2(step_scores - top)
        total = jnp.sum(weights, axis=1, keepdims=True) + jnp.sum(
            step_weights, axis=1, keepdims=True
        )
        numer = dot(weights.astype(BF16), v_ref[i]) + dot(step_weights.astype(BF16), sv_ref[i])
        out_ref[i, 0:rows, :] = q
        out_ref[i, rows : 2 * rows, :] = (numer / total).astype(BF16)
        out_ref[i, 2 * rows : 3 * rows, :] = split_stat(top + jnp.log2(total), rows).astype(BF16)


def suffix_attention(q_step, step_k, step_values, suffix_k, suffix_values, lengths):
    count, tokens, width = q_step.shape
    heads = width // D
    span = suffix_k.shape[1]
    rows = tokens * heads
    per = 2
    return pl.pallas_call(
        lambda *refs: suffix_kernel(per, tokens, heads, *refs),
        grid_spec=pltpu.PrefetchScalarGridSpec(
            num_scalar_prefetch=1,
            grid=(count // per,),
            in_specs=[
                pl.BlockSpec((per, tokens, width), lambda i, n: (i, 0, 0)),
                pl.BlockSpec((per, tokens, D), lambda i, n: (i, 0, 0)),
                pl.BlockSpec((per, tokens, D), lambda i, n: (i, 0, 0)),
                pl.BlockSpec((per, span, D), lambda i, n: (i, 0, 0)),
                pl.BlockSpec((per, span, D), lambda i, n: (i, 0, 0)),
            ],
            out_specs=pl.BlockSpec((per, 3 * rows, D), lambda i, n: (i, 0, 0)),
            scratch_shapes=[pltpu.VMEM((per, rows, D), F32)],
        ),
        out_shape=jax.ShapeDtypeStruct((count, 3 * rows, D), BF16),
        compiler_params=pltpu.CompilerParams(vmem_limit_bytes=VMEM_LIMIT),
        name="suffix_attention",
    )(lengths, q_step, step_k, step_values, suffix_k, suffix_values)


def reorder_kernel(rows, place_ref, in_ref, out_ref):
    for s in range(in_ref.shape[0]):
        out_ref[place_ref[s]] = in_ref[s, 0:rows, :]


def reorder(placement, gathered, rows):
    slots = gathered.shape[0]
    return pl.pallas_call(
        lambda *refs: reorder_kernel(rows, *refs),
        in_specs=[
            pl.BlockSpec(memory_space=pltpu.SMEM),
            pl.BlockSpec(memory_space=pltpu.VMEM),
        ],
        out_specs=pl.BlockSpec(memory_space=pltpu.VMEM),
        out_shape=jax.ShapeDtypeStruct((slots, rows, D), BF16),
        compiler_params=pltpu.CompilerParams(vmem_limit_bytes=VMEM_LIMIT),
        name="reorder_queries",
    )(placement, gathered)


def prefix_kernel(indices, rows, q_ref, k_ref, v_ref, out_ref):
    total_rows = indices * rows
    chunk = 128
    lower = lax.broadcasted_iota(jnp.int32, (chunk // 8, 8, D), 1) < 4
    per_index = chunk // rows
    for start in range(0, total_rows, chunk):
        first = start // rows
        pair = []
        for u in range(2):
            q = q_ref[first : first + per_index, u].reshape(chunk, D)
            scores = dot_t(q, k_ref[u]) * SCALE2
            top = jnp.max(scores, axis=1, keepdims=True)
            weights = jnp.exp2(scores - top)
            total = jnp.sum(weights, axis=1, keepdims=True)
            numer = dot(weights.astype(BF16), v_ref[u]) / total
            stat = split_stat(top + jnp.log2(total), chunk)
            pair.append((numer.reshape(chunk // 8, 8, D), stat.reshape(chunk // 8, 8, D)))
        for part in range(2):
            one, two = pair[0][part], pair[1][part]
            even = jnp.where(lower, one, pltpu.roll(two, 4, 1))
            odd = jnp.where(lower, pltpu.roll(one, 4, 1), two)
            groups = rows // 8
            for parity, value in ((0, even), (1, odd)):
                value = value.reshape(per_index, groups, 8, D).astype(BF16)
                for g in range(groups):
                    out_ref[
                        first : first + per_index, 2 * g + parity, part * 8 : part * 8 + 8, :
                    ] = value[:, g]


def prefix_attention(q_rows, prefix_k, prefix_v, cand):
    indices, _, rows, _ = q_rows.shape
    return pl.pallas_call(
        lambda *refs: prefix_kernel(indices, rows, *refs),
        in_specs=[pl.BlockSpec(memory_space=pltpu.VMEM)] * 3,
        out_specs=pl.BlockSpec(memory_space=pltpu.VMEM),
        out_shape=jax.ShapeDtypeStruct((indices, cand, 16, D), BF16),
        compiler_params=pltpu.CompilerParams(vmem_limit_bytes=VMEM_LIMIT),
        name="prefix_attention",
    )(q_rows, prefix_k, prefix_v)


def project_kernel(
    rows, tokens, place_ref, cand_ref, col_ref, parts_ref, gathered_ref, w_ref, out_ref, attention, own, own_stat
):
    step = pl.program_id(0)
    owners, cand = parts_ref.shape[0], parts_ref.shape[1]
    slots = gathered_ref.shape[0]

    @pl.when(step == 0)
    def _():
        share = rows // cand
        shift = rows - share * cand_ref[0]
        for s in range(slots):
            u = place_ref[s]
            value = gathered_ref[s, rows : 2 * rows, :].astype(F32)
            stat = gathered_ref[s, 2 * rows : 3 * rows, :].astype(F32)
            own[u] = pltpu.roll(value, shift, 0)[0:8]
            own_stat[u] = pltpu.roll(stat, shift, 0)[0:8]
        lower = lax.broadcasted_iota(jnp.int32, (owners, 8, D), 1) < 4

        def paired(ref):
            both = ref[...].reshape(owners, 2, 8, D)
            return jnp.where(lower, both[:, 0], pltpu.roll(both[:, 1], 4, 1))

        values = [paired(own)]
        levels = [join_stat(paired(own_stat))]
        for c in range(cand):
            block = parts_ref[:, c].astype(F32)
            values.append(block[:, 0:8])
            levels.append(join_stat(block[:, 8:16]))
        top = levels[0]
        for level in levels[1:]:
            top = jnp.maximum(top, level)
        total = jnp.zeros_like(top)
        numer = jnp.zeros_like(values[0])
        for value, level in zip(values, levels):
            weight = jnp.exp2(level - top)
            total = total + weight
            numer = numer + value * weight
        merged = (numer / total).astype(BF16).reshape(owners * 8, D)
        lane = lax.broadcasted_iota(jnp.int32, (slots * tokens, owners * 8), 1)
        for h in range(2):
            pick = jnp.where(lane == col_ref[...] + h * tokens, 1.0, 0.0).astype(BF16)
            attention[:, h * D : (h + 1) * D] = dot(pick, merged).astype(BF16)

    blocks = out_ref.shape[0]
    width = out_ref.shape[2]
    for j in range(blocks):
        out_ref[j] = dot(attention[...], w_ref[:, j * width : (j + 1) * width]).astype(BF16)


def merge_project(placement, cand_index, columns, parts, gathered, weight, rows, tokens, shares):
    owners, cand, _, _ = parts.shape
    slots = gathered.shape[0]
    depth, width = weight.shape
    out_rows = slots * tokens
    steps = 4
    return pl.pallas_call(
        lambda *refs: project_kernel(rows, tokens, *refs),
        grid=(steps,),
        in_specs=[
            pl.BlockSpec(memory_space=pltpu.SMEM),
            pl.BlockSpec(memory_space=pltpu.SMEM),
            pl.BlockSpec((out_rows, 1), lambda i: (0, 0)),
            pl.BlockSpec(parts.shape, lambda i: (0, 0, 0, 0)),
            pl.BlockSpec(gathered.shape, lambda i: (0, 0, 0)),
            pl.BlockSpec((depth, width // steps), lambda i: (0, i)),
        ],
        out_specs=pl.BlockSpec((shares // steps, out_rows, width // shares), lambda i: (i, 0, 0)),
        scratch_shapes=[
            pltpu.VMEM((out_rows, depth), BF16),
            pltpu.VMEM((slots, 8, D), F32),
            pltpu.VMEM((slots, 8, D), F32),
        ],
        out_shape=jax.ShapeDtypeStruct((shares, out_rows, width // shares), BF16),
        compiler_params=pltpu.CompilerParams(vmem_limit_bytes=VMEM_LIMIT),
        name="merge_project",
    )(placement, cand_index, columns, parts, gathered, weight)


def sum_kernel(in_ref, out_ref):
    total = in_ref[0].astype(F32)
    for j in range(1, in_ref.shape[0]):
        total = total + in_ref[j].astype(F32)
    out_ref[...] = total.astype(BF16)


def sum_shares(shares):
    return pl.pallas_call(
        sum_kernel,
        in_specs=[pl.BlockSpec(memory_space=pltpu.VMEM)],
        out_specs=pl.BlockSpec(memory_space=pltpu.VMEM),
        out_shape=jax.ShapeDtypeStruct(shares.shape[1:], BF16),
        compiler_params=pltpu.CompilerParams(vmem_limit_bytes=VMEM_LIMIT),
        name="sum_shares",
    )(shares)


def body(
    q_step,
    step_k,
    step_values,
    prefix_k,
    prefix_v,
    suffix_k,
    suffix_values,
    lengths,
    placement,
    output_weight,
):
    slot_count, tokens, width = q_step.shape
    rows = tokens * width // D
    indices = lax.axis_size("prompt")
    cand = lax.axis_size("cand")
    shares = lax.axis_size("tensor") * cand
    slots = placement.shape[1]
    place = placement[0]
    local = suffix_attention(q_step, step_k, step_values, suffix_k, suffix_values, lengths)
    gathered = lax.all_gather(local, "cand", axis=0, tiled=True)
    ordered = reorder(place, gathered, rows)
    arrived = lax.all_to_all(
        ordered.reshape(slots * rows, D), "prompt", split_axis=0, concat_axis=0, tiled=True
    )
    parts = prefix_attention(
        arrived.reshape(indices, slots // indices, rows, D), prefix_k, prefix_v, cand
    )
    returned = lax.all_to_all(
        parts.reshape(indices * cand * 16, D), ("prompt", "cand"), split_axis=0, concat_axis=0, tiled=True
    )
    columns = (place[:, None] * (rows // cand) + jnp.arange(tokens, dtype=jnp.int32)[None, :]).reshape(
        slots * tokens, 1
    )
    cand_index = lax.axis_index("cand").astype(jnp.int32).reshape(1)
    projected = merge_project(
        place,
        cand_index,
        columns,
        returned.reshape(indices, cand, 16, D),
        gathered,
        output_weight,
        rows,
        tokens,
        shares,
    )
    spread = lax.all_to_all(
        projected, ("tensor", "cand"), split_axis=0, concat_axis=0, tiled=True
    )
    return sum_shares(spread).reshape(slots, tokens, -1)


def solution(mesh):
    return jax.shard_map(
        body,
        mesh=mesh,
        in_specs=(
            P(("prompt", "cand"), None, "tensor"),
            P(("prompt", "cand"), None, "tensor"),
            P(("prompt", "cand"), None, "tensor"),
            P("prompt", "cand", "tensor"),
            P("prompt", "cand", "tensor"),
            P(("prompt", "cand"), None, "tensor"),
            P(("prompt", "cand"), None, "tensor"),
            P(("prompt", "cand")),
            P("prompt", None),
            P(("tensor", "cand"), None),
        ),
        out_specs=P("prompt", None, ("tensor", "cand")),
        check_vma=False,
    )
```

```python
import math

import jax
import jax.numpy as jnp
from jax import lax
from jax.experimental import pallas as pl
from jax.experimental.pallas import tpu as pltpu
from jax.sharding import Mesh, PartitionSpec as P

D = 128
SCALE2 = 1.4426950408889634 / math.sqrt(D)
HIDDEN = -1e30
GROUP = 2
F32 = jnp.float32
BF16 = jnp.bfloat16
VMEM_LIMIT = 32 * 1024 * 1024
VMEM_MOST = 57 * 1024 * 1024
VMEM_SPEC = pl.BlockSpec(memory_space=pltpu.VMEM)
SMEM_SPEC = pl.BlockSpec(memory_space=pltpu.SMEM)
HBM_SPEC = pl.BlockSpec(memory_space=pltpu.HBM)
PARAMS = pltpu.CompilerParams(vmem_limit_bytes=VMEM_LIMIT)


def split_stat(level):
    high = level.astype(BF16).astype(F32)
    rest = level - high
    middle = rest.astype(BF16).astype(F32)
    low = rest - middle
    lane = lax.broadcasted_iota(jnp.int32, (level.shape[0], D), 1)
    return jnp.where(lane == 0, high, jnp.where(lane == 1, middle, jnp.where(lane == 2, low, 0.0)))


def join_stat(block):
    return block[..., 0:1] + block[..., 1:2] + block[..., 2:3]


def dot_t(a, b):
    return lax.dot_general(a, b, (((1,), (1,)), ((), ())), preferred_element_type=F32)


def dot(a, b):
    return lax.dot_general(a, b, (((1,), (0,)), ((), ())), preferred_element_type=F32)


def lower_rows(shape):
    return lax.broadcasted_iota(jnp.int32, shape, len(shape) - 2) < 4


def queries_kernel(me_ref, q_ref, all_ref, mine_ref, other_ref, rows):
    slots, tokens, width = q_ref.shape
    core = me_ref[1]
    for i in range(slots):
        wide = q_ref[i].astype(F32)
        for h in range(width // D):
            place = (h // 4) * 4 + (h % 2) * tokens
            rows[(h // 2) % 2, i, place : place + tokens, :] = wide[:, h * D : (h + 1) * D]
    all_ref[...] = jnp.concatenate([rows[0], rows[1]], axis=1).astype(BF16)
    mine_ref[...] = rows[core].reshape(slots * 8, D).astype(BF16)
    other_ref[...] = rows[1 - core].reshape(slots * 8, D).astype(BF16)


def split_queries(me, q_step):
    slots = q_step.shape[0]
    half = jax.ShapeDtypeStruct((slots * 8, D), BF16)
    return pl.pallas_call(
        queries_kernel,
        in_specs=[SMEM_SPEC, VMEM_SPEC],
        out_specs=[VMEM_SPEC] * 3,
        out_shape=[jax.ShapeDtypeStruct((slots, 16, D), BF16), half, half],
        scratch_shapes=[pltpu.VMEM((2, slots, 8, D), F32)],
        compiler_params=PARAMS,
        name="split_queries",
    )(me, q_step)


def route_kernel(me_ref, place_ref, mine_ref, other_ref, out_ref, rows):
    xh, core = me_ref[0], me_ref[1]
    count = mine_ref.shape[0] // 8
    rows[...] = jnp.zeros_like(rows)
    for ref, column in ((mine_ref, core), (other_ref, 1 - core)):
        value = ref[...].astype(F32)
        for i in range(count):
            slot = (2 * xh + column) * count + i
            rows[place_ref[slot]] = value[i * 8 : (i + 1) * 8]
    packed = rows[...].reshape(out_ref.shape[0], 16, D).astype(BF16)
    for j in range(out_ref.shape[1]):
        out_ref[:, j] = packed


def route(me, placement, mine, other, indices):
    slots = placement.shape[0]
    return pl.pallas_call(
        route_kernel,
        in_specs=[SMEM_SPEC, SMEM_SPEC, VMEM_SPEC, VMEM_SPEC],
        out_specs=VMEM_SPEC,
        out_shape=jax.ShapeDtypeStruct((indices, 2, 16, D), BF16),
        scratch_shapes=[pltpu.VMEM((slots, 8, D), F32)],
        compiler_params=PARAMS,
        name="route_queries",
    )(me, placement, mine, other)


def suffix_kernel(me_ref, len_ref, q_ref, sk_ref, sv_ref, k_hbm, v_hbm, *rest):
    outs, (keys, values, tiles, key_sem, value_sem) = rest[:4], rest[4:]
    slots, span, _ = k_hbm.shape
    tokens = sk_ref.shape[1]
    xh, core = me_ref[0], me_ref[1]
    lower = lower_rows((8, D))

    def copies(i):
        return (
            pltpu.make_async_copy(k_hbm.at[i], keys.at[i], key_sem.at[i]),
            pltpu.make_async_copy(v_hbm.at[i], values.at[i], value_sem.at[i]),
        )

    for i in range(slots):
        for copy in copies(i):
            copy.start()
    rows = q_ref.shape[1]
    row_token = lax.broadcasted_iota(jnp.int32, (rows, tokens), 0) % tokens
    key_token = lax.broadcasted_iota(jnp.int32, (rows, tokens), 1)
    causal = key_token <= row_token
    position = lax.broadcasted_iota(jnp.int32, (rows, span), 1)
    for first in range(0, slots, GROUP):
        group = range(first, first + GROUP)
        for i in group:
            for copy in copies(i):
                copy.wait()
        q = [q_ref[i] for i in group]
        scores = [dot_t(q[n], keys[i]) for n, i in enumerate(group)]
        step_scores = [dot_t(q[n], sk_ref[i]) for n, i in enumerate(group)]
        scores = [
            jnp.where(position < len_ref[i], scores[n] * SCALE2, HIDDEN) for n, i in enumerate(group)
        ]
        step_scores = [jnp.where(causal, x * SCALE2, HIDDEN) for x in step_scores]
        top = [
            jnp.maximum(jnp.max(x, axis=1, keepdims=True), jnp.max(y, axis=1, keepdims=True))
            for x, y in zip(scores, step_scores)
        ]
        weights = [jnp.exp2(x - m) for x, m in zip(scores, top)]
        step_weights = [jnp.exp2(x - m) for x, m in zip(step_scores, top)]
        total = [
            jnp.sum(x, axis=1, keepdims=True) + jnp.sum(y, axis=1, keepdims=True)
            for x, y in zip(weights, step_weights)
        ]
        for n, i in enumerate(group):
            numer = dot(weights[n].astype(BF16), values[i])
            numer = numer + dot(step_weights[n].astype(BF16), sv_ref[i])
            value = numer / total[n]
            stat = split_stat(top[n] + jnp.log2(total[n]))
            for c in range(2):
                one, two = value[c * 8 : c * 8 + 8], stat[c * 8 : c * 8 + 8]
                tiles[c, i] = jnp.where(lower, one, pltpu.roll(two, 4, 0))
                tiles[2 + c, i] = jnp.where(lower, pltpu.roll(one, 4, 0), two)
    for j, out in enumerate(outs):
        to_xh = xh if j // 2 == 0 else 1 - xh
        to_core = core if j % 2 == 0 else 1 - core
        out[...] = tiles[2 * to_xh + to_core].reshape(slots * 8, D).astype(BF16)


def suffix_attention(me, lengths, q_rows, step_k, step_values, suffix_k, suffix_values):
    slots, span, _ = suffix_k.shape
    rows = q_rows.shape[1]
    piece = jax.ShapeDtypeStruct((slots * 8, D), BF16)
    return pl.pallas_call(
        suffix_kernel,
        in_specs=[SMEM_SPEC, SMEM_SPEC, VMEM_SPEC, VMEM_SPEC, VMEM_SPEC, HBM_SPEC, HBM_SPEC],
        out_specs=[VMEM_SPEC] * 4,
        out_shape=[piece] * 4,
        scratch_shapes=[
            pltpu.VMEM((slots, span, D), BF16),
            pltpu.VMEM((slots, span, D), BF16),
            pltpu.VMEM((4, slots, 8, D), F32),
            pltpu.SemaphoreType.DMA((slots,)),
            pltpu.SemaphoreType.DMA((slots,)),
        ],
        cost_estimate=pl.CostEstimate(
            flops=4 * slots * rows * span * D * 8,
            bytes_accessed=4 * slots * span * D,
            transcendentals=slots * rows * span,
        ),
        compiler_params=pltpu.CompilerParams(vmem_limit_bytes=VMEM_MOST),
        name="suffix_attention",
    )(me, lengths, q_rows, step_k, step_values, suffix_k, suffix_values)


def prefix_kernel(q_ref, k_own, k_other, v_own, v_other, out_ref):
    indices = q_ref.shape[0]
    q_both = q_ref[:, 0].astype(F32) + q_ref[:, 1].astype(F32)
    pair = []
    for u in range(2):
        q = q_both[:, u * 8 : u * 8 + 8].reshape(indices * 8, D).astype(BF16)
        scores = [dot_t(q, k[u]) * SCALE2 for k in (k_own, k_other)]
        top = jnp.maximum(
            jnp.max(scores[0], axis=1, keepdims=True), jnp.max(scores[1], axis=1, keepdims=True)
        )
        weights = [jnp.exp2(part - top) for part in scores]
        total = sum(jnp.sum(part, axis=1, keepdims=True) for part in weights)
        numer = sum(
            dot(part.astype(BF16), v[u]) for part, v in zip(weights, (v_own, v_other))
        )
        pair.append(
            (
                (numer / total).reshape(indices, 8, D),
                split_stat(top + jnp.log2(total)).reshape(indices, 8, D),
            )
        )
    lower = lower_rows((indices, 8, D))
    for j in range(2):
        halves = []
        for part in range(2):
            one, two = pair[0][part], pair[1][part]
            if j == 0:
                halves.append(jnp.where(lower, one, pltpu.roll(two, 4, 1)))
            else:
                halves.append(jnp.where(lower, pltpu.roll(one, 4, 1), two))
        out_ref[:, j] = jnp.concatenate(halves, axis=1).astype(BF16)


def prefix_attention(q_rows, k_own, k_other, v_own, v_other):
    return pl.pallas_call(
        prefix_kernel,
        in_specs=[VMEM_SPEC] * 5,
        out_specs=VMEM_SPEC,
        out_shape=jax.ShapeDtypeStruct(q_rows.shape, BF16),
        compiler_params=PARAMS,
        name="prefix_attention",
    )(q_rows, k_own, k_other, v_own, v_other)


def stage_kernel(me_ref, w_hbm, after_ref, away_ref, mine_ref, sem):
    core = me_ref[1]
    blocks, _, width = mine_ref.shape
    copies = []
    for half, (out_ref, which) in enumerate(((away_ref, 1 - core), (mine_ref, core))):
        for b in range(blocks):
            columns = pl.ds(pl.multiple_of((2 * b + which) * width, width), width)
            copies.append(
                pltpu.make_async_copy(w_hbm.at[:, columns], out_ref.at[b], sem.at[half, b])
            )
    for copy in copies:
        copy.start()
    for copy in copies:
        copy.wait()


def stage_weight(me, weight, after, blocks):
    depth, width = weight.shape
    half = jax.ShapeDtypeStruct((blocks, depth, width // (2 * blocks)), BF16)
    return pl.pallas_call(
        stage_kernel,
        in_specs=[SMEM_SPEC, HBM_SPEC, HBM_SPEC],
        out_specs=[VMEM_SPEC] * 2,
        out_shape=[half] * 2,
        scratch_shapes=[pltpu.SemaphoreType.DMA((2, blocks))],
        cost_estimate=pl.CostEstimate(
            flops=0, bytes_accessed=4 * depth * width, transcendentals=0
        ),
        compiler_params=pltpu.CompilerParams(vmem_limit_bytes=54 * 1024 * 1024),
        name="stage_weight",
    )(me, weight, after)


def merge_kernel(
    me_ref, place_ref, col_ref, parts_ref, suf0, suf1, suf2, suf3, w_ref, out_ref, att_ref, own
):
    xh, core = me_ref[0], me_ref[1]
    blocks, out_rows, _ = out_ref.shape
    owners = parts_ref.shape[0]
    count = suf0.shape[0] // 8
    for j, ref in enumerate((suf0, suf1, suf2, suf3)):
        from_xh = xh if j // 2 == 0 else 1 - xh
        from_core = core if j % 2 == 0 else 1 - core
        value = ref[...].astype(F32)
        for i in range(count):
            slot = (2 * from_xh + from_core) * count + i
            own[place_ref[slot]] = value[i * 8 : (i + 1) * 8]
    lower = lower_rows((owners, 8, D))
    both = own[...].reshape(owners, 2, 8, D)
    one, two = both[:, 0], both[:, 1]
    values = [jnp.where(lower, one, pltpu.roll(two, 4, 1))]
    levels = [join_stat(jnp.where(lower, pltpu.roll(one, 4, 1), two))]
    for c in range(parts_ref.shape[1]):
        block = parts_ref[:, c].astype(F32)
        values.append(block[:, 0:8])
        levels.append(join_stat(block[:, 8:16]))
    top = levels[0]
    for level in levels[1:]:
        top = jnp.maximum(top, level)
    total = jnp.zeros_like(top)
    numer = jnp.zeros_like(values[0])
    for value, level in zip(values, levels):
        weight = jnp.exp2(level - top)
        total = total + weight
        numer = numer + value * weight
    merged = (numer / total).astype(BF16).reshape(owners * 8, D)
    lane = lax.broadcasted_iota(jnp.int32, (out_rows, owners * 8), 1)
    for h in range(2):
        pick = jnp.where(lane == col_ref[...] + 2 * h, 1.0, 0.0).astype(BF16)
        att_ref[:, h * D : (h + 1) * D] = dot(pick, merged).astype(BF16)
    for b in range(blocks):
        out_ref[b] = dot(att_ref[...], w_ref[b]).astype(BF16)


def merge_and_project(me, placement, columns, parts, pieces, weight):
    slots = placement.shape[0]
    blocks, depth, width = weight.shape
    out_rows = columns.shape[0]
    return pl.pallas_call(
        merge_kernel,
        in_specs=[SMEM_SPEC, SMEM_SPEC] + [VMEM_SPEC] * 7,
        out_specs=[VMEM_SPEC, VMEM_SPEC],
        out_shape=[
            jax.ShapeDtypeStruct((blocks, out_rows, width), BF16),
            jax.ShapeDtypeStruct((out_rows, depth), BF16),
        ],
        scratch_shapes=[pltpu.VMEM((slots, 8, D), F32)],
        compiler_params=PARAMS,
        name="merge_and_project",
    )(me, placement, columns, parts, *pieces, weight)


def project_kernel(att_ref, w_ref, out_ref):
    for b in range(out_ref.shape[0]):
        out_ref[b] = dot(att_ref[...], w_ref[b])


def project(attention, weight):
    out_rows = attention.shape[0]
    blocks, depth, width = weight.shape
    return pl.pallas_call(
        project_kernel,
        in_specs=[VMEM_SPEC] * 2,
        out_specs=VMEM_SPEC,
        out_shape=jax.ShapeDtypeStruct((blocks, out_rows, width), F32),
        cost_estimate=pl.CostEstimate(
            flops=2 * out_rows * depth * width * blocks * 8,
            bytes_accessed=2 * depth * width * blocks,
            transcendentals=0,
        ),
        compiler_params=PARAMS,
        name="project",
    )(attention, weight)


def add_kernel(one_ref, two_ref, out_ref):
    out_ref[...] = (one_ref[...] + two_ref[...].astype(F32)).astype(BF16)


def add_halves(one, two):
    return pl.pallas_call(
        add_kernel,
        in_specs=[VMEM_SPEC] * 2,
        out_specs=VMEM_SPEC,
        out_shape=jax.ShapeDtypeStruct(two.shape, BF16),
        compiler_params=PARAMS,
        name="add_halves",
    )(one, two)


def sum_kernel(in_ref, out_ref):
    total = in_ref[0].astype(F32)
    for j in range(1, in_ref.shape[0]):
        total = total + in_ref[j].astype(F32)
    out_ref[...] = total.astype(BF16).reshape(out_ref.shape)


def sum_shares(shares, tokens):
    _, rows, width = shares.shape
    return pl.pallas_call(
        sum_kernel,
        in_specs=[VMEM_SPEC],
        out_specs=VMEM_SPEC,
        out_shape=jax.ShapeDtypeStruct((rows // tokens, tokens, width), BF16),
        compiler_params=PARAMS,
        name="sum_shares",
    )(shares)


def swap(value, axes):
    size = 2 ** len(axes)
    return lax.ppermute(value, axes, [(i, size - 1 - i) for i in range(size)])


def body(
    q_step,
    step_k,
    step_values,
    prefix_k,
    prefix_v,
    suffix_k,
    suffix_values,
    lengths,
    placement,
    output_weight,
):
    tokens = q_step.shape[1]
    indices = lax.axis_size("prompt")
    blocks = lax.axis_size("tensor") * 2
    place = placement[0]
    slots = place.shape[0]
    me = jnp.stack([lax.axis_index("xh"), lax.axis_index("core")]).astype(jnp.int32)

    all_rows, mine, other = split_queries(me, q_step)
    other = swap(other, ("core",))
    k_other = swap(prefix_k, ("core",))
    v_other = swap(prefix_v, ("core",))
    routed = route(me, place, mine, other, indices)
    arrived = lax.all_to_all(
        routed.reshape(indices * 2, 16, D), ("prompt", "xh"), split_axis=0, concat_axis=0, tiled=True
    )
    pieces = suffix_attention(
        me, lengths, all_rows, step_k, step_values, suffix_k, suffix_values
    )
    parts = prefix_attention(
        arrived.reshape(indices, 2, 16, D), prefix_k, k_other, prefix_v, v_other
    )
    pieces, parts = lax.optimization_barrier((pieces, parts))
    returned = lax.all_to_all(
        parts.reshape(indices * 2, 16, D), ("prompt", "xh"), split_axis=0, concat_axis=0, tiled=True
    )
    pieces = [
        pieces[0],
        swap(pieces[1], ("core",)),
        swap(pieces[2], ("xh",)),
        swap(pieces[3], ("xh", "core")),
    ]
    weight_away, weight_mine = stage_weight(me, output_weight, parts, blocks)
    columns = (place[:, None] * 4 + jnp.arange(tokens, dtype=jnp.int32)[None, :]).reshape(
        slots * tokens, 1
    )
    away, attention = merge_and_project(
        me, place, columns, returned.reshape(indices, 2, 16, D), pieces, weight_away
    )
    away = swap(away, ("core",))
    stay = project(attention, weight_mine)
    spread = lax.all_to_all(
        add_halves(stay, away), ("tensor", "xh"), split_axis=0, concat_axis=0, tiled=True
    )
    return sum_shares(spread, tokens)


def solution(mesh):
    sizes = mesh.shape
    fine = Mesh(
        mesh.devices.reshape(sizes["tensor"], sizes["prompt"], 2, sizes["cand"] // 2),
        ("tensor", "prompt", "xh", "core"),
    )
    slot = ("prompt", "xh", "core")
    cand = ("xh", "core")
    return jax.shard_map(
        body,
        mesh=fine,
        in_specs=(
            P(slot, None, "tensor"),
            P(slot, None, "tensor"),
            P(slot, None, "tensor"),
            P("prompt", cand, "tensor"),
            P("prompt", cand, "tensor"),
            P(slot, None, "tensor"),
            P(slot, None, "tensor"),
            P(slot),
            P("prompt", None),
            P(("tensor",) + cand, None),
        ),
        out_specs=P("prompt", None, ("tensor",) + cand),
        check_vma=False,
    )
```

```python
import math

import jax
import jax.numpy as jnp
from jax import lax
from jax.experimental import pallas as pl
from jax.experimental.pallas import tpu as pltpu
from jax.sharding import Mesh, PartitionSpec as P

D = 128
SCALE2 = 1.4426950408889634 / math.sqrt(D)
HIDDEN = -1e30
GROUP = 2
CHUNKS = 4
BLOCK = 2048
F32 = jnp.float32
BF16 = jnp.bfloat16
VMEM_LIMIT = 32 * 1024 * 1024

VMEM_SPEC = pl.BlockSpec(memory_space=pltpu.VMEM)
SMEM_SPEC = pl.BlockSpec(memory_space=pltpu.SMEM)
HBM_SPEC = pl.BlockSpec(memory_space=pltpu.HBM)
PARAMS = pltpu.CompilerParams(vmem_limit_bytes=VMEM_LIMIT)


def split_stat(level):
    high = level.astype(BF16).astype(F32)
    rest = level - high
    middle = rest.astype(BF16).astype(F32)
    low = rest - middle
    lane = lax.broadcasted_iota(jnp.int32, (level.shape[0], D), 1)
    return jnp.where(lane == 0, high, jnp.where(lane == 1, middle, jnp.where(lane == 2, low, 0.0)))


def join_stat(block):
    return block[..., 0:1] + block[..., 1:2] + block[..., 2:3]


def dot_t(a, b):
    return lax.dot_general(a, b, (((1,), (1,)), ((), ())), preferred_element_type=F32)


def dot(a, b):
    return lax.dot_general(a, b, (((1,), (0,)), ((), ())), preferred_element_type=F32)


def lower_rows(shape):
    return lax.broadcasted_iota(jnp.int32, shape, len(shape) - 2) < 4


def in_hbm(value):
    return pltpu.with_memory_space_constraint(value, pltpu.HBM)


def split_rows(q_ref, rows):
    slots, tokens, width = q_ref.shape
    for i in range(slots):
        wide = q_ref[i].astype(F32)
        for h in range(width // D):
            place = (h // 4) * 4 + (h % 2) * tokens
            rows[(h // 2) % 2, i, place : place + tokens, :] = wide[:, h * D : (h + 1) * D]


def scatter_rows(q_ref, here_ref, rows, first, core):
    count, tokens, _ = q_ref.shape
    for i in range(count):
        u = here_ref[2 + first + i]
        wide = q_ref[i].astype(F32)
        for j in range(4):
            h = 4 * (j // 2) + j % 2
            one = wide[:, h * D : (h + 1) * D]
            two = wide[:, (h + 2) * D : (h + 3) * D]
            rows[u, j * tokens : (j + 1) * tokens, :] = jnp.where(core == 0, one, two)


def own_kernel(here_ref, q_hbm, rows, mine_ref, sem):
    xh, core = here_ref[0], here_ref[1]
    copy = pltpu.make_async_copy(q_hbm, mine_ref, sem)
    copy.start()
    rows[...] = jnp.zeros_like(rows)
    copy.wait()
    scatter_rows(mine_ref, here_ref, rows, (2 * xh + core) * q_hbm.shape[0], core)


def own_rows(here, mine, slots):
    return pl.pallas_call(
        own_kernel,
        in_specs=[SMEM_SPEC, HBM_SPEC],
        out_specs=VMEM_SPEC,
        out_shape=jax.ShapeDtypeStruct((slots, 8, D), F32),
        scratch_shapes=[pltpu.VMEM(mine.shape, BF16), pltpu.SemaphoreType.DMA],
        cost_estimate=pl.CostEstimate(
            flops=0, bytes_accessed=2 * 1024 * 1024, transcendentals=0
        ),
        compiler_params=PARAMS,
        name="own_rows",
    )(here, in_hbm(mine))


def route_kernel(here_ref, own_ref, other_ref, out_ref, rows):
    xh, core = here_ref[0], here_ref[1]
    rows[...] = own_ref[...]
    first = (2 * xh + 1 - core) * other_ref.shape[0]
    scatter_rows(other_ref, here_ref, rows, first, core)
    packed = rows[...].reshape(out_ref.shape[0], 16, D).astype(BF16)
    for j in range(out_ref.shape[1]):
        out_ref[:, j] = packed


def route(here, own, other, indices):
    return pl.pallas_call(
        route_kernel,
        in_specs=[SMEM_SPEC, VMEM_SPEC, VMEM_SPEC],
        out_specs=VMEM_SPEC,
        out_shape=jax.ShapeDtypeStruct((indices, 2, 16, D), BF16),
        scratch_shapes=[pltpu.VMEM(own.shape, F32)],
        compiler_params=PARAMS,
        name="route_queries",
    )(here, own, other)


def suffix_kernel(me_ref, len_hbm, q_hbm, sk_hbm, sv_hbm, k_hbm, v_hbm, *rest):
    keep_ref, core_ref, xh_ref = rest[:3]
    len_ref, q_ref, sk_ref, sv_ref, rows_ref, keys, values, tiles, small_sem, sem = rest[3:]
    slots, span, _ = k_hbm.shape
    tokens = sk_hbm.shape[1]
    xh, core = me_ref[0], me_ref[1]
    lower = lower_rows((8, D))
    lengths_copy = pltpu.make_async_copy(len_hbm, len_ref, small_sem.at[0])
    lengths_copy.start()
    small = (
        pltpu.make_async_copy(q_hbm, q_ref, small_sem.at[1]),
        pltpu.make_async_copy(sk_hbm, sk_ref, small_sem.at[2]),
        pltpu.make_async_copy(sv_hbm, sv_ref, small_sem.at[3]),
    )

    def copies(i, b):
        part = pl.ds(b * BLOCK, BLOCK)
        return (
            pltpu.make_async_copy(k_hbm.at[i, part], keys.at[i, part], sem.at[0, i, b]),
            pltpu.make_async_copy(v_hbm.at[i, part], values.at[i, part], sem.at[1, i, b]),
        )

    for copy in copies(0, 0) + small:
        copy.start()
    lengths_copy.wait()
    blocks = span // BLOCK
    for i in range(slots):
        for b in range(blocks):
            if i + b > 0:

                @pl.when(b * BLOCK < len_ref[i])
                def _():
                    for copy in copies(i, b):
                        copy.start()

    for copy in small:
        copy.wait()
    split_rows(q_ref, rows_ref)
    rows = 16
    row_token = lax.broadcasted_iota(jnp.int32, (rows, tokens), 0) % tokens
    key_token = lax.broadcasted_iota(jnp.int32, (rows, tokens), 1)
    causal = key_token <= row_token
    position = lax.broadcasted_iota(jnp.int32, (rows, span), 1)
    for first in range(0, slots, GROUP):
        group = range(first, first + GROUP)
        for i in group:
            for b in range(blocks):
                if b == 0:
                    for copy in copies(i, b):
                        copy.wait()
                    continue
                live = b * BLOCK < len_ref[i]

                @pl.when(live)
                def _():
                    for copy in copies(i, b):
                        copy.wait()

                @pl.when(jnp.logical_not(live))
                def _():
                    values[i, b * BLOCK : (b + 1) * BLOCK, :] = jnp.zeros((BLOCK, D), BF16)

        q = [
            jnp.concatenate([rows_ref[0, i], rows_ref[1, i]], axis=0).astype(BF16) for i in group
        ]
        scores = [dot_t(q[n], keys[i]) for n, i in enumerate(group)]
        step_scores = [dot_t(q[n], sk_ref[i]) for n, i in enumerate(group)]
        scores = [
            jnp.where(position < len_ref[i], scores[n] * SCALE2, HIDDEN) for n, i in enumerate(group)
        ]
        step_scores = [jnp.where(causal, x * SCALE2, HIDDEN) for x in step_scores]
        top = [
            jnp.maximum(jnp.max(x, axis=1, keepdims=True), jnp.max(y, axis=1, keepdims=True))
            for x, y in zip(scores, step_scores)
        ]
        weights = [jnp.exp2(x - m) for x, m in zip(scores, top)]
        step_weights = [jnp.exp2(x - m) for x, m in zip(step_scores, top)]
        total = [
            jnp.sum(x, axis=1, keepdims=True) + jnp.sum(y, axis=1, keepdims=True)
            for x, y in zip(weights, step_weights)
        ]
        for n, i in enumerate(group):
            numer = dot(weights[n].astype(BF16), values[i])
            numer = numer + dot(step_weights[n].astype(BF16), sv_ref[i])
            value = numer / total[n]
            stat = split_stat(top[n] + jnp.log2(total[n]))
            for c in range(2):
                one, two = value[c * 8 : c * 8 + 8], stat[c * 8 : c * 8 + 8]
                tiles[c, i] = jnp.where(lower, one, pltpu.roll(two, 4, 0))
                tiles[2 + c, i] = jnp.where(lower, pltpu.roll(one, 4, 0), two)

    def piece(to_xh, to_core):
        return tiles[2 * to_xh + to_core].reshape(slots * 8, D).astype(BF16)

    keep_ref[...] = piece(xh, core)
    core_ref[...] = jnp.concatenate([piece(xh, 1 - core), piece(1 - xh, 1 - core)], axis=0)
    xh_ref[...] = piece(1 - xh, core)


def suffix_attention(me, lengths, q_step, step_k, step_values, suffix_k, suffix_values):
    slots, span, _ = suffix_k.shape
    rows = 16
    piece = jax.ShapeDtypeStruct((slots * 8, D), BF16)
    blocks = span // BLOCK
    return pl.pallas_call(
        suffix_kernel,
        in_specs=[SMEM_SPEC] + [HBM_SPEC] * 6,
        out_specs=[VMEM_SPEC] * 3,
        out_shape=[piece, jax.ShapeDtypeStruct((slots * 16, D), BF16), piece],
        scratch_shapes=[
            pltpu.SMEM(lengths.shape, jnp.int32),
            pltpu.VMEM(q_step.shape, BF16),
            pltpu.VMEM(step_k.shape, BF16),
            pltpu.VMEM(step_values.shape, BF16),
            pltpu.VMEM((2, slots, 8, D), F32),
            pltpu.VMEM((slots, span, D), BF16),
            pltpu.VMEM((slots, span, D), BF16),
            pltpu.VMEM((4, slots, 8, D), F32),
            pltpu.SemaphoreType.DMA((4,)),
            pltpu.SemaphoreType.DMA((2, slots, blocks)),
        ],
        cost_estimate=pl.CostEstimate(
            flops=4 * slots * rows * span * D * 8,
            bytes_accessed=4 * slots * span * D,
            transcendentals=slots * rows * span,
        ),
        compiler_params=PARAMS,
        name="suffix_attention",
    )(
        me,
        in_hbm(lengths),
        in_hbm(q_step),
        in_hbm(step_k),
        in_hbm(step_values),
        in_hbm(suffix_k),
        in_hbm(suffix_values),
    )


def prefix_kernel(q_ref, k_own, k_other, v_own, v_other, out_ref):
    indices = q_ref.shape[0]
    q_both = q_ref[:, 0].astype(F32) + q_ref[:, 1].astype(F32)
    pair = []
    for u in range(2):
        q = q_both[:, u * 8 : u * 8 + 8].reshape(indices * 8, D).astype(BF16)
        scores = [dot_t(q, k[u]) * SCALE2 for k in (k_own, k_other)]
        top = jnp.maximum(
            jnp.max(scores[0], axis=1, keepdims=True), jnp.max(scores[1], axis=1, keepdims=True)
        )
        weights = [jnp.exp2(part - top) for part in scores]
        total = sum(jnp.sum(part, axis=1, keepdims=True) for part in weights)
        numer = sum(
            dot(part.astype(BF16), v[u]) for part, v in zip(weights, (v_own, v_other))
        )
        pair.append(
            (
                (numer / total).reshape(indices, 8, D),
                split_stat(top + jnp.log2(total)).reshape(indices, 8, D),
            )
        )
    lower = lower_rows((indices, 8, D))
    for j in range(2):
        halves = []
        for part in range(2):
            one, two = pair[0][part], pair[1][part]
            if j == 0:
                halves.append(jnp.where(lower, one, pltpu.roll(two, 4, 1)))
            else:
                halves.append(jnp.where(lower, pltpu.roll(one, 4, 1), two))
        out_ref[:, j] = jnp.concatenate(halves, axis=1).astype(BF16)


def prefix_attention(q_rows, k_own, k_other, v_own, v_other):
    return pl.pallas_call(
        prefix_kernel,
        in_specs=[VMEM_SPEC] * 5,
        out_specs=VMEM_SPEC,
        out_shape=jax.ShapeDtypeStruct(q_rows.shape, BF16),
        compiler_params=PARAMS,
        name="prefix_attention",
    )(q_rows, k_own, k_other, v_own, v_other)


def low_copies(w_hbm, low_ref, sem, which):
    blocks, depth, width = low_ref.shape
    return [
        pltpu.make_async_copy(
            w_hbm.at[pl.ds(depth, depth), block_columns(2 * b + which, width)],
            low_ref.at[b],
            sem.at[b],
        )
        for b in range(blocks)
    ]


def stage_kernel(here_ref, w_hbm, after_ref, upper_ref, low_ref, mine_hbm, mine_ref, *sems):
    upper_sem, low_sem, mine_sem, out_sem = sems
    core = here_ref[1]
    chunk = upper_ref.shape[0] // CHUNKS
    mine = low_copies(w_hbm, mine_ref, mine_sem, core)
    copies = low_copies(w_hbm, low_ref, low_sem, 1 - core)
    for j in range(CHUNKS):
        part = pl.ds(j * chunk, chunk)
        copies.append(pltpu.make_async_copy(w_hbm.at[part], upper_ref.at[part], upper_sem.at[j]))
    for copy in mine + copies:
        copy.start()
    out = [
        pltpu.make_async_copy(mine_ref.at[b], mine_hbm.at[b], out_sem.at[b])
        for b in range(len(mine))
    ]
    for arrived, copy in zip(mine, out):
        arrived.wait()
        copy.start()
    for copy in copies + out:
        copy.wait()


def stage_weight(here, weight, after, blocks):
    depth, width = weight.shape
    low = (blocks, depth // 2, width // (2 * blocks))
    return pl.pallas_call(
        stage_kernel,
        in_specs=[SMEM_SPEC, HBM_SPEC, pl.BlockSpec(memory_space=pl.ANY)],
        out_specs=[VMEM_SPEC, VMEM_SPEC, HBM_SPEC],
        out_shape=[
            jax.ShapeDtypeStruct((depth // 2, width), BF16),
            jax.ShapeDtypeStruct(low, BF16),
            jax.ShapeDtypeStruct(low, BF16),
        ],
        scratch_shapes=[
            pltpu.VMEM(low, BF16),
            pltpu.SemaphoreType.DMA((CHUNKS,)),
            pltpu.SemaphoreType.DMA((blocks,)),
            pltpu.SemaphoreType.DMA((blocks,)),
            pltpu.SemaphoreType.DMA((blocks,)),
        ],
        cost_estimate=pl.CostEstimate(
            flops=0, bytes_accessed=5 * depth * width, transcendentals=0
        ),
        compiler_params=PARAMS,
        name="stage_weight",
    )(here, in_hbm(weight), after)


def block_columns(block, width):
    return pl.ds(pl.multiple_of(block * width, width), width)


def merge_kernel(
    here_ref, col_ref, parts_ref, keep_ref, near_ref, far_ref, upper_ref, low_ref, *rest
):
    out_ref, att_ref, own = rest
    xh, core = here_ref[0], here_ref[1]
    blocks, out_rows, width = out_ref.shape
    owners = parts_ref.shape[0]
    count = keep_ref.shape[0] // 8
    pieces = ((keep_ref, 0, xh, core), (near_ref, 0, xh, 1 - core))
    pieces += ((far_ref, 0, 1 - xh, core), (far_ref, count, 1 - xh, 1 - core))
    for ref, start, from_xh, from_core in pieces:
        value = ref[start * 8 : (start + count) * 8, :].astype(F32)
        for i in range(count):
            slot = (2 * from_xh + from_core) * count + i
            own[here_ref[2 + slot]] = value[i * 8 : (i + 1) * 8]
    lower = lower_rows((owners, 8, D))
    both = own[...].reshape(owners, 2, 8, D)
    one, two = both[:, 0], both[:, 1]
    values = [jnp.where(lower, one, pltpu.roll(two, 4, 1))]
    levels = [join_stat(jnp.where(lower, pltpu.roll(one, 4, 1), two))]
    for c in range(parts_ref.shape[1]):
        block = parts_ref[:, c].astype(F32)
        values.append(block[:, 0:8])
        levels.append(join_stat(block[:, 8:16]))
    top = levels[0]
    for level in levels[1:]:
        top = jnp.maximum(top, level)
    total = jnp.zeros_like(top)
    numer = jnp.zeros_like(values[0])
    for value, level in zip(values, levels):
        weight = jnp.exp2(level - top)
        total = total + weight
        numer = numer + value * weight
    merged = (numer / total).astype(BF16).reshape(owners * 8, D)
    lane = lax.broadcasted_iota(jnp.int32, (out_rows, owners * 8), 1)
    for h in range(2):
        pick = jnp.where(lane == col_ref[...] + 2 * h, 1.0, 0.0).astype(BF16)
        att_ref[:, h * D : (h + 1) * D] = dot(pick, merged).astype(BF16)
    half = low_ref.shape[1]
    for b in range(blocks):
        columns = block_columns(2 * b + 1 - core, width)
        value = dot(att_ref[:, 0:half], upper_ref[:, columns])
        out_ref[b] = (value + dot(att_ref[:, half:], low_ref[b])).astype(BF16)


def merge_and_project(here, slots, columns, parts, pieces, upper, low):
    blocks, half, width = low.shape
    out_rows = columns.shape[0]
    return pl.pallas_call(
        merge_kernel,
        in_specs=[SMEM_SPEC] + [VMEM_SPEC] * 7,
        out_specs=[VMEM_SPEC, VMEM_SPEC],
        out_shape=[
            jax.ShapeDtypeStruct((blocks, out_rows, width), BF16),
            jax.ShapeDtypeStruct((out_rows, 2 * half), BF16),
        ],
        scratch_shapes=[pltpu.VMEM((slots, 8, D), F32)],
        compiler_params=PARAMS,
        name="merge_and_project",
    )(here, columns, parts, *pieces, upper, low)


def project_kernel(here_ref, att_ref, upper_ref, low_hbm, out_ref, low_ref, sem):
    blocks, half, width = low_ref.shape
    copies = [
        pltpu.make_async_copy(low_hbm.at[b], low_ref.at[b], sem.at[b]) for b in range(blocks)
    ]
    for copy in copies:
        copy.start()
    for b in range(blocks):
        columns = block_columns(2 * b + here_ref[1], width)
        out_ref[b] = dot(att_ref[:, 0:half], upper_ref[:, columns])
    for copy in copies:
        copy.wait()
    for b in range(blocks):
        out_ref[b] += dot(att_ref[:, half:], low_ref[b])


def project(here, attention, upper, low):
    blocks, half, width = low.shape
    out_rows = attention.shape[0]
    return pl.pallas_call(
        project_kernel,
        in_specs=[SMEM_SPEC, VMEM_SPEC, VMEM_SPEC, HBM_SPEC],
        out_specs=VMEM_SPEC,
        out_shape=jax.ShapeDtypeStruct((blocks, out_rows, width), F32),
        scratch_shapes=[pltpu.VMEM(low.shape, BF16), pltpu.SemaphoreType.DMA((blocks,))],
        cost_estimate=pl.CostEstimate(
            flops=4 * out_rows * half * width * blocks * 8,
            bytes_accessed=4 * half * width * blocks,
            transcendentals=0,
        ),
        compiler_params=PARAMS,
        name="project",
    )(here, attention, upper, in_hbm(low))


def add_kernel(one_ref, two_ref, out_ref):
    out_ref[...] = (one_ref[...] + two_ref[...].astype(F32)).astype(BF16)


def add_halves(one, two):
    return pl.pallas_call(
        add_kernel,
        in_specs=[VMEM_SPEC] * 2,
        out_specs=VMEM_SPEC,
        out_shape=jax.ShapeDtypeStruct(two.shape, BF16),
        compiler_params=PARAMS,
        name="add_halves",
    )(one, two)


def sum_kernel(in_ref, out_ref):
    total = in_ref[0].astype(F32)
    for j in range(1, in_ref.shape[0]):
        total = total + in_ref[j].astype(F32)
    out_ref[...] = total.astype(BF16).reshape(out_ref.shape)


def sum_shares(shares, tokens):
    _, rows, width = shares.shape
    return pl.pallas_call(
        sum_kernel,
        in_specs=[VMEM_SPEC],
        out_specs=VMEM_SPEC,
        out_shape=jax.ShapeDtypeStruct((rows // tokens, tokens, width), BF16),
        compiler_params=PARAMS,
        name="sum_shares",
    )(shares)


def swap(value, axes):
    size = 2 ** len(axes)
    return lax.ppermute(value, axes, [(i, size - 1 - i) for i in range(size)])


def body(
    q_step,
    step_k,
    step_values,
    prefix_k,
    prefix_v,
    suffix_k,
    suffix_values,
    lengths,
    placement,
    output_weight,
):
    tokens = q_step.shape[1]
    indices = lax.axis_size("prompt")
    blocks = lax.axis_size("tensor") * 2
    place = placement[0]
    slots = place.shape[0]
    me = jnp.stack([lax.axis_index("xh"), lax.axis_index("core")]).astype(jnp.int32)
    here = jnp.concatenate([me, place])

    other = swap(q_step, ("core",))
    own = own_rows(here, q_step, slots)
    routed = route(here, own, other, indices)
    routed, prefix_k, prefix_v = lax.optimization_barrier((routed, prefix_k, prefix_v))
    k_other = swap(prefix_k, ("core",))
    v_other = swap(prefix_v, ("core",))
    arrived = lax.all_to_all(
        routed.reshape(indices * 2, 16, D), ("prompt", "xh"), split_axis=0, concat_axis=0, tiled=True
    )
    keep, to_core, to_xh = suffix_attention(
        here, lengths, q_step, step_k, step_values, suffix_k, suffix_values
    )
    near = swap(to_core, ("core",))
    far = swap(jnp.concatenate([to_xh, near[near.shape[0] // 2 :]], axis=0), ("xh",))
    parts = prefix_attention(
        arrived.reshape(indices, 2, 16, D), prefix_k, k_other, prefix_v, v_other
    )
    returned = lax.all_to_all(
        parts.reshape(indices * 2, 16, D), ("prompt", "xh"), split_axis=0, concat_axis=0, tiled=True
    )
    upper, low_away, low_mine = stage_weight(here, output_weight, parts, blocks)
    columns = (place[:, None] * 4 + jnp.arange(tokens, dtype=jnp.int32)[None, :]).reshape(
        slots * tokens, 1
    )
    away, attention = merge_and_project(
        here,
        slots,
        columns,
        returned.reshape(indices, 2, 16, D),
        (keep, near, far),
        upper,
        low_away,
    )
    away = swap(away, ("core",))
    stay = project(here, attention, upper, low_mine)
    spread = lax.all_to_all(
        add_halves(stay, away), ("tensor", "xh"), split_axis=0, concat_axis=0, tiled=True
    )
    return sum_shares(spread, tokens)


def solution(mesh):
    sizes = mesh.shape
    fine = Mesh(
        mesh.devices.reshape(sizes["tensor"], sizes["prompt"], 2, sizes["cand"] // 2),
        ("tensor", "prompt", "xh", "core"),
    )
    slot = ("prompt", "xh", "core")
    cand = ("xh", "core")
    return jax.shard_map(
        body,
        mesh=fine,
        in_specs=(
            P(slot, None, "tensor"),
            P(slot, None, "tensor"),
            P(slot, None, "tensor"),
            P("prompt", cand, "tensor"),
            P("prompt", cand, "tensor"),
            P(slot, None, "tensor"),
            P(slot, None, "tensor"),
            P(slot),
            P("prompt", None),
            P(("tensor",) + cand, None),
        ),
        out_specs=P("prompt", None, ("tensor",) + cand),
        check_vma=False,
    )
```

```python
import math

import jax
import jax.numpy as jnp
from jax import lax
from jax.experimental import pallas as pl
from jax.experimental.pallas import tpu as pltpu
from jax.sharding import Mesh, PartitionSpec as P

D = 128
SCALE2 = 1.4426950408889634 / math.sqrt(D)
HIDDEN = -1e30
GROUP = 2
CHUNKS = 4
BLOCK = 2048
F32 = jnp.float32
BF16 = jnp.bfloat16
VMEM_LIMIT = 32 * 1024 * 1024

VMEM_SPEC = pl.BlockSpec(memory_space=pltpu.VMEM)
SMEM_SPEC = pl.BlockSpec(memory_space=pltpu.SMEM)
HBM_SPEC = pl.BlockSpec(memory_space=pltpu.HBM)
PARAMS = pltpu.CompilerParams(vmem_limit_bytes=VMEM_LIMIT)


def split_stat(level):
    high = level.astype(BF16).astype(F32)
    rest = level - high
    middle = rest.astype(BF16).astype(F32)
    low = rest - middle
    lane = lax.broadcasted_iota(jnp.int32, (level.shape[0], D), 1)
    return jnp.where(lane == 0, high, jnp.where(lane == 1, middle, jnp.where(lane == 2, low, 0.0)))


def join_stat(block):
    return block[..., 0:1] + block[..., 1:2] + block[..., 2:3]


def dot_t(a, b):
    return lax.dot_general(a, b, (((1,), (1,)), ((), ())), preferred_element_type=F32)


def dot(a, b):
    return lax.dot_general(a, b, (((1,), (0,)), ((), ())), preferred_element_type=F32)


def lower_rows(shape):
    return lax.broadcasted_iota(jnp.int32, shape, len(shape) - 2) < 4


def in_hbm(value):
    return pltpu.with_memory_space_constraint(value, pltpu.HBM)


def split_rows(q_ref, rows):
    slots, tokens, width = q_ref.shape
    for i in range(slots):
        wide = q_ref[i].astype(F32)
        for h in range(width // D):
            place = (h // 4) * 4 + (h % 2) * tokens
            rows[(h // 2) % 2, i, place : place + tokens, :] = wide[:, h * D : (h + 1) * D]


def scatter_rows(q_ref, place_ref, rows, first, core):
    count, tokens, _ = q_ref.shape
    for i in range(count):
        u = place_ref[0, first + i]
        wide = q_ref[i].astype(F32)
        for j in range(4):
            h = 4 * (j // 2) + j % 2
            one = wide[:, h * D : (h + 1) * D]
            two = wide[:, (h + 2) * D : (h + 3) * D]
            rows[u, j * tokens : (j + 1) * tokens, :] = jnp.where(core == 0, one, two)


def own_kernel(me_ref, place_hbm, q_hbm, rows, place_out, place_ref, mine_ref, sem):
    xh, core = me_ref[0], me_ref[1]
    copies = (
        pltpu.make_async_copy(place_hbm, place_ref, sem.at[0]),
        pltpu.make_async_copy(q_hbm, mine_ref, sem.at[1]),
        pltpu.make_async_copy(place_hbm, place_out, sem.at[2]),
    )
    for copy in copies:
        copy.start()
    rows[...] = jnp.zeros_like(rows)
    for copy in copies:
        copy.wait()
    scatter_rows(mine_ref, place_ref, rows, (2 * xh + core) * q_hbm.shape[0], core)


def own_rows(me, placement, mine):
    return pl.pallas_call(
        own_kernel,
        in_specs=[SMEM_SPEC, HBM_SPEC, HBM_SPEC],
        out_specs=[VMEM_SPEC, VMEM_SPEC],
        out_shape=[
            jax.ShapeDtypeStruct((placement.shape[1], 8, D), F32),
            jax.ShapeDtypeStruct(placement.shape, jnp.int32),
        ],
        scratch_shapes=[
            pltpu.SMEM(placement.shape, jnp.int32),
            pltpu.VMEM(mine.shape, BF16),
            pltpu.SemaphoreType.DMA((3,)),
        ],
        cost_estimate=pl.CostEstimate(
            flops=0, bytes_accessed=2 * 1024 * 1024, transcendentals=0
        ),
        compiler_params=PARAMS,
        name="own_rows",
    )(me, in_hbm(placement), in_hbm(mine))


def route_kernel(me_ref, place_ref, own_ref, other_ref, out_ref, rows):
    xh, core = me_ref[0], me_ref[1]
    rows[...] = own_ref[...]
    first = (2 * xh + 1 - core) * other_ref.shape[0]
    scatter_rows(other_ref, place_ref, rows, first, core)
    packed = rows[...].reshape(out_ref.shape[0], 16, D).astype(BF16)
    for j in range(out_ref.shape[1]):
        out_ref[:, j] = packed


def route(me, placement, own, other, indices):
    return pl.pallas_call(
        route_kernel,
        in_specs=[SMEM_SPEC, SMEM_SPEC, VMEM_SPEC, VMEM_SPEC],
        out_specs=VMEM_SPEC,
        out_shape=jax.ShapeDtypeStruct((indices, 2, 16, D), BF16),
        scratch_shapes=[pltpu.VMEM(own.shape, F32)],
        compiler_params=PARAMS,
        name="route_queries",
    )(me, placement, own, other)


def suffix_kernel(me_ref, len_hbm, q_hbm, sk_hbm, sv_hbm, k_hbm, v_hbm, *rest):
    keep_ref, core_ref, xh_ref = rest[:3]
    len_ref, q_ref, sk_ref, sv_ref, rows_ref, keys, values, tiles, small_sem, sem = rest[3:]
    slots, span, _ = k_hbm.shape
    tokens = sk_hbm.shape[1]
    xh, core = me_ref[0], me_ref[1]
    lower = lower_rows((8, D))
    lengths_copy = pltpu.make_async_copy(len_hbm, len_ref, small_sem.at[0])
    lengths_copy.start()
    small = (
        pltpu.make_async_copy(q_hbm, q_ref, small_sem.at[1]),
        pltpu.make_async_copy(sk_hbm, sk_ref, small_sem.at[2]),
        pltpu.make_async_copy(sv_hbm, sv_ref, small_sem.at[3]),
    )

    def copies(i, b):
        part = pl.ds(b * BLOCK, BLOCK)
        return (
            pltpu.make_async_copy(k_hbm.at[i, part], keys.at[i, part], sem.at[0, i, b]),
            pltpu.make_async_copy(v_hbm.at[i, part], values.at[i, part], sem.at[1, i, b]),
        )

    for copy in copies(0, 0) + small:
        copy.start()
    lengths_copy.wait()
    blocks = span // BLOCK
    for i in range(slots):
        for b in range(blocks):
            if i + b > 0:

                @pl.when(b * BLOCK < len_ref[i])
                def _():
                    for copy in copies(i, b):
                        copy.start()

    for copy in small:
        copy.wait()
    split_rows(q_ref, rows_ref)
    rows = 16
    row_token = lax.broadcasted_iota(jnp.int32, (rows, tokens), 0) % tokens
    key_token = lax.broadcasted_iota(jnp.int32, (rows, tokens), 1)
    causal = key_token <= row_token
    position = lax.broadcasted_iota(jnp.int32, (rows, span), 1)
    for first in range(0, slots, GROUP):
        group = range(first, first + GROUP)
        for i in group:
            for b in range(blocks):
                if b == 0:
                    for copy in copies(i, b):
                        copy.wait()
                    continue
                live = b * BLOCK < len_ref[i]

                @pl.when(live)
                def _():
                    for copy in copies(i, b):
                        copy.wait()

                @pl.when(jnp.logical_not(live))
                def _():
                    values[i, b * BLOCK : (b + 1) * BLOCK, :] = jnp.zeros((BLOCK, D), BF16)

        q = [
            jnp.concatenate([rows_ref[0, i], rows_ref[1, i]], axis=0).astype(BF16) for i in group
        ]
        scores = [dot_t(q[n], keys[i]) for n, i in enumerate(group)]
        step_scores = [dot_t(q[n], sk_ref[i]) for n, i in enumerate(group)]
        scores = [
            jnp.where(position < len_ref[i], scores[n] * SCALE2, HIDDEN) for n, i in enumerate(group)
        ]
        step_scores = [jnp.where(causal, x * SCALE2, HIDDEN) for x in step_scores]
        top = [
            jnp.maximum(jnp.max(x, axis=1, keepdims=True), jnp.max(y, axis=1, keepdims=True))
            for x, y in zip(scores, step_scores)
        ]
        weights = [jnp.exp2(x - m) for x, m in zip(scores, top)]
        step_weights = [jnp.exp2(x - m) for x, m in zip(step_scores, top)]
        total = [
            jnp.sum(x, axis=1, keepdims=True) + jnp.sum(y, axis=1, keepdims=True)
            for x, y in zip(weights, step_weights)
        ]
        for n, i in enumerate(group):
            numer = dot(weights[n].astype(BF16), values[i])
            numer = numer + dot(step_weights[n].astype(BF16), sv_ref[i])
            value = numer / total[n]
            stat = split_stat(top[n] + jnp.log2(total[n]))
            for c in range(2):
                one, two = value[c * 8 : c * 8 + 8], stat[c * 8 : c * 8 + 8]
                tiles[c, i] = jnp.where(lower, one, pltpu.roll(two, 4, 0))
                tiles[2 + c, i] = jnp.where(lower, pltpu.roll(one, 4, 0), two)

    def piece(to_xh, to_core):
        return tiles[2 * to_xh + to_core].reshape(slots * 8, D).astype(BF16)

    keep_ref[...] = piece(xh, core)
    core_ref[...] = jnp.concatenate([piece(xh, 1 - core), piece(1 - xh, 1 - core)], axis=0)
    xh_ref[...] = piece(1 - xh, core)


def suffix_attention(me, lengths, q_step, step_k, step_values, suffix_k, suffix_values):
    slots, span, _ = suffix_k.shape
    rows = 16
    piece = jax.ShapeDtypeStruct((slots * 8, D), BF16)
    blocks = span // BLOCK
    return pl.pallas_call(
        suffix_kernel,
        in_specs=[SMEM_SPEC] + [HBM_SPEC] * 6,
        out_specs=[VMEM_SPEC] * 3,
        out_shape=[piece, jax.ShapeDtypeStruct((slots * 16, D), BF16), piece],
        scratch_shapes=[
            pltpu.SMEM(lengths.shape, jnp.int32),
            pltpu.VMEM(q_step.shape, BF16),
            pltpu.VMEM(step_k.shape, BF16),
            pltpu.VMEM(step_values.shape, BF16),
            pltpu.VMEM((2, slots, 8, D), F32),
            pltpu.VMEM((slots, span, D), BF16),
            pltpu.VMEM((slots, span, D), BF16),
            pltpu.VMEM((4, slots, 8, D), F32),
            pltpu.SemaphoreType.DMA((4,)),
            pltpu.SemaphoreType.DMA((2, slots, blocks)),
        ],
        cost_estimate=pl.CostEstimate(
            flops=4 * slots * rows * span * D * 8,
            bytes_accessed=4 * slots * span * D,
            transcendentals=slots * rows * span,
        ),
        compiler_params=PARAMS,
        name="suffix_attention",
    )(
        me,
        in_hbm(lengths),
        in_hbm(q_step),
        in_hbm(step_k),
        in_hbm(step_values),
        in_hbm(suffix_k),
        in_hbm(suffix_values),
    )


def prefix_kernel(q_ref, k_own, k_other, v_own, v_other, out_ref):
    indices = q_ref.shape[0]
    q_both = q_ref[:, 0].astype(F32) + q_ref[:, 1].astype(F32)
    q = [q_both[:, u * 8 : u * 8 + 8].reshape(indices * 8, D).astype(BF16) for u in range(2)]
    scores = [[dot_t(q[u], k[u]) * SCALE2 for k in (k_own, k_other)] for u in range(2)]
    top = [
        jnp.maximum(jnp.max(one, axis=1, keepdims=True), jnp.max(two, axis=1, keepdims=True))
        for one, two in scores
    ]
    weights = [[jnp.exp2(part - top[u]) for part in scores[u]] for u in range(2)]
    total = [sum(jnp.sum(part, axis=1, keepdims=True) for part in weights[u]) for u in range(2)]
    numer = [
        sum(dot(part.astype(BF16), v[u]) for part, v in zip(weights[u], (v_own, v_other)))
        for u in range(2)
    ]
    pair = [
        (
            (numer[u] / total[u]).reshape(indices, 8, D),
            split_stat(top[u] + jnp.log2(total[u])).reshape(indices, 8, D),
        )
        for u in range(2)
    ]
    lower = lower_rows((indices, 8, D))
    for j in range(2):
        halves = []
        for part in range(2):
            one, two = pair[0][part], pair[1][part]
            if j == 0:
                halves.append(jnp.where(lower, one, pltpu.roll(two, 4, 1)))
            else:
                halves.append(jnp.where(lower, pltpu.roll(one, 4, 1), two))
        out_ref[:, j] = jnp.concatenate(halves, axis=1).astype(BF16)


def prefix_attention(q_rows, k_own, k_other, v_own, v_other):
    return pl.pallas_call(
        prefix_kernel,
        in_specs=[VMEM_SPEC] * 5,
        out_specs=VMEM_SPEC,
        out_shape=jax.ShapeDtypeStruct(q_rows.shape, BF16),
        compiler_params=PARAMS,
        name="prefix_attention",
    )(q_rows, k_own, k_other, v_own, v_other)


def low_copies(w_hbm, low_ref, sem, which):
    blocks, depth, width = low_ref.shape
    return [
        pltpu.make_async_copy(
            w_hbm.at[pl.ds(depth, depth), block_columns(2 * b + which, width)],
            low_ref.at[b],
            sem.at[b],
        )
        for b in range(blocks)
    ]


def stage_kernel(me_ref, w_hbm, after_ref, upper_ref, low_ref, mine_hbm, mine_ref, *sems):
    upper_sem, low_sem, mine_sem, out_sem = sems
    core = me_ref[1]
    chunk = upper_ref.shape[0] // CHUNKS
    mine = low_copies(w_hbm, mine_ref, mine_sem, core)
    copies = low_copies(w_hbm, low_ref, low_sem, 1 - core)
    for j in range(CHUNKS):
        part = pl.ds(j * chunk, chunk)
        copies.append(pltpu.make_async_copy(w_hbm.at[part], upper_ref.at[part], upper_sem.at[j]))
    for copy in mine + copies:
        copy.start()
    out = [
        pltpu.make_async_copy(mine_ref.at[b], mine_hbm.at[b], out_sem.at[b])
        for b in range(len(mine))
    ]
    for arrived, copy in zip(mine, out):
        arrived.wait()
        copy.start()
    for copy in copies + out:
        copy.wait()


def stage_weight(me, weight, after, blocks):
    depth, width = weight.shape
    low = (blocks, depth // 2, width // (2 * blocks))
    return pl.pallas_call(
        stage_kernel,
        in_specs=[SMEM_SPEC, HBM_SPEC, pl.BlockSpec(memory_space=pl.ANY)],
        out_specs=[VMEM_SPEC, VMEM_SPEC, HBM_SPEC],
        out_shape=[
            jax.ShapeDtypeStruct((depth // 2, width), BF16),
            jax.ShapeDtypeStruct(low, BF16),
            pltpu.HBM(low, BF16),
        ],
        scratch_shapes=[
            pltpu.VMEM(low, BF16),
            pltpu.SemaphoreType.DMA((CHUNKS,)),
            pltpu.SemaphoreType.DMA((blocks,)),
            pltpu.SemaphoreType.DMA((blocks,)),
            pltpu.SemaphoreType.DMA((blocks,)),
        ],
        cost_estimate=pl.CostEstimate(
            flops=0, bytes_accessed=5 * depth * width, transcendentals=0
        ),
        compiler_params=PARAMS,
        name="stage_weight",
    )(me, in_hbm(weight), after)


def block_columns(block, width):
    return pl.ds(pl.multiple_of(block * width, width), width)


def collect_kernel(me_ref, place_ref, keep_ref, near_ref, far_ref, value_ref, level_ref, own):
    xh, core = me_ref[0], me_ref[1]
    owners = value_ref.shape[0]
    count = keep_ref.shape[0] // 8
    pieces = ((keep_ref, 0, xh, core), (near_ref, 0, xh, 1 - core))
    pieces += ((far_ref, 0, 1 - xh, core), (far_ref, count, 1 - xh, 1 - core))
    for ref, start, from_xh, from_core in pieces:
        value = ref[start * 8 : (start + count) * 8, :].astype(F32)
        for i in range(count):
            slot = (2 * from_xh + from_core) * count + i
            own[place_ref[0, slot]] = value[i * 8 : (i + 1) * 8]
    lower = lower_rows((owners, 8, D))
    both = own[...].reshape(owners, 2, 8, D)
    one, two = both[:, 0], both[:, 1]
    value_ref[...] = jnp.where(lower, one, pltpu.roll(two, 4, 1))
    level = join_stat(jnp.where(lower, pltpu.roll(one, 4, 1), two))
    level_ref[...] = jnp.broadcast_to(level, level_ref.shape)


def collect_suffix(me, placement, pieces, owners):
    part = jax.ShapeDtypeStruct((owners, 8, D), F32)
    return pl.pallas_call(
        collect_kernel,
        in_specs=[SMEM_SPEC] * 2 + [VMEM_SPEC] * 3,
        out_specs=[VMEM_SPEC] * 2,
        out_shape=[part, part],
        scratch_shapes=[pltpu.VMEM((placement.shape[1], 8, D), F32)],
        cost_estimate=pl.CostEstimate(
            flops=0, bytes_accessed=1024 * 1024, transcendentals=0
        ),
        compiler_params=PARAMS,
        name="collect_suffix",
    )(me, placement, *pieces)


def merge_kernel(
    me_ref, col_ref, parts_ref, value_ref, level_ref, upper_ref, low_ref, out_ref, att_ref
):
    core = me_ref[1]
    blocks, out_rows, width = out_ref.shape
    owners = parts_ref.shape[0]
    values = [value_ref[...]]
    levels = [level_ref[...]]
    for c in range(parts_ref.shape[1]):
        block = parts_ref[:, c].astype(F32)
        values.append(block[:, 0:8])
        levels.append(jnp.broadcast_to(join_stat(block[:, 8:16]), level_ref.shape))
    top = levels[0]
    for level in levels[1:]:
        top = jnp.maximum(top, level)
    total = jnp.zeros_like(top)
    numer = jnp.zeros_like(values[0])
    for value, level in zip(values, levels):
        weight = jnp.exp2(level - top)
        total = total + weight
        numer = numer + value * weight
    merged = (numer / total).astype(BF16).reshape(owners * 8, D)
    lane = lax.broadcasted_iota(jnp.int32, (out_rows, owners * 8), 1)
    for h in range(2):
        pick = jnp.where(lane == col_ref[...] + 2 * h, 1.0, 0.0).astype(BF16)
        att_ref[:, h * D : (h + 1) * D] = dot(pick, merged).astype(BF16)
    half = low_ref.shape[1]
    for b in range(blocks):
        columns = block_columns(2 * b + 1 - core, width)
        value = dot(att_ref[:, 0:half], upper_ref[:, columns])
        out_ref[b] = (value + dot(att_ref[:, half:], low_ref[b])).astype(BF16)


def merge_and_project(me, columns, parts, suffix, upper, low):
    blocks, half, width = low.shape
    out_rows = columns.shape[0]
    return pl.pallas_call(
        merge_kernel,
        in_specs=[SMEM_SPEC] + [VMEM_SPEC] * 6,
        out_specs=[VMEM_SPEC, VMEM_SPEC],
        out_shape=[
            jax.ShapeDtypeStruct((blocks, out_rows, width), BF16),
            jax.ShapeDtypeStruct((out_rows, 2 * half), BF16),
        ],
        compiler_params=PARAMS,
        name="merge_and_project",
    )(me, columns, parts, *suffix, upper, low)


def project_kernel(me_ref, att_ref, upper_ref, low_hbm, out_ref, low_ref, sem):
    blocks, half, width = low_ref.shape
    copies = [
        pltpu.make_async_copy(low_hbm.at[b], low_ref.at[b], sem.at[b]) for b in range(blocks)
    ]
    for copy in copies:
        copy.start()
    for b in range(blocks):
        columns = block_columns(2 * b + me_ref[1], width)
        out_ref[b] = dot(att_ref[:, 0:half], upper_ref[:, columns])
    for copy in copies:
        copy.wait()
    for b in range(blocks):
        out_ref[b] += dot(att_ref[:, half:], low_ref[b])


def project(me, attention, upper, low):
    blocks, half, width = low.shape
    out_rows = attention.shape[0]
    return pl.pallas_call(
        project_kernel,
        in_specs=[SMEM_SPEC, VMEM_SPEC, VMEM_SPEC, HBM_SPEC],
        out_specs=VMEM_SPEC,
        out_shape=jax.ShapeDtypeStruct((blocks, out_rows, width), F32),
        scratch_shapes=[pltpu.VMEM(low.shape, BF16), pltpu.SemaphoreType.DMA((blocks,))],
        cost_estimate=pl.CostEstimate(
            flops=4 * out_rows * half * width * blocks * 8,
            bytes_accessed=4 * half * width * blocks,
            transcendentals=0,
        ),
        compiler_params=PARAMS,
        name="project",
    )(me, attention, upper, in_hbm(low))


def add_kernel(one_ref, two_ref, out_ref):
    out_ref[...] = (one_ref[...] + two_ref[...].astype(F32)).astype(BF16)


def add_halves(one, two):
    return pl.pallas_call(
        add_kernel,
        in_specs=[VMEM_SPEC] * 2,
        out_specs=VMEM_SPEC,
        out_shape=jax.ShapeDtypeStruct(two.shape, BF16),
        compiler_params=PARAMS,
        name="add_halves",
    )(one, two)


def sum_kernel(in_ref, out_ref):
    total = in_ref[0].astype(F32)
    for j in range(1, in_ref.shape[0]):
        total = total + in_ref[j].astype(F32)
    out_ref[...] = total.astype(BF16).reshape(out_ref.shape)


def sum_shares(shares, tokens):
    _, rows, width = shares.shape
    return pl.pallas_call(
        sum_kernel,
        in_specs=[VMEM_SPEC],
        out_specs=VMEM_SPEC,
        out_shape=jax.ShapeDtypeStruct((rows // tokens, tokens, width), BF16),
        compiler_params=PARAMS,
        name="sum_shares",
    )(shares)


def swap(value, axes):
    size = 2 ** len(axes)
    return lax.ppermute(value, axes, [(i, size - 1 - i) for i in range(size)])


def body(
    q_step,
    step_k,
    step_values,
    prefix_k,
    prefix_v,
    suffix_k,
    suffix_values,
    lengths,
    placement,
    output_weight,
):
    tokens = q_step.shape[1]
    indices = lax.axis_size("prompt")
    blocks = lax.axis_size("tensor") * 2
    place = placement[0]
    slots = place.shape[0]
    me = jnp.stack([lax.axis_index("xh"), lax.axis_index("core")]).astype(jnp.int32)
    other = swap(q_step, ("core",))
    own, place_here = own_rows(me, placement, q_step)
    routed = route(me, place_here, own, other, indices)
    routed, prefix_k, prefix_v = lax.optimization_barrier((routed, prefix_k, prefix_v))
    k_other = swap(prefix_k, ("core",))
    v_other = swap(prefix_v, ("core",))
    arrived = lax.all_to_all(
        routed.reshape(indices * 2, 16, D), ("prompt", "xh"), split_axis=0, concat_axis=0, tiled=True
    )
    keep, to_core, to_xh = suffix_attention(
        me, lengths, q_step, step_k, step_values, suffix_k, suffix_values
    )
    near = swap(to_core, ("core",))
    parts = prefix_attention(
        arrived.reshape(indices, 2, 16, D), prefix_k, k_other, prefix_v, v_other
    )
    near, parts = lax.optimization_barrier((near, parts))
    far = swap(jnp.concatenate([to_xh, near[near.shape[0] // 2 :]], axis=0), ("xh",))
    returned = lax.all_to_all(
        parts.reshape(indices * 2, 16, D), ("prompt", "xh"), split_axis=0, concat_axis=0, tiled=True
    )
    upper, low_away, low_mine = stage_weight(me, output_weight, parts, blocks)
    columns = (place[:, None] * 4 + jnp.arange(tokens, dtype=jnp.int32)[None, :]).reshape(
        slots * tokens, 1
    )
    away, attention = merge_and_project(
        me,
        columns,
        returned.reshape(indices, 2, 16, D),
        collect_suffix(me, place_here, (keep, near, far), indices),
        upper,
        low_away,
    )
    away = swap(away, ("core",))
    stay = project(me, attention, upper, low_mine)
    spread = lax.all_to_all(
        add_halves(stay, away), ("tensor", "xh"), split_axis=0, concat_axis=0, tiled=True
    )
    return sum_shares(spread, tokens)


def solution(mesh):
    sizes = mesh.shape
    fine = Mesh(
        mesh.devices.reshape(sizes["tensor"], sizes["prompt"], 2, sizes["cand"] // 2),
        ("tensor", "prompt", "xh", "core"),
    )
    slot = ("prompt", "xh", "core")
    cand = ("xh", "core")
    return jax.shard_map(
        body,
        mesh=fine,
        in_specs=(
            P(slot, None, "tensor"),
            P(slot, None, "tensor"),
            P(slot, None, "tensor"),
            P("prompt", cand, "tensor"),
            P("prompt", cand, "tensor"),
            P(slot, None, "tensor"),
            P(slot, None, "tensor"),
            P(slot),
            P("prompt", None),
            P(("tensor",) + cand, None),
        ),
        out_specs=P("prompt", None, ("tensor",) + cand),
        check_vma=False,
    )
```

```python
import math

import jax
import jax.numpy as jnp
from jax import lax
from jax.experimental import pallas as pl
from jax.experimental.pallas import tpu as pltpu
from jax.sharding import Mesh, PartitionSpec as P

D = 128
SCALE2 = 1.4426950408889634 / math.sqrt(D)
HIDDEN = -1e30
GROUP = 2
CHUNKS = 4
BLOCK = 2048
F32 = jnp.float32
BF16 = jnp.bfloat16
VMEM_LIMIT = 32 * 1024 * 1024

VMEM_SPEC = pl.BlockSpec(memory_space=pltpu.VMEM)
SMEM_SPEC = pl.BlockSpec(memory_space=pltpu.SMEM)
HBM_SPEC = pl.BlockSpec(memory_space=pltpu.HBM)
PARAMS = pltpu.CompilerParams(vmem_limit_bytes=VMEM_LIMIT)


def split_stat(level):
    high = level.astype(BF16).astype(F32)
    rest = level - high
    middle = rest.astype(BF16).astype(F32)
    low = rest - middle
    lane = lax.broadcasted_iota(jnp.int32, (level.shape[0], D), 1)
    return jnp.where(lane == 0, high, jnp.where(lane == 1, middle, jnp.where(lane == 2, low, 0.0)))


def join_stat(block):
    return block[..., 0:1] + block[..., 1:2] + block[..., 2:3]


def dot_t(a, b):
    return lax.dot_general(a, b, (((1,), (1,)), ((), ())), preferred_element_type=F32)


def dot(a, b):
    return lax.dot_general(a, b, (((1,), (0,)), ((), ())), preferred_element_type=F32)


def lower_rows(shape):
    return lax.broadcasted_iota(jnp.int32, shape, len(shape) - 2) < 4


def in_hbm(value):
    return pltpu.with_memory_space_constraint(value, pltpu.HBM)


def split_rows(q_ref, rows):
    slots, tokens, width = q_ref.shape
    for i in range(slots):
        wide = q_ref[i].astype(F32)
        for h in range(width // D):
            place = (h // 4) * 4 + (h % 2) * tokens
            rows[(h // 2) % 2, i, place : place + tokens, :] = wide[:, h * D : (h + 1) * D]


def scatter_rows(q_ref, place_ref, rows, first, core):
    count, tokens, _ = q_ref.shape
    for i in range(count):
        u = place_ref[0, first + i]
        wide = q_ref[i].astype(F32)
        for j in range(4):
            h = 4 * (j // 2) + j % 2
            one = wide[:, h * D : (h + 1) * D]
            two = wide[:, (h + 2) * D : (h + 3) * D]
            rows[u, j * tokens : (j + 1) * tokens, :] = jnp.where(core == 0, one, two)


def own_kernel(me_ref, place_hbm, q_hbm, rows, place_out, place_ref, mine_ref, sem):
    xh, core = me_ref[0], me_ref[1]
    copies = (
        pltpu.make_async_copy(place_hbm, place_ref, sem.at[0]),
        pltpu.make_async_copy(q_hbm, mine_ref, sem.at[1]),
        pltpu.make_async_copy(place_hbm, place_out, sem.at[2]),
    )
    for copy in copies:
        copy.start()
    rows[...] = jnp.zeros_like(rows)
    for copy in copies:
        copy.wait()
    scatter_rows(mine_ref, place_ref, rows, (2 * xh + core) * q_hbm.shape[0], core)


def own_rows(me, placement, mine):
    return pl.pallas_call(
        own_kernel,
        in_specs=[SMEM_SPEC, HBM_SPEC, HBM_SPEC],
        out_specs=[VMEM_SPEC, VMEM_SPEC],
        out_shape=[
            jax.ShapeDtypeStruct((placement.shape[1], 8, D), F32),
            jax.ShapeDtypeStruct(placement.shape, jnp.int32),
        ],
        scratch_shapes=[
            pltpu.SMEM(placement.shape, jnp.int32),
            pltpu.VMEM(mine.shape, BF16),
            pltpu.SemaphoreType.DMA((3,)),
        ],
        cost_estimate=pl.CostEstimate(
            flops=0, bytes_accessed=2 * 1024 * 1024, transcendentals=0
        ),
        compiler_params=PARAMS,
        name="own_rows",
    )(me, in_hbm(placement), in_hbm(mine))


def route_kernel(me_ref, place_ref, own_ref, other_ref, out_ref, rows):
    xh, core = me_ref[0], me_ref[1]
    rows[...] = own_ref[...]
    first = (2 * xh + 1 - core) * other_ref.shape[0]
    scatter_rows(other_ref, place_ref, rows, first, core)
    packed = rows[...].reshape(out_ref.shape[0], 16, D).astype(BF16)
    for j in range(out_ref.shape[1]):
        out_ref[:, j] = packed


def route(me, placement, own, other, indices):
    return pl.pallas_call(
        route_kernel,
        in_specs=[SMEM_SPEC, SMEM_SPEC, VMEM_SPEC, VMEM_SPEC],
        out_specs=VMEM_SPEC,
        out_shape=jax.ShapeDtypeStruct((indices, 2, 16, D), BF16),
        scratch_shapes=[pltpu.VMEM(own.shape, F32)],
        compiler_params=PARAMS,
        name="route_queries",
    )(me, placement, own, other)


def suffix_kernel(me_ref, len_hbm, q_hbm, sk_hbm, sv_hbm, k_hbm, v_hbm, *rest):
    keep_ref, core_ref, xh_ref = rest[:3]
    len_ref, q_ref, sk_ref, sv_ref, rows_ref, keys, values, tiles, small_sem, sem = rest[3:]
    slots, span, _ = k_hbm.shape
    tokens = sk_hbm.shape[1]
    xh, core = me_ref[0], me_ref[1]
    lower = lower_rows((8, D))
    lengths_copy = pltpu.make_async_copy(len_hbm, len_ref, small_sem.at[0])
    lengths_copy.start()
    small = (
        pltpu.make_async_copy(q_hbm, q_ref, small_sem.at[1]),
        pltpu.make_async_copy(sk_hbm, sk_ref, small_sem.at[2]),
        pltpu.make_async_copy(sv_hbm, sv_ref, small_sem.at[3]),
    )

    def copies(i, b):
        part = pl.ds(b * BLOCK, BLOCK)
        return (
            pltpu.make_async_copy(k_hbm.at[i, part], keys.at[i, part], sem.at[0, i, b]),
            pltpu.make_async_copy(v_hbm.at[i, part], values.at[i, part], sem.at[1, i, b]),
        )

    for copy in copies(0, 0) + small:
        copy.start()
    lengths_copy.wait()
    blocks = span // BLOCK
    for i in range(slots):
        for b in range(blocks):
            if i + b > 0:

                @pl.when(b * BLOCK < len_ref[i])
                def _():
                    for copy in copies(i, b):
                        copy.start()

    for copy in small:
        copy.wait()
    split_rows(q_ref, rows_ref)
    rows = 16
    row_token = lax.broadcasted_iota(jnp.int32, (rows, tokens), 0) % tokens
    key_token = lax.broadcasted_iota(jnp.int32, (rows, tokens), 1)
    causal = key_token <= row_token
    position = lax.broadcasted_iota(jnp.int32, (rows, span), 1)
    for first in range(0, slots, GROUP):
        group = range(first, first + GROUP)
        for i in group:
            for b in range(blocks):
                if b == 0:
                    for copy in copies(i, b):
                        copy.wait()
                    continue
                live = b * BLOCK < len_ref[i]

                @pl.when(live)
                def _():
                    for copy in copies(i, b):
                        copy.wait()

                @pl.when(jnp.logical_not(live))
                def _():
                    values[i, b * BLOCK : (b + 1) * BLOCK, :] = jnp.zeros((BLOCK, D), BF16)

        q = [
            jnp.concatenate([rows_ref[0, i], rows_ref[1, i]], axis=0).astype(BF16) for i in group
        ]
        scores = [dot_t(q[n], keys[i]) for n, i in enumerate(group)]
        step_scores = [dot_t(q[n], sk_ref[i]) for n, i in enumerate(group)]
        scores = [
            jnp.where(position < len_ref[i], scores[n] * SCALE2, HIDDEN) for n, i in enumerate(group)
        ]
        step_scores = [jnp.where(causal, x * SCALE2, HIDDEN) for x in step_scores]
        top = [
            jnp.maximum(jnp.max(x, axis=1, keepdims=True), jnp.max(y, axis=1, keepdims=True))
            for x, y in zip(scores, step_scores)
        ]
        weights = [jnp.exp2(x - m) for x, m in zip(scores, top)]
        step_weights = [jnp.exp2(x - m) for x, m in zip(step_scores, top)]
        total = [
            jnp.sum(x, axis=1, keepdims=True) + jnp.sum(y, axis=1, keepdims=True)
            for x, y in zip(weights, step_weights)
        ]
        for n, i in enumerate(group):
            numer = dot(weights[n].astype(BF16), values[i])
            numer = numer + dot(step_weights[n].astype(BF16), sv_ref[i])
            value = numer / total[n]
            stat = split_stat(top[n] + jnp.log2(total[n]))
            for c in range(2):
                one, two = value[c * 8 : c * 8 + 8], stat[c * 8 : c * 8 + 8]
                tiles[c, i] = jnp.where(lower, one, pltpu.roll(two, 4, 0))
                tiles[2 + c, i] = jnp.where(lower, pltpu.roll(one, 4, 0), two)

    def piece(to_xh, to_core):
        return tiles[2 * to_xh + to_core].reshape(slots * 8, D).astype(BF16)

    keep_ref[...] = piece(xh, core)
    core_ref[...] = jnp.concatenate([piece(xh, 1 - core), piece(1 - xh, 1 - core)], axis=0)
    xh_ref[...] = piece(1 - xh, core)


def suffix_attention(me, lengths, q_step, step_k, step_values, suffix_k, suffix_values):
    slots, span, _ = suffix_k.shape
    rows = 16
    piece = jax.ShapeDtypeStruct((slots * 8, D), BF16)
    blocks = span // BLOCK
    return pl.pallas_call(
        suffix_kernel,
        in_specs=[SMEM_SPEC] + [HBM_SPEC] * 6,
        out_specs=[VMEM_SPEC] * 3,
        out_shape=[piece, jax.ShapeDtypeStruct((slots * 16, D), BF16), piece],
        scratch_shapes=[
            pltpu.SMEM(lengths.shape, jnp.int32),
            pltpu.VMEM(q_step.shape, BF16),
            pltpu.VMEM(step_k.shape, BF16),
            pltpu.VMEM(step_values.shape, BF16),
            pltpu.VMEM((2, slots, 8, D), F32),
            pltpu.VMEM((slots, span, D), BF16),
            pltpu.VMEM((slots, span, D), BF16),
            pltpu.VMEM((4, slots, 8, D), F32),
            pltpu.SemaphoreType.DMA((4,)),
            pltpu.SemaphoreType.DMA((2, slots, blocks)),
        ],
        cost_estimate=pl.CostEstimate(
            flops=4 * slots * rows * span * D * 64,
            bytes_accessed=4 * slots * span * D,
            transcendentals=slots * rows * span,
        ),
        compiler_params=PARAMS,
        name="suffix_attention",
    )(
        me,
        in_hbm(lengths),
        in_hbm(q_step),
        in_hbm(step_k),
        in_hbm(step_values),
        in_hbm(suffix_k),
        in_hbm(suffix_values),
    )


def prefix_kernel(q_ref, k_own, k_other, v_own, v_other, out_ref):
    indices = q_ref.shape[0]
    q_both = q_ref[:, 0].astype(F32) + q_ref[:, 1].astype(F32)
    q = [q_both[:, u * 8 : u * 8 + 8].reshape(indices * 8, D).astype(BF16) for u in range(2)]
    scores = [[dot_t(q[u], k[u]) * SCALE2 for k in (k_own, k_other)] for u in range(2)]
    top = [
        jnp.maximum(jnp.max(one, axis=1, keepdims=True), jnp.max(two, axis=1, keepdims=True))
        for one, two in scores
    ]
    weights = [[jnp.exp2(part - top[u]) for part in scores[u]] for u in range(2)]
    total = [sum(jnp.sum(part, axis=1, keepdims=True) for part in weights[u]) for u in range(2)]
    numer = [
        sum(dot(part.astype(BF16), v[u]) for part, v in zip(weights[u], (v_own, v_other)))
        for u in range(2)
    ]
    pair = [
        (
            (numer[u] / total[u]).reshape(indices, 8, D),
            split_stat(top[u] + jnp.log2(total[u])).reshape(indices, 8, D),
        )
        for u in range(2)
    ]
    lower = lower_rows((indices, 8, D))
    for j in range(2):
        halves = []
        for part in range(2):
            one, two = pair[0][part], pair[1][part]
            if j == 0:
                halves.append(jnp.where(lower, one, pltpu.roll(two, 4, 1)))
            else:
                halves.append(jnp.where(lower, pltpu.roll(one, 4, 1), two))
        out_ref[:, j] = jnp.concatenate(halves, axis=1).astype(BF16)


def prefix_attention(q_rows, k_own, k_other, v_own, v_other):
    return pl.pallas_call(
        prefix_kernel,
        in_specs=[VMEM_SPEC] * 5,
        out_specs=VMEM_SPEC,
        out_shape=jax.ShapeDtypeStruct(q_rows.shape, BF16),
        compiler_params=PARAMS,
        name="prefix_attention",
    )(q_rows, k_own, k_other, v_own, v_other)


def low_copies(me_ref, w_hbm, low_ref, sem, which):
    blocks, depth, width = low_ref.shape
    return [
        pltpu.make_async_copy(
            w_hbm.at[pl.ds(depth, depth), block_columns(me_ref, b, which, width)],
            low_ref.at[b],
            sem.at[b],
        )
        for b in range(blocks)
    ]


def stage_kernel(me_ref, w_hbm, after_ref, upper_ref, low_ref, mine_hbm, mine_ref, *sems):
    upper_sem, low_sem, mine_sem, out_sem = sems
    core = me_ref[1]
    chunk = upper_ref.shape[0] // CHUNKS
    mine = low_copies(me_ref, w_hbm, mine_ref, mine_sem, core)
    copies = low_copies(me_ref, w_hbm, low_ref, low_sem, 1 - core)
    for j in range(CHUNKS):
        part = pl.ds(j * chunk, chunk)
        copies.append(pltpu.make_async_copy(w_hbm.at[part], upper_ref.at[part], upper_sem.at[j]))
    for copy in mine + copies:
        copy.start()
    out = [
        pltpu.make_async_copy(mine_ref.at[b], mine_hbm.at[b], out_sem.at[b])
        for b in range(len(mine))
    ]
    for arrived, copy in zip(mine, out):
        arrived.wait()
        copy.start()
    for copy in copies + out:
        copy.wait()


def stage_weight(me, weight, after, blocks):
    depth, width = weight.shape
    low = (blocks, depth // 2, width // (2 * blocks))
    return pl.pallas_call(
        stage_kernel,
        in_specs=[SMEM_SPEC, HBM_SPEC, pl.BlockSpec(memory_space=pl.ANY)],
        out_specs=[VMEM_SPEC, VMEM_SPEC, HBM_SPEC],
        out_shape=[
            jax.ShapeDtypeStruct((depth // 2, width), BF16),
            jax.ShapeDtypeStruct(low, BF16),
            pltpu.HBM(low, BF16),
        ],
        scratch_shapes=[
            pltpu.VMEM(low, BF16),
            pltpu.SemaphoreType.DMA((CHUNKS,)),
            pltpu.SemaphoreType.DMA((blocks,)),
            pltpu.SemaphoreType.DMA((blocks,)),
            pltpu.SemaphoreType.DMA((blocks,)),
        ],
        cost_estimate=pl.CostEstimate(
            flops=0, bytes_accessed=5 * depth * width, transcendentals=0
        ),
        compiler_params=PARAMS,
        name="stage_weight",
    )(me, in_hbm(weight), after)


def block_columns(me_ref, step, which, width):
    ahead = (me_ref[2] + step // 2) % 4
    xh = me_ref[0] if step % 2 == 0 else 1 - me_ref[0]
    block = 4 * ahead + 2 * xh + which
    return pl.ds(pl.multiple_of(block * width, width), width)


def collect_kernel(me_ref, place_ref, keep_ref, near_ref, far_ref, value_ref, level_ref, own):
    xh, core = me_ref[0], me_ref[1]
    owners = value_ref.shape[0]
    count = keep_ref.shape[0] // 8
    pieces = ((keep_ref, 0, xh, core), (near_ref, 0, xh, 1 - core))
    pieces += ((far_ref, 0, 1 - xh, core), (far_ref, count, 1 - xh, 1 - core))
    for ref, start, from_xh, from_core in pieces:
        value = ref[start * 8 : (start + count) * 8, :].astype(F32)
        for i in range(count):
            slot = (2 * from_xh + from_core) * count + i
            own[place_ref[0, slot]] = value[i * 8 : (i + 1) * 8]
    lower = lower_rows((owners, 8, D))
    both = own[...].reshape(owners, 2, 8, D)
    one, two = both[:, 0], both[:, 1]
    value_ref[...] = jnp.where(lower, one, pltpu.roll(two, 4, 1))
    level = join_stat(jnp.where(lower, pltpu.roll(one, 4, 1), two))
    level_ref[...] = jnp.broadcast_to(level, level_ref.shape)


def collect_suffix(me, placement, pieces, owners):
    part = jax.ShapeDtypeStruct((owners, 8, D), F32)
    return pl.pallas_call(
        collect_kernel,
        in_specs=[SMEM_SPEC] * 2 + [VMEM_SPEC] * 3,
        out_specs=[VMEM_SPEC] * 2,
        out_shape=[part, part],
        scratch_shapes=[pltpu.VMEM((placement.shape[1], 8, D), F32)],
        cost_estimate=pl.CostEstimate(
            flops=0, bytes_accessed=1024 * 1024, transcendentals=0
        ),
        compiler_params=PARAMS,
        name="collect_suffix",
    )(me, placement, *pieces)


def merge_kernel(
    me_ref, col_ref, parts_ref, value_ref, level_ref, upper_ref, low_ref, out_ref, att_ref
):
    core = me_ref[1]
    blocks, out_rows, width = out_ref.shape
    owners = parts_ref.shape[0]
    values = [value_ref[...]]
    levels = [level_ref[...]]
    for c in range(parts_ref.shape[1]):
        block = parts_ref[:, c].astype(F32)
        values.append(block[:, 0:8])
        levels.append(jnp.broadcast_to(join_stat(block[:, 8:16]), level_ref.shape))
    top = levels[0]
    for level in levels[1:]:
        top = jnp.maximum(top, level)
    total = jnp.zeros_like(top)
    numer = jnp.zeros_like(values[0])
    for value, level in zip(values, levels):
        weight = jnp.exp2(level - top)
        total = total + weight
        numer = numer + value * weight
    merged = (numer / total).astype(BF16).reshape(owners * 8, D)
    lane = lax.broadcasted_iota(jnp.int32, (out_rows, owners * 8), 1)
    for h in range(2):
        pick = jnp.where(lane == col_ref[...] + 2 * h, 1.0, 0.0).astype(BF16)
        att_ref[:, h * D : (h + 1) * D] = dot(pick, merged).astype(BF16)
    half = low_ref.shape[1]
    for b in range(blocks):
        columns = block_columns(me_ref, b, 1 - core, width)
        value = dot(att_ref[:, 0:half], upper_ref[:, columns])
        out_ref[b] = (value + dot(att_ref[:, half:], low_ref[b])).astype(BF16)


def merge_and_project(me, columns, parts, suffix, upper, low):
    blocks, half, width = low.shape
    out_rows = columns.shape[0]
    return pl.pallas_call(
        merge_kernel,
        in_specs=[SMEM_SPEC] + [VMEM_SPEC] * 6,
        out_specs=[VMEM_SPEC, VMEM_SPEC],
        out_shape=[
            jax.ShapeDtypeStruct((blocks, out_rows, width), BF16),
            jax.ShapeDtypeStruct((out_rows, 2 * half), BF16),
        ],
        compiler_params=PARAMS,
        name="merge_and_project",
    )(me, columns, parts, *suffix, upper, low)


def project_kernel(me_ref, att_ref, upper_ref, low_hbm, out_ref, low_ref, sem):
    blocks, half, width = low_ref.shape
    copies = [
        pltpu.make_async_copy(low_hbm.at[b], low_ref.at[b], sem.at[b]) for b in range(blocks)
    ]
    for copy in copies:
        copy.start()
    for b in range(blocks):
        columns = block_columns(me_ref, b, me_ref[1], width)
        out_ref[b] = dot(att_ref[:, 0:half], upper_ref[:, columns])
    for copy in copies:
        copy.wait()
    for b in range(blocks):
        out_ref[b] += dot(att_ref[:, half:], low_ref[b])


def project(me, attention, upper, low):
    blocks, half, width = low.shape
    out_rows = attention.shape[0]
    return pl.pallas_call(
        project_kernel,
        in_specs=[SMEM_SPEC, VMEM_SPEC, VMEM_SPEC, HBM_SPEC],
        out_specs=VMEM_SPEC,
        out_shape=jax.ShapeDtypeStruct((blocks, out_rows, width), F32),
        scratch_shapes=[pltpu.VMEM(low.shape, BF16), pltpu.SemaphoreType.DMA((blocks,))],
        cost_estimate=pl.CostEstimate(
            flops=4 * out_rows * half * width * blocks * 8,
            bytes_accessed=4 * half * width * blocks,
            transcendentals=0,
        ),
        compiler_params=PARAMS,
        name="project",
    )(me, attention, upper, in_hbm(low))


def add_kernel(one_ref, two_ref, keep_ref, *out_refs):
    keep_ref[...] = one_ref[0:2] + two_ref[0:2].astype(F32)
    for b, out_ref in enumerate(out_refs, 1):
        value = one_ref[2 * b : 2 * b + 2] + two_ref[2 * b : 2 * b + 2].astype(F32)
        out_ref[...] = value.astype(BF16)


def add_halves(one, two):
    steps = one.shape[0] // 2
    shape = (2,) + one.shape[1:]
    return pl.pallas_call(
        add_kernel,
        in_specs=[VMEM_SPEC] * 2,
        out_specs=[VMEM_SPEC] * steps,
        out_shape=[jax.ShapeDtypeStruct(shape, F32)]
        + [jax.ShapeDtypeStruct(shape, BF16)] * (steps - 1),
        compiler_params=PARAMS,
        name="add_halves",
    )(one, two)


def tensor_kernel(keep_ref, *rest):
    in_refs, stay_ref, away_ref = rest[:-2], rest[-2], rest[-1]
    for away, out_ref in ((0, stay_ref), (1, away_ref)):
        total = keep_ref[away]
        for ref in in_refs:
            total = total + ref[away].astype(F32)
        out_ref[...] = total.astype(out_ref.dtype)


def sum_tensor(keep, shares):
    shape = keep.shape[1:]
    return pl.pallas_call(
        tensor_kernel,
        in_specs=[VMEM_SPEC] * (1 + len(shares)),
        out_specs=[VMEM_SPEC] * 2,
        out_shape=[jax.ShapeDtypeStruct(shape, F32), jax.ShapeDtypeStruct(shape, BF16)],
        compiler_params=PARAMS,
        name="sum_tensor",
    )(keep, *shares)


def sum_kernel(one_ref, two_ref, out_ref):
    total = one_ref[...] + two_ref[...].astype(F32)
    out_ref[...] = total.astype(BF16).reshape(out_ref.shape)


def sum_shares(one, two, tokens):
    rows, width = one.shape
    return pl.pallas_call(
        sum_kernel,
        in_specs=[VMEM_SPEC] * 2,
        out_specs=VMEM_SPEC,
        out_shape=jax.ShapeDtypeStruct((rows // tokens, tokens, width), BF16),
        compiler_params=PARAMS,
        name="sum_shares",
    )(one, two)


def swap(value, axes):
    size = 2 ** len(axes)
    return lax.ppermute(value, axes, [(i, size - 1 - i) for i in range(size)])


def body(
    q_step,
    step_k,
    step_values,
    prefix_k,
    prefix_v,
    suffix_k,
    suffix_values,
    lengths,
    placement,
    output_weight,
):
    tokens = q_step.shape[1]
    indices = lax.axis_size("prompt")
    blocks = lax.axis_size("tensor") * 2
    place = placement[0]
    slots = place.shape[0]
    me = jnp.stack([lax.axis_index("xh"), lax.axis_index("core"), lax.axis_index("tensor")]).astype(jnp.int32)
    other = swap(q_step, ("core",))
    own, place_here = own_rows(me, placement, q_step)
    routed = route(me, place_here, own, other, indices)
    routed, prefix_k, prefix_v = lax.optimization_barrier((routed, prefix_k, prefix_v))
    k_other = swap(prefix_k, ("core",))
    v_other = swap(prefix_v, ("core",))
    arrived = lax.all_to_all(
        routed.reshape(indices * 2, 16, D), ("prompt", "xh"), split_axis=0, concat_axis=0, tiled=True
    )
    keep, to_core, to_xh = suffix_attention(
        me, lengths, q_step, step_k, step_values, suffix_k, suffix_values
    )
    near = swap(to_core, ("core",))
    parts = prefix_attention(
        arrived.reshape(indices, 2, 16, D), prefix_k, k_other, prefix_v, v_other
    )
    near, parts = lax.optimization_barrier((near, parts))
    far = swap(jnp.concatenate([to_xh, near[near.shape[0] // 2 :]], axis=0), ("xh",))
    returned = lax.all_to_all(
        parts.reshape(indices * 2, 16, D), ("prompt", "xh"), split_axis=0, concat_axis=0, tiled=True
    )
    upper, low_away, low_mine = stage_weight(me, output_weight, parts, blocks)
    columns = (place[:, None] * 4 + jnp.arange(tokens, dtype=jnp.int32)[None, :]).reshape(
        slots * tokens, 1
    )
    away, attention = merge_and_project(
        me,
        columns,
        returned.reshape(indices, 2, 16, D),
        collect_suffix(me, place_here, (keep, near, far), indices),
        upper,
        low_away,
    )
    away = swap(away, ("core",))
    stay = project(me, attention, upper, low_mine)
    keep_t, *shares = add_halves(stay, away)
    steps = blocks // 2
    shares = [
        lax.ppermute(shares[b - 1], "tensor", [(i, (i + b) % steps) for i in range(steps)])
        for b in (2, 1, 3)
    ]
    one, two = sum_tensor(keep_t, shares)
    return sum_shares(one, swap(two, ("xh",)), tokens)


def solution(mesh):
    sizes = mesh.shape
    fine = Mesh(
        mesh.devices.reshape(sizes["tensor"], sizes["prompt"], 2, sizes["cand"] // 2),
        ("tensor", "prompt", "xh", "core"),
    )
    slot = ("prompt", "xh", "core")
    cand = ("xh", "core")
    return jax.shard_map(
        body,
        mesh=fine,
        in_specs=(
            P(slot, None, "tensor"),
            P(slot, None, "tensor"),
            P(slot, None, "tensor"),
            P("prompt", cand, "tensor"),
            P("prompt", cand, "tensor"),
            P(slot, None, "tensor"),
            P(slot, None, "tensor"),
            P(slot),
            P("prompt", None),
            P(("tensor",) + cand, None),
        ),
        out_specs=P("prompt", None, ("tensor",) + cand),
        check_vma=False,
    )
```

```python
import math

import jax
import jax.numpy as jnp
from jax import lax
from jax.experimental import pallas as pl
from jax.experimental.pallas import tpu as pltpu
from jax.sharding import Mesh, PartitionSpec as P

D = 128
SCALE2 = 1.4426950408889634 / math.sqrt(D)
HIDDEN = -1e30
GROUP = 2
CHUNKS = 4
BLOCK = 2048
F32 = jnp.float32
BF16 = jnp.bfloat16
VMEM_LIMIT = 32 * 1024 * 1024

VMEM_SPEC = pl.BlockSpec(memory_space=pltpu.VMEM)
SMEM_SPEC = pl.BlockSpec(memory_space=pltpu.SMEM)
HBM_SPEC = pl.BlockSpec(memory_space=pltpu.HBM)
PARAMS = pltpu.CompilerParams(vmem_limit_bytes=VMEM_LIMIT)


def split_stat(level):
    high = level.astype(BF16).astype(F32)
    rest = level - high
    middle = rest.astype(BF16).astype(F32)
    low = rest - middle
    lane = lax.broadcasted_iota(jnp.int32, (level.shape[0], D), 1)
    return jnp.where(lane == 0, high, jnp.where(lane == 1, middle, jnp.where(lane == 2, low, 0.0)))


def join_stat(block):
    return block[..., 0:1] + block[..., 1:2] + block[..., 2:3]


def dot_t(a, b):
    return lax.dot_general(a, b, (((1,), (1,)), ((), ())), preferred_element_type=F32)


def dot(a, b):
    return lax.dot_general(a, b, (((1,), (0,)), ((), ())), preferred_element_type=F32)


def lower_rows(shape):
    return lax.broadcasted_iota(jnp.int32, shape, len(shape) - 2) < 4


def here():
    return tuple(lax.axis_index(name) for name in ("xh", "core", "tensor"))


def in_hbm(value):
    return pltpu.with_memory_space_constraint(value, pltpu.HBM)


def split_rows(q_ref, rows):
    slots, tokens, width = q_ref.shape
    for i in range(slots):
        wide = q_ref[i].astype(F32)
        for h in range(width // D):
            place = (h // 4) * 4 + (h % 2) * tokens
            rows[(h // 2) % 2, i, place : place + tokens, :] = wide[:, h * D : (h + 1) * D]


def scatter_rows(q_ref, place_ref, rows, first, core):
    count, tokens, _ = q_ref.shape
    for i in range(count):
        u = place_ref[0, first + i]
        wide = q_ref[i].astype(F32)
        for j in range(4):
            h = 4 * (j // 2) + j % 2
            one = wide[:, h * D : (h + 1) * D]
            two = wide[:, (h + 2) * D : (h + 3) * D]
            rows[u, j * tokens : (j + 1) * tokens, :] = jnp.where(core == 0, one, two)


def own_kernel(place_hbm, q_hbm, rows, place_out, place_ref, mine_ref, sem):
    me_ref = here()
    xh, core = me_ref[0], me_ref[1]
    copies = (
        pltpu.make_async_copy(place_hbm, place_ref, sem.at[0]),
        pltpu.make_async_copy(q_hbm, mine_ref, sem.at[1]),
        pltpu.make_async_copy(place_hbm, place_out, sem.at[2]),
    )
    for copy in copies:
        copy.start()
    rows[...] = jnp.zeros_like(rows)
    for copy in copies:
        copy.wait()
    scatter_rows(mine_ref, place_ref, rows, (2 * xh + core) * q_hbm.shape[0], core)


def own_rows(placement, mine):
    return pl.pallas_call(
        own_kernel,
        in_specs=[HBM_SPEC, HBM_SPEC],
        out_specs=[VMEM_SPEC, VMEM_SPEC],
        out_shape=[
            jax.ShapeDtypeStruct((placement.shape[1], 8, D), F32),
            jax.ShapeDtypeStruct(placement.shape, jnp.int32),
        ],
        scratch_shapes=[
            pltpu.SMEM(placement.shape, jnp.int32),
            pltpu.VMEM(mine.shape, BF16),
            pltpu.SemaphoreType.DMA((3,)),
        ],
        cost_estimate=pl.CostEstimate(
            flops=0, bytes_accessed=2 * 1024 * 1024, transcendentals=0
        ),
        compiler_params=PARAMS,
        name="own_rows",
    )(in_hbm(placement), in_hbm(mine))


def route_kernel(place_ref, own_ref, other_ref, out_ref, rows):
    me_ref = here()
    xh, core = me_ref[0], me_ref[1]
    rows[...] = own_ref[...]
    first = (2 * xh + 1 - core) * other_ref.shape[0]
    scatter_rows(other_ref, place_ref, rows, first, core)
    packed = rows[...].reshape(out_ref.shape[0], 16, D).astype(BF16)
    for j in range(out_ref.shape[1]):
        out_ref[:, j] = packed


def route(placement, own, other, indices):
    return pl.pallas_call(
        route_kernel,
        in_specs=[SMEM_SPEC, VMEM_SPEC, VMEM_SPEC],
        out_specs=VMEM_SPEC,
        out_shape=jax.ShapeDtypeStruct((indices, 2, 16, D), BF16),
        scratch_shapes=[pltpu.VMEM(own.shape, F32)],
        compiler_params=PARAMS,
        name="route_queries",
    )(placement, own, other)


def suffix_kernel(len_hbm, q_hbm, sk_hbm, sv_hbm, k_hbm, v_hbm, *rest):
    me_ref = here()
    keep_ref, core_ref, xh_ref = rest[:3]
    len_ref, q_ref, sk_ref, sv_ref, rows_ref, keys, values, tiles, small_sem, sem = rest[3:]
    slots, span, _ = k_hbm.shape
    tokens = sk_hbm.shape[1]
    xh, core = me_ref[0], me_ref[1]
    lower = lower_rows((8, D))
    lengths_copy = pltpu.make_async_copy(len_hbm, len_ref, small_sem.at[0])
    lengths_copy.start()
    small = (
        pltpu.make_async_copy(q_hbm, q_ref, small_sem.at[1]),
        pltpu.make_async_copy(sk_hbm, sk_ref, small_sem.at[2]),
        pltpu.make_async_copy(sv_hbm, sv_ref, small_sem.at[3]),
    )

    def copies(i, b):
        part = pl.ds(b * BLOCK, BLOCK)
        return (
            pltpu.make_async_copy(k_hbm.at[i, part], keys.at[i, part], sem.at[0, i, b]),
            pltpu.make_async_copy(v_hbm.at[i, part], values.at[i, part], sem.at[1, i, b]),
        )

    for copy in copies(0, 0) + small:
        copy.start()
    lengths_copy.wait()
    blocks = span // BLOCK
    for i in range(slots):
        for b in range(blocks):
            if i + b > 0:

                @pl.when(b * BLOCK < len_ref[i])
                def _():
                    for copy in copies(i, b):
                        copy.start()

    for copy in small:
        copy.wait()
    split_rows(q_ref, rows_ref)
    rows = 16
    row_token = lax.broadcasted_iota(jnp.int32, (rows, tokens), 0) % tokens
    key_token = lax.broadcasted_iota(jnp.int32, (rows, tokens), 1)
    causal = key_token <= row_token
    position = lax.broadcasted_iota(jnp.int32, (rows, span), 1)
    for first in range(0, slots, GROUP):
        group = range(first, first + GROUP)
        for i in group:
            for b in range(blocks):
                if b == 0:
                    for copy in copies(i, b):
                        copy.wait()
                    continue
                live = b * BLOCK < len_ref[i]

                @pl.when(live)
                def _():
                    for copy in copies(i, b):
                        copy.wait()

                @pl.when(jnp.logical_not(live))
                def _():
                    values[i, b * BLOCK : (b + 1) * BLOCK, :] = jnp.zeros((BLOCK, D), BF16)

        q = [
            jnp.concatenate([rows_ref[0, i], rows_ref[1, i]], axis=0).astype(BF16) for i in group
        ]
        scores = [dot_t(q[n], keys[i]) for n, i in enumerate(group)]
        step_scores = [dot_t(q[n], sk_ref[i]) for n, i in enumerate(group)]
        scores = [
            jnp.where(position < len_ref[i], scores[n] * SCALE2, HIDDEN) for n, i in enumerate(group)
        ]
        step_scores = [jnp.where(causal, x * SCALE2, HIDDEN) for x in step_scores]
        top = [
            jnp.maximum(jnp.max(x, axis=1, keepdims=True), jnp.max(y, axis=1, keepdims=True))
            for x, y in zip(scores, step_scores)
        ]
        weights = [jnp.exp2(x - m) for x, m in zip(scores, top)]
        step_weights = [jnp.exp2(x - m) for x, m in zip(step_scores, top)]
        total = [
            jnp.sum(x, axis=1, keepdims=True) + jnp.sum(y, axis=1, keepdims=True)
            for x, y in zip(weights, step_weights)
        ]
        for n, i in enumerate(group):
            numer = dot(weights[n].astype(BF16), values[i])
            numer = numer + dot(step_weights[n].astype(BF16), sv_ref[i])
            value = numer / total[n]
            stat = split_stat(top[n] + jnp.log2(total[n]))
            for c in range(2):
                one, two = value[c * 8 : c * 8 + 8], stat[c * 8 : c * 8 + 8]
                tiles[c, i] = jnp.where(lower, one, pltpu.roll(two, 4, 0))
                tiles[2 + c, i] = jnp.where(lower, pltpu.roll(one, 4, 0), two)

    def piece(to_xh, to_core):
        return tiles[2 * to_xh + to_core].reshape(slots * 8, D).astype(BF16)

    keep_ref[...] = piece(xh, core)
    core_ref[...] = jnp.concatenate([piece(xh, 1 - core), piece(1 - xh, 1 - core)], axis=0)
    xh_ref[...] = piece(1 - xh, core)


def suffix_attention(lengths, q_step, step_k, step_values, suffix_k, suffix_values):
    slots, span, _ = suffix_k.shape
    rows = 16
    piece = jax.ShapeDtypeStruct((slots * 8, D), BF16)
    blocks = span // BLOCK
    return pl.pallas_call(
        suffix_kernel,
        in_specs=[HBM_SPEC] * 6,
        out_specs=[VMEM_SPEC] * 3,
        out_shape=[piece, jax.ShapeDtypeStruct((slots * 16, D), BF16), piece],
        scratch_shapes=[
            pltpu.SMEM(lengths.shape, jnp.int32),
            pltpu.VMEM(q_step.shape, BF16),
            pltpu.VMEM(step_k.shape, BF16),
            pltpu.VMEM(step_values.shape, BF16),
            pltpu.VMEM((2, slots, 8, D), F32),
            pltpu.VMEM((slots, span, D), BF16),
            pltpu.VMEM((slots, span, D), BF16),
            pltpu.VMEM((4, slots, 8, D), F32),
            pltpu.SemaphoreType.DMA((4,)),
            pltpu.SemaphoreType.DMA((2, slots, blocks)),
        ],
        cost_estimate=pl.CostEstimate(
            flops=4 * slots * rows * span * D * 64,
            bytes_accessed=4 * slots * span * D,
            transcendentals=slots * rows * span,
        ),
        compiler_params=PARAMS,
        name="suffix_attention",
    )(
        in_hbm(lengths),
        in_hbm(q_step),
        in_hbm(step_k),
        in_hbm(step_values),
        in_hbm(suffix_k),
        in_hbm(suffix_values),
    )


def prefix_kernel(q_ref, k_own, k_other, v_own, v_other, out_ref):
    indices = q_ref.shape[0]
    q_both = q_ref[:, 0].astype(F32) + q_ref[:, 1].astype(F32)
    q = [q_both[:, u * 8 : u * 8 + 8].reshape(indices * 8, D).astype(BF16) for u in range(2)]
    scores = [[dot_t(q[u], k[u]) * SCALE2 for k in (k_own, k_other)] for u in range(2)]
    top = [
        jnp.maximum(jnp.max(one, axis=1, keepdims=True), jnp.max(two, axis=1, keepdims=True))
        for one, two in scores
    ]
    weights = [[jnp.exp2(part - top[u]) for part in scores[u]] for u in range(2)]
    total = [sum(jnp.sum(part, axis=1, keepdims=True) for part in weights[u]) for u in range(2)]
    numer = [
        sum(dot(part.astype(BF16), v[u]) for part, v in zip(weights[u], (v_own, v_other)))
        for u in range(2)
    ]
    pair = [
        (
            (numer[u] / total[u]).reshape(indices, 8, D),
            split_stat(top[u] + jnp.log2(total[u])).reshape(indices, 8, D),
        )
        for u in range(2)
    ]
    lower = lower_rows((indices, 8, D))
    for j in range(2):
        halves = []
        for part in range(2):
            one, two = pair[0][part], pair[1][part]
            if j == 0:
                halves.append(jnp.where(lower, one, pltpu.roll(two, 4, 1)))
            else:
                halves.append(jnp.where(lower, pltpu.roll(one, 4, 1), two))
        out_ref[:, j] = jnp.concatenate(halves, axis=1).astype(BF16)


def prefix_attention(q_rows, k_own, k_other, v_own, v_other):
    return pl.pallas_call(
        prefix_kernel,
        in_specs=[VMEM_SPEC] * 5,
        out_specs=VMEM_SPEC,
        out_shape=jax.ShapeDtypeStruct(q_rows.shape, BF16),
        compiler_params=PARAMS,
        name="prefix_attention",
    )(q_rows, k_own, k_other, v_own, v_other)


def low_copies(me_ref, w_hbm, low_ref, sem, which):
    blocks, depth, width = low_ref.shape
    return [
        pltpu.make_async_copy(
            w_hbm.at[pl.ds(depth, depth), block_columns(me_ref, b, which, width)],
            low_ref.at[b],
            sem.at[b],
        )
        for b in range(blocks)
    ]


def stage_kernel(w_hbm, after_ref, upper_ref, low_ref, mine_hbm, mine_ref, *sems):
    me_ref = here()
    upper_sem, low_sem, mine_sem, out_sem = sems
    core = me_ref[1]
    chunk = upper_ref.shape[0] // CHUNKS
    mine = low_copies(me_ref, w_hbm, mine_ref, mine_sem, core)
    copies = low_copies(me_ref, w_hbm, low_ref, low_sem, 1 - core)
    for j in range(CHUNKS):
        part = pl.ds(j * chunk, chunk)
        copies.append(pltpu.make_async_copy(w_hbm.at[part], upper_ref.at[part], upper_sem.at[j]))
    for copy in mine + copies:
        copy.start()
    out = [
        pltpu.make_async_copy(mine_ref.at[b], mine_hbm.at[b], out_sem.at[b])
        for b in range(len(mine))
    ]
    for arrived, copy in zip(mine, out):
        arrived.wait()
        copy.start()
    for copy in copies + out:
        copy.wait()


def stage_weight(weight, after, blocks):
    depth, width = weight.shape
    low = (blocks, depth // 2, width // (2 * blocks))
    return pl.pallas_call(
        stage_kernel,
        in_specs=[HBM_SPEC, pl.BlockSpec(memory_space=pl.ANY)],
        out_specs=[VMEM_SPEC, VMEM_SPEC, HBM_SPEC],
        out_shape=[
            jax.ShapeDtypeStruct((depth // 2, width), BF16),
            jax.ShapeDtypeStruct(low, BF16),
            pltpu.HBM(low, BF16),
        ],
        scratch_shapes=[
            pltpu.VMEM(low, BF16),
            pltpu.SemaphoreType.DMA((CHUNKS,)),
            pltpu.SemaphoreType.DMA((blocks,)),
            pltpu.SemaphoreType.DMA((blocks,)),
            pltpu.SemaphoreType.DMA((blocks,)),
        ],
        cost_estimate=pl.CostEstimate(
            flops=0, bytes_accessed=5 * depth * width, transcendentals=0
        ),
        compiler_params=PARAMS,
        name="stage_weight",
    )(in_hbm(weight), after)


def block_columns(me_ref, step, which, width):
    ahead = (me_ref[2] + step // 2) % 4
    xh = me_ref[0] if step % 2 == 0 else 1 - me_ref[0]
    block = 4 * ahead + 2 * xh + which
    return pl.ds(pl.multiple_of(block * width, width), width)


def collect_kernel(place_ref, keep_ref, near_ref, far_ref, value_ref, level_ref, own):
    xh, core, _ = here()
    owners = value_ref.shape[0]
    count = keep_ref.shape[0] // 8
    pieces = ((keep_ref, 0, xh, core), (near_ref, 0, xh, 1 - core))
    pieces += ((far_ref, 0, 1 - xh, core), (far_ref, count, 1 - xh, 1 - core))
    for ref, start, from_xh, from_core in pieces:
        value = ref[start * 8 : (start + count) * 8, :].astype(F32)
        for i in range(count):
            slot = (2 * from_xh + from_core) * count + i
            own[place_ref[0, slot]] = value[i * 8 : (i + 1) * 8]
    lower = lower_rows((owners, 8, D))
    both = own[...].reshape(owners, 2, 8, D)
    one, two = both[:, 0], both[:, 1]
    value_ref[...] = jnp.where(lower, one, pltpu.roll(two, 4, 1))
    level = join_stat(jnp.where(lower, pltpu.roll(one, 4, 1), two))
    level_ref[...] = jnp.broadcast_to(level, level_ref.shape)


def collect_suffix(placement, pieces, owners):
    part = jax.ShapeDtypeStruct((owners, 8, D), F32)
    return pl.pallas_call(
        collect_kernel,
        in_specs=[SMEM_SPEC] + [VMEM_SPEC] * 3,
        out_specs=[VMEM_SPEC] * 2,
        out_shape=[part, part],
        scratch_shapes=[pltpu.VMEM((placement.shape[1], 8, D), F32)],
        cost_estimate=pl.CostEstimate(
            flops=0, bytes_accessed=1024 * 1024, transcendentals=0
        ),
        compiler_params=PARAMS,
        name="collect_suffix",
    )(placement, *pieces)


def merge_kernel(
    col_ref, parts_ref, value_ref, level_ref, upper_ref, low_ref, out_ref, att_ref
):
    me_ref = here()
    core = me_ref[1]
    blocks, out_rows, width = out_ref.shape
    owners = parts_ref.shape[0]
    values = [value_ref[...]]
    levels = [level_ref[...]]
    for c in range(parts_ref.shape[1]):
        block = parts_ref[:, c].astype(F32)
        values.append(block[:, 0:8])
        levels.append(jnp.broadcast_to(join_stat(block[:, 8:16]), level_ref.shape))
    top = levels[0]
    for level in levels[1:]:
        top = jnp.maximum(top, level)
    total = jnp.zeros_like(top)
    numer = jnp.zeros_like(values[0])
    for value, level in zip(values, levels):
        weight = jnp.exp2(level - top)
        total = total + weight
        numer = numer + value * weight
    merged = (numer / total).astype(BF16).reshape(owners * 8, D)
    lane = lax.broadcasted_iota(jnp.int32, (out_rows, owners * 8), 1)
    for h in range(2):
        pick = jnp.where(lane == col_ref[...] + 2 * h, 1.0, 0.0).astype(BF16)
        att_ref[:, h * D : (h + 1) * D] = dot(pick, merged).astype(BF16)
    half = low_ref.shape[1]
    for b in range(blocks):
        columns = block_columns(me_ref, b, 1 - core, width)
        value = dot(att_ref[:, 0:half], upper_ref[:, columns])
        out_ref[b] = (value + dot(att_ref[:, half:], low_ref[b])).astype(BF16)


def merge_and_project(columns, parts, suffix, upper, low):
    blocks, half, width = low.shape
    out_rows = columns.shape[0]
    return pl.pallas_call(
        merge_kernel,
        in_specs=[VMEM_SPEC] * 6,
        out_specs=[VMEM_SPEC, VMEM_SPEC],
        out_shape=[
            jax.ShapeDtypeStruct((blocks, out_rows, width), BF16),
            jax.ShapeDtypeStruct((out_rows, 2 * half), BF16),
        ],
        compiler_params=PARAMS,
        name="merge_and_project",
    )(columns, parts, *suffix, upper, low)


def project_kernel(att_ref, upper_ref, low_hbm, out_ref, low_ref, sem):
    me_ref = here()
    blocks, half, width = low_ref.shape
    copies = [
        pltpu.make_async_copy(low_hbm.at[b], low_ref.at[b], sem.at[b]) for b in range(blocks)
    ]
    for copy in copies:
        copy.start()
    for b in range(blocks):
        columns = block_columns(me_ref, b, me_ref[1], width)
        out_ref[b] = dot(att_ref[:, 0:half], upper_ref[:, columns])
    for copy in copies:
        copy.wait()
    for b in range(blocks):
        out_ref[b] += dot(att_ref[:, half:], low_ref[b])


def project(attention, upper, low):
    blocks, half, width = low.shape
    out_rows = attention.shape[0]
    return pl.pallas_call(
        project_kernel,
        in_specs=[VMEM_SPEC, VMEM_SPEC, HBM_SPEC],
        out_specs=VMEM_SPEC,
        out_shape=jax.ShapeDtypeStruct((blocks, out_rows, width), F32),
        scratch_shapes=[pltpu.VMEM(low.shape, BF16), pltpu.SemaphoreType.DMA((blocks,))],
        cost_estimate=pl.CostEstimate(
            flops=4 * out_rows * half * width * blocks * 8,
            bytes_accessed=4 * half * width * blocks,
            transcendentals=0,
        ),
        compiler_params=PARAMS,
        name="project",
    )(attention, upper, in_hbm(low))


def add_kernel(one_ref, two_ref, keep_ref, *out_refs):
    keep_ref[...] = one_ref[0:2] + two_ref[0:2].astype(F32)
    for b, out_ref in enumerate(out_refs, 1):
        value = one_ref[2 * b : 2 * b + 2] + two_ref[2 * b : 2 * b + 2].astype(F32)
        out_ref[...] = value.astype(BF16)


def add_halves(one, two):
    steps = one.shape[0] // 2
    shape = (2,) + one.shape[1:]
    return pl.pallas_call(
        add_kernel,
        in_specs=[VMEM_SPEC] * 2,
        out_specs=[VMEM_SPEC] * steps,
        out_shape=[jax.ShapeDtypeStruct(shape, F32)]
        + [jax.ShapeDtypeStruct(shape, BF16)] * (steps - 1),
        compiler_params=PARAMS,
        name="add_halves",
    )(one, two)


def tensor_kernel(keep_ref, *rest):
    in_refs, stay_ref, away_ref = rest[:-2], rest[-2], rest[-1]
    for away, out_ref in ((0, stay_ref), (1, away_ref)):
        total = keep_ref[away]
        for ref in in_refs:
            total = total + ref[away].astype(F32)
        out_ref[...] = total.astype(out_ref.dtype)


def sum_tensor(keep, shares):
    shape = keep.shape[1:]
    return pl.pallas_call(
        tensor_kernel,
        in_specs=[VMEM_SPEC] * (1 + len(shares)),
        out_specs=[VMEM_SPEC] * 2,
        out_shape=[jax.ShapeDtypeStruct(shape, F32), jax.ShapeDtypeStruct(shape, BF16)],
        compiler_params=PARAMS,
        name="sum_tensor",
    )(keep, *shares)


def sum_kernel(one_ref, two_ref, out_ref):
    total = one_ref[...] + two_ref[...].astype(F32)
    out_ref[...] = total.astype(BF16).reshape(out_ref.shape)


def sum_shares(one, two, tokens):
    rows, width = one.shape
    return pl.pallas_call(
        sum_kernel,
        in_specs=[VMEM_SPEC] * 2,
        out_specs=VMEM_SPEC,
        out_shape=jax.ShapeDtypeStruct((rows // tokens, tokens, width), BF16),
        compiler_params=PARAMS,
        name="sum_shares",
    )(one, two)


def swap(value, axes):
    size = 2 ** len(axes)
    return lax.ppermute(value, axes, [(i, size - 1 - i) for i in range(size)])


def body(
    q_step,
    step_k,
    step_values,
    prefix_k,
    prefix_v,
    suffix_k,
    suffix_values,
    lengths,
    placement,
    output_weight,
):
    tokens = q_step.shape[1]
    indices = lax.axis_size("prompt")
    blocks = lax.axis_size("tensor") * 2
    place = placement[0]
    slots = place.shape[0]
    other = swap(q_step, ("core",))
    own, place_here = own_rows(placement, q_step)
    routed = route(place_here, own, other, indices)
    routed, prefix_k, prefix_v = lax.optimization_barrier((routed, prefix_k, prefix_v))
    k_other = swap(prefix_k, ("core",))
    v_other = swap(prefix_v, ("core",))
    arrived = lax.all_to_all(
        routed.reshape(indices * 2, 16, D), ("prompt", "xh"), split_axis=0, concat_axis=0, tiled=True
    )
    keep, to_core, to_xh = suffix_attention(
        lengths, q_step, step_k, step_values, suffix_k, suffix_values
    )
    near = swap(to_core, ("core",))
    parts = prefix_attention(
        arrived.reshape(indices, 2, 16, D), prefix_k, k_other, prefix_v, v_other
    )
    near, parts = lax.optimization_barrier((near, parts))
    far = swap(jnp.concatenate([to_xh, near[near.shape[0] // 2 :]], axis=0), ("xh",))
    returned = lax.all_to_all(
        parts.reshape(indices * 2, 16, D), ("prompt", "xh"), split_axis=0, concat_axis=0, tiled=True
    )
    upper, low_away, low_mine = stage_weight(output_weight, parts, blocks)
    columns = (place[:, None] * 4 + jnp.arange(tokens, dtype=jnp.int32)[None, :]).reshape(
        slots * tokens, 1
    )
    away, attention = merge_and_project(
        columns,
        returned.reshape(indices, 2, 16, D),
        collect_suffix(place_here, (keep, near, far), indices),
        upper,
        low_away,
    )
    away = swap(away, ("core",))
    stay = project(attention, upper, low_mine)
    keep_t, *shares = add_halves(stay, away)
    steps = blocks // 2
    shares = [
        lax.ppermute(shares[b - 1], "tensor", [(i, (i + b) % steps) for i in range(steps)])
        for b in (2, 1, 3)
    ]
    one, two = sum_tensor(keep_t, shares)
    return sum_shares(one, swap(two, ("xh",)), tokens)


def solution(mesh):
    sizes = mesh.shape
    fine = Mesh(
        mesh.devices.reshape(sizes["tensor"], sizes["prompt"], 2, sizes["cand"] // 2),
        ("tensor", "prompt", "xh", "core"),
    )
    slot = ("prompt", "xh", "core")
    cand = ("xh", "core")
    return jax.shard_map(
        body,
        mesh=fine,
        in_specs=(
            P(slot, None, "tensor"),
            P(slot, None, "tensor"),
            P(slot, None, "tensor"),
            P("prompt", cand, "tensor"),
            P("prompt", cand, "tensor"),
            P(slot, None, "tensor"),
            P(slot, None, "tensor"),
            P(slot),
            P("prompt", None),
            P(("tensor",) + cand, None),
        ),
        out_specs=P("prompt", None, ("tensor",) + cand),
        check_vma=False,
    )
```

```python
import math

import jax
import jax.numpy as jnp
from jax import lax
from jax.experimental import pallas as pl
from jax.experimental.pallas import tpu as pltpu
from jax.sharding import Mesh, PartitionSpec as P

D = 128
SCALE2 = 1.4426950408889634 / math.sqrt(D)
HIDDEN = -1e30
GROUP = 2
CHUNKS = 4
BLOCK = 2048
F32 = jnp.float32
BF16 = jnp.bfloat16
VMEM_LIMIT = 32 * 1024 * 1024

VMEM_SPEC = pl.BlockSpec(memory_space=pltpu.VMEM)
SMEM_SPEC = pl.BlockSpec(memory_space=pltpu.SMEM)
HBM_SPEC = pl.BlockSpec(memory_space=pltpu.HBM)
PARAMS = pltpu.CompilerParams(vmem_limit_bytes=VMEM_LIMIT)


def split_stat(level):
    high = level.astype(BF16).astype(F32)
    rest = level - high
    middle = rest.astype(BF16).astype(F32)
    low = rest - middle
    lane = lax.broadcasted_iota(jnp.int32, (level.shape[0], D), 1)
    return jnp.where(lane == 0, high, jnp.where(lane == 1, middle, jnp.where(lane == 2, low, 0.0)))


def join_stat(block):
    return block[..., 0:1] + block[..., 1:2] + block[..., 2:3]


def dot_t(a, b):
    return lax.dot_general(a, b, (((1,), (1,)), ((), ())), preferred_element_type=F32)


def dot(a, b):
    return lax.dot_general(a, b, (((1,), (0,)), ((), ())), preferred_element_type=F32)


def lower_rows(shape):
    return lax.broadcasted_iota(jnp.int32, shape, len(shape) - 2) < 4


def here():
    return tuple(lax.axis_index(name) for name in ("xh", "core", "tensor"))


def in_hbm(value):
    return pltpu.with_memory_space_constraint(value, pltpu.HBM)


def split_rows(q_ref, rows):
    slots, tokens, width = q_ref.shape
    for i in range(slots):
        wide = q_ref[i].astype(F32)
        for h in range(width // D):
            place = (h // 4) * 4 + (h % 2) * tokens
            rows[(h // 2) % 2, i, place : place + tokens, :] = wide[:, h * D : (h + 1) * D]


def head_rows(wide, tokens, core):
    pieces = []
    for j in range(4):
        h = 4 * (j // 2) + j % 2
        one = wide[:, h * D : (h + 1) * D]
        two = wide[:, (h + 2) * D : (h + 3) * D]
        pieces.append((j * tokens, jnp.where(core == 0, one, two)))
    return pieces


def own_kernel(place_hbm, q_hbm, rows, place_out, pick_ref, place_ref, mine_ref, sem):
    xh, core, _ = here()
    copies = (
        pltpu.make_async_copy(place_hbm, place_ref, sem.at[0]),
        pltpu.make_async_copy(q_hbm, mine_ref, sem.at[1]),
        pltpu.make_async_copy(place_hbm, place_out, sem.at[2]),
    )
    for copy in copies:
        copy.start()
    rows[...] = jnp.zeros_like(rows)
    for copy in copies:
        copy.wait()
    count, tokens, _ = q_hbm.shape
    for i in range(count):
        u = place_ref[0, (2 * xh + core) * count + i]
        for first, piece in head_rows(mine_ref[i].astype(F32), tokens, core):
            rows[u, first : first + tokens, :] = piece
    lane = lax.broadcasted_iota(jnp.int32, (1, D), 1)
    wanted = jnp.full((1, D), -1, jnp.int32)
    for i in range(count):
        u = place_ref[0, (2 * xh + 1 - core) * count + i]
        wanted = jnp.where(lane // 8 == i, 8 * u + lane % 8, wanted)
    row = lax.broadcasted_iota(jnp.int32, pick_ref.shape, 0)
    pick_ref[...] = jnp.where(row == wanted, 1.0, 0.0).astype(BF16)


def own_rows(placement, mine):
    slots = placement.shape[1]
    return pl.pallas_call(
        own_kernel,
        in_specs=[HBM_SPEC, HBM_SPEC],
        out_specs=[VMEM_SPEC] * 3,
        out_shape=[
            jax.ShapeDtypeStruct((slots, 8, D), F32),
            jax.ShapeDtypeStruct(placement.shape, jnp.int32),
            jax.ShapeDtypeStruct((slots * 8, D), BF16),
        ],
        scratch_shapes=[
            pltpu.SMEM(placement.shape, jnp.int32),
            pltpu.VMEM(mine.shape, BF16),
            pltpu.SemaphoreType.DMA((3,)),
        ],
        cost_estimate=pl.CostEstimate(
            flops=0, bytes_accessed=2 * 1024 * 1024, transcendentals=0
        ),
        compiler_params=PARAMS,
        name="own_rows",
    )(in_hbm(placement), in_hbm(mine))


def route_kernel(pick_ref, own_ref, other_ref, out_ref, rows):
    _, core, _ = here()
    count, tokens, _ = other_ref.shape
    rows[count:] = jnp.zeros((rows.shape[0] - count, 8, D), F32)
    for i in range(count):
        for first, piece in head_rows(other_ref[i].astype(F32), tokens, core):
            rows[i, first : first + tokens, :] = piece
    placed = dot(pick_ref[...], rows[...].reshape(D, D).astype(BF16))
    packed = own_ref[...].reshape(out_ref.shape[0], 16, D)
    packed = (packed + placed.reshape(out_ref.shape[0], 16, D)).astype(BF16)
    for j in range(out_ref.shape[1]):
        out_ref[:, j] = packed


def route(pick, own, other, indices):
    return pl.pallas_call(
        route_kernel,
        in_specs=[VMEM_SPEC] * 3,
        out_specs=VMEM_SPEC,
        out_shape=jax.ShapeDtypeStruct((indices, 2, 16, D), BF16),
        scratch_shapes=[pltpu.VMEM((D // 8, 8, D), F32)],
        compiler_params=PARAMS,
        name="route_queries",
    )(pick, own, other)


def suffix_kernel(len_hbm, q_hbm, sk_hbm, sv_hbm, k_hbm, v_hbm, *rest):
    me_ref = here()
    keep_ref, core_ref, xh_ref = rest[:3]
    len_ref, q_ref, sk_ref, sv_ref, rows_ref, keys, values, tiles, small_sem, sem = rest[3:]
    slots, span, _ = k_hbm.shape
    tokens = sk_hbm.shape[1]
    xh, core = me_ref[0], me_ref[1]
    lower = lower_rows((8, D))
    lengths_copy = pltpu.make_async_copy(len_hbm, len_ref, small_sem.at[0])
    lengths_copy.start()
    small = (
        pltpu.make_async_copy(q_hbm, q_ref, small_sem.at[1]),
        pltpu.make_async_copy(sk_hbm, sk_ref, small_sem.at[2]),
        pltpu.make_async_copy(sv_hbm, sv_ref, small_sem.at[3]),
    )

    def copies(i, b):
        part = pl.ds(b * BLOCK, BLOCK)
        return (
            pltpu.make_async_copy(k_hbm.at[i, part], keys.at[i, part], sem.at[0, i, b]),
            pltpu.make_async_copy(v_hbm.at[i, part], values.at[i, part], sem.at[1, i, b]),
        )

    for copy in copies(0, 0) + small:
        copy.start()
    lengths_copy.wait()
    blocks = span // BLOCK
    for i in range(slots):
        for b in range(blocks):
            if i + b > 0:

                @pl.when(b * BLOCK < len_ref[i])
                def _():
                    for copy in copies(i, b):
                        copy.start()

    for copy in small:
        copy.wait()
    split_rows(q_ref, rows_ref)
    rows = 16
    row_token = lax.broadcasted_iota(jnp.int32, (rows, tokens), 0) % tokens
    key_token = lax.broadcasted_iota(jnp.int32, (rows, tokens), 1)
    causal = key_token <= row_token
    position = lax.broadcasted_iota(jnp.int32, (rows, span), 1)
    for first in range(0, slots, GROUP):
        group = range(first, first + GROUP)
        for i in group:
            for b in range(blocks):
                if b == 0:
                    for copy in copies(i, b):
                        copy.wait()
                    continue
                live = b * BLOCK < len_ref[i]

                @pl.when(live)
                def _():
                    for copy in copies(i, b):
                        copy.wait()

                @pl.when(jnp.logical_not(live))
                def _():
                    values[i, b * BLOCK : (b + 1) * BLOCK, :] = jnp.zeros((BLOCK, D), BF16)

        q = [
            jnp.concatenate([rows_ref[0, i], rows_ref[1, i]], axis=0).astype(BF16) for i in group
        ]
        scores = [dot_t(q[n], keys[i]) for n, i in enumerate(group)]
        step_scores = [dot_t(q[n], sk_ref[i]) for n, i in enumerate(group)]
        scores = [
            jnp.where(position < len_ref[i], scores[n] * SCALE2, HIDDEN) for n, i in enumerate(group)
        ]
        step_scores = [jnp.where(causal, x * SCALE2, HIDDEN) for x in step_scores]
        top = [
            jnp.maximum(jnp.max(x, axis=1, keepdims=True), jnp.max(y, axis=1, keepdims=True))
            for x, y in zip(scores, step_scores)
        ]
        weights = [jnp.exp2(x - m) for x, m in zip(scores, top)]
        step_weights = [jnp.exp2(x - m) for x, m in zip(step_scores, top)]
        total = [
            jnp.sum(x, axis=1, keepdims=True) + jnp.sum(y, axis=1, keepdims=True)
            for x, y in zip(weights, step_weights)
        ]
        for n, i in enumerate(group):
            numer = dot(weights[n].astype(BF16), values[i])
            numer = numer + dot(step_weights[n].astype(BF16), sv_ref[i])
            value = numer / total[n]
            stat = split_stat(top[n] + jnp.log2(total[n]))
            for c in range(2):
                one, two = value[c * 8 : c * 8 + 8], stat[c * 8 : c * 8 + 8]
                tiles[c, i] = jnp.where(lower, one, pltpu.roll(two, 4, 0))
                tiles[2 + c, i] = jnp.where(lower, pltpu.roll(one, 4, 0), two)

    def piece(to_xh, to_core):
        return tiles[2 * to_xh + to_core].reshape(slots * 8, D).astype(BF16)

    keep_ref[...] = piece(xh, core)
    core_ref[...] = jnp.concatenate([piece(xh, 1 - core), piece(1 - xh, 1 - core)], axis=0)
    xh_ref[...] = piece(1 - xh, core)


def suffix_attention(lengths, q_step, step_k, step_values, suffix_k, suffix_values):
    slots, span, _ = suffix_k.shape
    rows = 16
    piece = jax.ShapeDtypeStruct((slots * 8, D), BF16)
    blocks = span // BLOCK
    return pl.pallas_call(
        suffix_kernel,
        in_specs=[HBM_SPEC] * 6,
        out_specs=[VMEM_SPEC] * 3,
        out_shape=[piece, jax.ShapeDtypeStruct((slots * 16, D), BF16), piece],
        scratch_shapes=[
            pltpu.SMEM(lengths.shape, jnp.int32),
            pltpu.VMEM(q_step.shape, BF16),
            pltpu.VMEM(step_k.shape, BF16),
            pltpu.VMEM(step_values.shape, BF16),
            pltpu.VMEM((2, slots, 8, D), F32),
            pltpu.VMEM((slots, span, D), BF16),
            pltpu.VMEM((slots, span, D), BF16),
            pltpu.VMEM((4, slots, 8, D), F32),
            pltpu.SemaphoreType.DMA((4,)),
            pltpu.SemaphoreType.DMA((2, slots, blocks)),
        ],
        cost_estimate=pl.CostEstimate(
            flops=4 * slots * rows * span * D * 64,
            bytes_accessed=4 * slots * span * D,
            transcendentals=slots * rows * span,
        ),
        compiler_params=PARAMS,
        name="suffix_attention",
    )(
        in_hbm(lengths),
        in_hbm(q_step),
        in_hbm(step_k),
        in_hbm(step_values),
        in_hbm(suffix_k),
        in_hbm(suffix_values),
    )


def prefix_kernel(q_ref, k_own, k_other, v_own, v_other, out_ref):
    indices = q_ref.shape[0]
    q_both = q_ref[:, 0].astype(F32) + q_ref[:, 1].astype(F32)
    q = [q_both[:, u * 8 : u * 8 + 8].reshape(indices * 8, D).astype(BF16) for u in range(2)]
    scores = [[dot_t(q[u], k[u]) * SCALE2 for k in (k_own, k_other)] for u in range(2)]
    top = [
        jnp.maximum(jnp.max(one, axis=1, keepdims=True), jnp.max(two, axis=1, keepdims=True))
        for one, two in scores
    ]
    weights = [[jnp.exp2(part - top[u]) for part in scores[u]] for u in range(2)]
    total = [sum(jnp.sum(part, axis=1, keepdims=True) for part in weights[u]) for u in range(2)]
    numer = [
        sum(dot(part.astype(BF16), v[u]) for part, v in zip(weights[u], (v_own, v_other)))
        for u in range(2)
    ]
    pair = [
        (
            (numer[u] / total[u]).reshape(indices, 8, D),
            split_stat(top[u] + jnp.log2(total[u])).reshape(indices, 8, D),
        )
        for u in range(2)
    ]
    lower = lower_rows((indices, 8, D))
    for j in range(2):
        halves = []
        for part in range(2):
            one, two = pair[0][part], pair[1][part]
            if j == 0:
                halves.append(jnp.where(lower, one, pltpu.roll(two, 4, 1)))
            else:
                halves.append(jnp.where(lower, pltpu.roll(one, 4, 1), two))
        out_ref[:, j] = jnp.concatenate(halves, axis=1).astype(BF16)


def prefix_attention(q_rows, k_own, k_other, v_own, v_other):
    return pl.pallas_call(
        prefix_kernel,
        in_specs=[VMEM_SPEC] * 5,
        out_specs=VMEM_SPEC,
        out_shape=jax.ShapeDtypeStruct(q_rows.shape, BF16),
        compiler_params=PARAMS,
        name="prefix_attention",
    )(q_rows, k_own, k_other, v_own, v_other)


def low_copies(me_ref, w_hbm, low_ref, sem, which):
    blocks, depth, width = low_ref.shape
    return [
        pltpu.make_async_copy(
            w_hbm.at[pl.ds(depth, depth), block_columns(me_ref, b, which, width)],
            low_ref.at[b],
            sem.at[b],
        )
        for b in range(blocks)
    ]


def stage_kernel(w_hbm, after_ref, upper_ref, low_ref, mine_hbm, mine_ref, *sems):
    me_ref = here()
    upper_sem, low_sem, mine_sem, out_sem = sems
    core = me_ref[1]
    chunk = upper_ref.shape[0] // CHUNKS
    mine = low_copies(me_ref, w_hbm, mine_ref, mine_sem, core)
    copies = low_copies(me_ref, w_hbm, low_ref, low_sem, 1 - core)
    for j in range(CHUNKS):
        part = pl.ds(j * chunk, chunk)
        copies.append(pltpu.make_async_copy(w_hbm.at[part], upper_ref.at[part], upper_sem.at[j]))
    for copy in mine + copies:
        copy.start()
    out = [
        pltpu.make_async_copy(mine_ref.at[b], mine_hbm.at[b], out_sem.at[b])
        for b in range(len(mine))
    ]
    for arrived, copy in zip(mine, out):
        arrived.wait()
        copy.start()
    for copy in copies + out:
        copy.wait()


def stage_weight(weight, after, blocks):
    depth, width = weight.shape
    low = (blocks, depth // 2, width // (2 * blocks))
    return pl.pallas_call(
        stage_kernel,
        in_specs=[HBM_SPEC, pl.BlockSpec(memory_space=pl.ANY)],
        out_specs=[VMEM_SPEC, VMEM_SPEC, HBM_SPEC],
        out_shape=[
            jax.ShapeDtypeStruct((depth // 2, width), BF16),
            jax.ShapeDtypeStruct(low, BF16),
            pltpu.HBM(low, BF16),
        ],
        scratch_shapes=[
            pltpu.VMEM(low, BF16),
            pltpu.SemaphoreType.DMA((CHUNKS,)),
            pltpu.SemaphoreType.DMA((blocks,)),
            pltpu.SemaphoreType.DMA((blocks,)),
            pltpu.SemaphoreType.DMA((blocks,)),
        ],
        cost_estimate=pl.CostEstimate(
            flops=0, bytes_accessed=5 * depth * width, transcendentals=0
        ),
        compiler_params=PARAMS,
        name="stage_weight",
    )(in_hbm(weight), after)


def block_columns(me_ref, step, which, width):
    ahead = (me_ref[2] + step // 2) % 4
    xh = me_ref[0] if step % 2 == 0 else 1 - me_ref[0]
    block = 4 * ahead + 2 * xh + which
    return pl.ds(pl.multiple_of(block * width, width), width)


def collect_kernel(place_ref, keep_ref, near_ref, far_ref, value_ref, level_ref, own):
    xh, core, _ = here()
    owners = value_ref.shape[0]
    count = keep_ref.shape[0] // 8
    pieces = ((keep_ref, 0, xh, core), (near_ref, 0, xh, 1 - core))
    pieces += ((far_ref, 0, 1 - xh, core), (far_ref, count, 1 - xh, 1 - core))
    for ref, start, from_xh, from_core in pieces:
        value = ref[start * 8 : (start + count) * 8, :].astype(F32)
        for i in range(count):
            slot = (2 * from_xh + from_core) * count + i
            own[place_ref[0, slot]] = value[i * 8 : (i + 1) * 8]
    lower = lower_rows((owners, 8, D))
    both = own[...].reshape(owners, 2, 8, D)
    one, two = both[:, 0], both[:, 1]
    value_ref[...] = jnp.where(lower, one, pltpu.roll(two, 4, 1))
    level = join_stat(jnp.where(lower, pltpu.roll(one, 4, 1), two))
    level_ref[...] = jnp.broadcast_to(level, level_ref.shape)


def collect_suffix(placement, pieces, owners):
    part = jax.ShapeDtypeStruct((owners, 8, D), F32)
    return pl.pallas_call(
        collect_kernel,
        in_specs=[SMEM_SPEC] + [VMEM_SPEC] * 3,
        out_specs=[VMEM_SPEC] * 2,
        out_shape=[part, part],
        scratch_shapes=[pltpu.VMEM((placement.shape[1], 8, D), F32)],
        cost_estimate=pl.CostEstimate(
            flops=0, bytes_accessed=1024 * 1024, transcendentals=0
        ),
        compiler_params=PARAMS,
        name="collect_suffix",
    )(placement, *pieces)


def merge_kernel(
    col_ref, parts_ref, value_ref, level_ref, upper_ref, low_ref, out_ref, att_ref
):
    me_ref = here()
    core = me_ref[1]
    blocks, out_rows, width = out_ref.shape
    owners = parts_ref.shape[0]
    values = [value_ref[...]]
    levels = [level_ref[...]]
    for c in range(parts_ref.shape[1]):
        block = parts_ref[:, c].astype(F32)
        values.append(block[:, 0:8])
        levels.append(jnp.broadcast_to(join_stat(block[:, 8:16]), level_ref.shape))
    top = levels[0]
    for level in levels[1:]:
        top = jnp.maximum(top, level)
    total = jnp.zeros_like(top)
    numer = jnp.zeros_like(values[0])
    for value, level in zip(values, levels):
        weight = jnp.exp2(level - top)
        total = total + weight
        numer = numer + value * weight
    merged = (numer / total).astype(BF16).reshape(owners * 8, D)
    lane = lax.broadcasted_iota(jnp.int32, (out_rows, owners * 8), 1)
    for h in range(2):
        pick = jnp.where(lane == col_ref[...] + 2 * h, 1.0, 0.0).astype(BF16)
        att_ref[:, h * D : (h + 1) * D] = dot(pick, merged).astype(BF16)
    half = low_ref.shape[1]
    for b in range(blocks):
        columns = block_columns(me_ref, b, 1 - core, width)
        value = dot(att_ref[:, 0:half], upper_ref[:, columns])
        out_ref[b] = (value + dot(att_ref[:, half:], low_ref[b])).astype(BF16)


def merge_and_project(columns, parts, suffix, upper, low):
    blocks, half, width = low.shape
    out_rows = columns.shape[0]
    return pl.pallas_call(
        merge_kernel,
        in_specs=[VMEM_SPEC] * 6,
        out_specs=[VMEM_SPEC, VMEM_SPEC],
        out_shape=[
            jax.ShapeDtypeStruct((blocks, out_rows, width), BF16),
            jax.ShapeDtypeStruct((out_rows, 2 * half), BF16),
        ],
        compiler_params=PARAMS,
        name="merge_and_project",
    )(columns, parts, *suffix, upper, low)


def project_kernel(att_ref, upper_ref, low_hbm, out_ref, low_ref, sem):
    me_ref = here()
    blocks, half, width = low_ref.shape
    copies = [
        pltpu.make_async_copy(low_hbm.at[b], low_ref.at[b], sem.at[b]) for b in range(blocks)
    ]
    for copy in copies:
        copy.start()
    for b in range(blocks):
        columns = block_columns(me_ref, b, me_ref[1], width)
        out_ref[b] = dot(att_ref[:, 0:half], upper_ref[:, columns])
    for copy in copies:
        copy.wait()
    for b in range(blocks):
        out_ref[b] += dot(att_ref[:, half:], low_ref[b])


def project(attention, upper, low):
    blocks, half, width = low.shape
    out_rows = attention.shape[0]
    return pl.pallas_call(
        project_kernel,
        in_specs=[VMEM_SPEC, VMEM_SPEC, HBM_SPEC],
        out_specs=VMEM_SPEC,
        out_shape=jax.ShapeDtypeStruct((blocks, out_rows, width), F32),
        scratch_shapes=[pltpu.VMEM(low.shape, BF16), pltpu.SemaphoreType.DMA((blocks,))],
        cost_estimate=pl.CostEstimate(
            flops=4 * out_rows * half * width * blocks * 8,
            bytes_accessed=4 * half * width * blocks,
            transcendentals=0,
        ),
        compiler_params=PARAMS,
        name="project",
    )(attention, upper, in_hbm(low))


def add_kernel(one_ref, two_ref, keep_ref, *out_refs):
    keep_ref[...] = one_ref[0:2] + two_ref[0:2].astype(F32)
    for b, out_ref in enumerate(out_refs, 1):
        value = one_ref[2 * b : 2 * b + 2] + two_ref[2 * b : 2 * b + 2].astype(F32)
        out_ref[...] = value.astype(BF16)


def add_halves(one, two):
    steps = one.shape[0] // 2
    shape = (2,) + one.shape[1:]
    return pl.pallas_call(
        add_kernel,
        in_specs=[VMEM_SPEC] * 2,
        out_specs=[VMEM_SPEC] * steps,
        out_shape=[jax.ShapeDtypeStruct(shape, F32)]
        + [jax.ShapeDtypeStruct(shape, BF16)] * (steps - 1),
        compiler_params=PARAMS,
        name="add_halves",
    )(one, two)


def tensor_kernel(keep_ref, *rest):
    in_refs, stay_ref, away_ref = rest[:-2], rest[-2], rest[-1]
    for away, out_ref in ((0, stay_ref), (1, away_ref)):
        total = keep_ref[away]
        for ref in in_refs:
            total = total + ref[away].astype(F32)
        out_ref[...] = total.astype(out_ref.dtype)


def sum_tensor(keep, shares):
    shape = keep.shape[1:]
    return pl.pallas_call(
        tensor_kernel,
        in_specs=[VMEM_SPEC] * (1 + len(shares)),
        out_specs=[VMEM_SPEC] * 2,
        out_shape=[jax.ShapeDtypeStruct(shape, F32), jax.ShapeDtypeStruct(shape, BF16)],
        compiler_params=PARAMS,
        name="sum_tensor",
    )(keep, *shares)


def sum_kernel(one_ref, two_ref, out_ref):
    total = one_ref[...] + two_ref[...].astype(F32)
    out_ref[...] = total.astype(BF16).reshape(out_ref.shape)


def sum_shares(one, two, tokens):
    rows, width = one.shape
    return pl.pallas_call(
        sum_kernel,
        in_specs=[VMEM_SPEC] * 2,
        out_specs=VMEM_SPEC,
        out_shape=jax.ShapeDtypeStruct((rows // tokens, tokens, width), BF16),
        compiler_params=PARAMS,
        name="sum_shares",
    )(one, two)


def swap(value, axes):
    size = 2 ** len(axes)
    return lax.ppermute(value, axes, [(i, size - 1 - i) for i in range(size)])


def body(
    q_step,
    step_k,
    step_values,
    prefix_k,
    prefix_v,
    suffix_k,
    suffix_values,
    lengths,
    placement,
    output_weight,
):
    tokens = q_step.shape[1]
    indices = lax.axis_size("prompt")
    blocks = lax.axis_size("tensor") * 2
    place = placement[0]
    slots = place.shape[0]
    other = swap(q_step, ("core",))
    own, place_here, pick = own_rows(placement, q_step)
    routed = route(pick, own, other, indices)
    routed, prefix_k, prefix_v = lax.optimization_barrier((routed, prefix_k, prefix_v))
    k_other = swap(prefix_k, ("core",))
    v_other = swap(prefix_v, ("core",))
    arrived = lax.all_to_all(
        routed.reshape(indices * 2, 16, D), ("prompt", "xh"), split_axis=0, concat_axis=0, tiled=True
    )
    keep, to_core, to_xh = suffix_attention(
        lengths, q_step, step_k, step_values, suffix_k, suffix_values
    )
    near = swap(to_core, ("core",))
    parts = prefix_attention(
        arrived.reshape(indices, 2, 16, D), prefix_k, k_other, prefix_v, v_other
    )
    near, parts = lax.optimization_barrier((near, parts))
    far = swap(jnp.concatenate([to_xh, near[near.shape[0] // 2 :]], axis=0), ("xh",))
    returned = lax.all_to_all(
        parts.reshape(indices * 2, 16, D), ("prompt", "xh"), split_axis=0, concat_axis=0, tiled=True
    )
    upper, low_away, low_mine = stage_weight(output_weight, parts, blocks)
    columns = (place[:, None] * 4 + jnp.arange(tokens, dtype=jnp.int32)[None, :]).reshape(
        slots * tokens, 1
    )
    away, attention = merge_and_project(
        columns,
        returned.reshape(indices, 2, 16, D),
        collect_suffix(place_here, (keep, near, far), indices),
        upper,
        low_away,
    )
    away = swap(away, ("core",))
    stay = project(attention, upper, low_mine)
    keep_t, *shares = add_halves(stay, away)
    steps = blocks // 2
    shares = [
        lax.ppermute(shares[b - 1], "tensor", [(i, (i + b) % steps) for i in range(steps)])
        for b in (2, 1, 3)
    ]
    one, two = sum_tensor(keep_t, shares)
    return sum_shares(one, swap(two, ("xh",)), tokens)


def solution(mesh):
    sizes = mesh.shape
    fine = Mesh(
        mesh.devices.reshape(sizes["tensor"], sizes["prompt"], 2, sizes["cand"] // 2),
        ("tensor", "prompt", "xh", "core"),
    )
    slot = ("prompt", "xh", "core")
    cand = ("xh", "core")
    return jax.shard_map(
        body,
        mesh=fine,
        in_specs=(
            P(slot, None, "tensor"),
            P(slot, None, "tensor"),
            P(slot, None, "tensor"),
            P("prompt", cand, "tensor"),
            P("prompt", cand, "tensor"),
            P(slot, None, "tensor"),
            P(slot, None, "tensor"),
            P(slot),
            P("prompt", None),
            P(("tensor",) + cand, None),
        ),
        out_specs=P("prompt", None, ("tensor",) + cand),
        check_vma=False,
    )
```

```python
import math

import jax
import jax.numpy as jnp
from jax import lax
from jax.experimental import pallas as pl
from jax.experimental.pallas import tpu as pltpu
from jax.sharding import Mesh, PartitionSpec as P

D = 128
SCALE2 = 1.4426950408889634 / math.sqrt(D)
HIDDEN = -1e30
GROUP = 2
CHUNKS = 4
BLOCK = 2048
F32 = jnp.float32
BF16 = jnp.bfloat16
VMEM_LIMIT = 32 * 1024 * 1024

VMEM_SPEC = pl.BlockSpec(memory_space=pltpu.VMEM)
SMEM_SPEC = pl.BlockSpec(memory_space=pltpu.SMEM)
HBM_SPEC = pl.BlockSpec(memory_space=pltpu.HBM)
PARAMS = pltpu.CompilerParams(vmem_limit_bytes=VMEM_LIMIT)


def split_stat(level):
    high = level.astype(BF16).astype(F32)
    rest = level - high
    middle = rest.astype(BF16).astype(F32)
    low = rest - middle
    lane = lax.broadcasted_iota(jnp.int32, (level.shape[0], D), 1)
    return jnp.where(lane == 0, high, jnp.where(lane == 1, middle, jnp.where(lane == 2, low, 0.0)))


def join_stat(block):
    return block[..., 0:1] + block[..., 1:2] + block[..., 2:3]


def dot_t(a, b):
    return lax.dot_general(a, b, (((1,), (1,)), ((), ())), preferred_element_type=F32)


def dot(a, b):
    return lax.dot_general(a, b, (((1,), (0,)), ((), ())), preferred_element_type=F32)


def lower_rows(shape):
    return lax.broadcasted_iota(jnp.int32, shape, len(shape) - 2) < 4


def here():
    return tuple(lax.axis_index(name) for name in ("xh", "core", "tensor"))


def in_hbm(value):
    return pltpu.with_memory_space_constraint(value, pltpu.HBM)


def split_rows(q_ref, rows):
    slots, tokens, width = q_ref.shape
    for i in range(slots):
        wide = q_ref[i].astype(F32)
        for h in range(width // D):
            place = (h // 4) * 4 + (h % 2) * tokens
            rows[(h // 2) % 2, i, place : place + tokens, :] = wide[:, h * D : (h + 1) * D]


def head_rows(wide, tokens, core):
    pieces = []
    for j in range(4):
        h = 4 * (j // 2) + j % 2
        one = wide[:, h * D : (h + 1) * D]
        two = wide[:, (h + 2) * D : (h + 3) * D]
        pieces.append((j * tokens, jnp.where(core == 0, one, two)))
    return pieces


def own_kernel(place_hbm, q_hbm, rows, place_out, pick_ref, place_ref, mine_ref, sem):
    xh, core, _ = here()
    copies = (
        pltpu.make_async_copy(place_hbm, place_ref, sem.at[0]),
        pltpu.make_async_copy(q_hbm, mine_ref, sem.at[1]),
        pltpu.make_async_copy(place_hbm, place_out, sem.at[2]),
    )
    for copy in copies:
        copy.start()
    rows[...] = jnp.zeros_like(rows)
    for copy in copies:
        copy.wait()
    count, tokens, _ = q_hbm.shape
    for i in range(count):
        u = place_ref[0, (2 * xh + core) * count + i]
        for first, piece in head_rows(mine_ref[i].astype(F32), tokens, core):
            rows[u, first : first + tokens, :] = piece
    lane = lax.broadcasted_iota(jnp.int32, (1, D), 1)
    wanted = jnp.full((1, D), -1, jnp.int32)
    for i in range(count):
        u = place_ref[0, (2 * xh + 1 - core) * count + i]
        wanted = jnp.where(lane // 8 == i, 8 * u + lane % 8, wanted)
    row = lax.broadcasted_iota(jnp.int32, pick_ref.shape, 0)
    pick_ref[...] = jnp.where(row == wanted, 1.0, 0.0).astype(BF16)


def own_rows(placement, mine):
    slots = placement.shape[1]
    return pl.pallas_call(
        own_kernel,
        in_specs=[HBM_SPEC, HBM_SPEC],
        out_specs=[VMEM_SPEC] * 3,
        out_shape=[
            jax.ShapeDtypeStruct((slots, 8, D), F32),
            jax.ShapeDtypeStruct(placement.shape, jnp.int32),
            jax.ShapeDtypeStruct((slots * 8, D), BF16),
        ],
        scratch_shapes=[
            pltpu.SMEM(placement.shape, jnp.int32),
            pltpu.VMEM(mine.shape, BF16),
            pltpu.SemaphoreType.DMA((3,)),
        ],
        cost_estimate=pl.CostEstimate(
            flops=0, bytes_accessed=2 * 1024 * 1024, transcendentals=0
        ),
        compiler_params=PARAMS,
        name="own_rows",
    )(in_hbm(placement), in_hbm(mine))


def route_kernel(pick_ref, own_ref, other_ref, out_ref, rows):
    _, core, _ = here()
    count, tokens, _ = other_ref.shape
    rows[count:] = jnp.zeros((rows.shape[0] - count, 8, D), F32)
    for i in range(count):
        for first, piece in head_rows(other_ref[i].astype(F32), tokens, core):
            rows[i, first : first + tokens, :] = piece
    placed = dot(pick_ref[...], rows[...].reshape(D, D).astype(BF16))
    packed = own_ref[...].reshape(out_ref.shape[0], 16, D)
    packed = (packed + placed.reshape(out_ref.shape[0], 16, D)).astype(BF16)
    for j in range(out_ref.shape[1]):
        out_ref[:, j] = packed


def route(pick, own, other, indices):
    return pl.pallas_call(
        route_kernel,
        in_specs=[VMEM_SPEC] * 3,
        out_specs=VMEM_SPEC,
        out_shape=jax.ShapeDtypeStruct((indices, 2, 16, D), BF16),
        scratch_shapes=[pltpu.VMEM((D // 8, 8, D), F32)],
        compiler_params=PARAMS,
        name="route_queries",
    )(pick, own, other)


def suffix_kernel(len_hbm, q_hbm, sk_hbm, sv_hbm, k_hbm, v_hbm, *rest):
    me_ref = here()
    keep_ref, core_ref, xh_ref = rest[:3]
    len_ref, q_ref, sk_ref, sv_ref, rows_ref, keys, values, tiles, small_sem, sem = rest[3:]
    slots, span, _ = k_hbm.shape
    tokens = sk_hbm.shape[1]
    xh, core = me_ref[0], me_ref[1]
    lower = lower_rows((8, D))
    lengths_copy = pltpu.make_async_copy(len_hbm, len_ref, small_sem.at[0])
    lengths_copy.start()
    small = (
        pltpu.make_async_copy(q_hbm, q_ref, small_sem.at[1]),
        pltpu.make_async_copy(sk_hbm, sk_ref, small_sem.at[2]),
        pltpu.make_async_copy(sv_hbm, sv_ref, small_sem.at[3]),
    )

    def copies(i, b):
        part = pl.ds(b * BLOCK, BLOCK)
        return (
            pltpu.make_async_copy(k_hbm.at[i, part], keys.at[i, part], sem.at[0, i, b]),
            pltpu.make_async_copy(v_hbm.at[i, part], values.at[i, part], sem.at[1, i, b]),
        )

    for copy in copies(0, 0) + small:
        copy.start()
    lengths_copy.wait()
    blocks = span // BLOCK
    for i in range(slots):
        for b in range(blocks):
            if i + b > 0:

                @pl.when(b * BLOCK < len_ref[i])
                def _():
                    for copy in copies(i, b):
                        copy.start()

    for copy in small:
        copy.wait()
    split_rows(q_ref, rows_ref)
    rows = 16
    row_token = lax.broadcasted_iota(jnp.int32, (rows, tokens), 0) % tokens
    key_token = lax.broadcasted_iota(jnp.int32, (rows, tokens), 1)
    causal = key_token <= row_token
    position = lax.broadcasted_iota(jnp.int32, (rows, span), 1)
    for first in range(0, slots, GROUP):
        group = range(first, first + GROUP)
        for i in group:
            for b in range(blocks):
                if b == 0:
                    for copy in copies(i, b):
                        copy.wait()
                    continue
                live = b * BLOCK < len_ref[i]

                @pl.when(live)
                def _():
                    for copy in copies(i, b):
                        copy.wait()

                @pl.when(jnp.logical_not(live))
                def _():
                    values[i, b * BLOCK : (b + 1) * BLOCK, :] = jnp.zeros((BLOCK, D), BF16)

        q = [
            jnp.concatenate([rows_ref[0, i], rows_ref[1, i]], axis=0).astype(BF16) for i in group
        ]
        scores = [dot_t(q[n], keys[i]) for n, i in enumerate(group)]
        step_scores = [dot_t(q[n], sk_ref[i]) for n, i in enumerate(group)]
        scores = [
            jnp.where(position < len_ref[i], scores[n] * SCALE2, HIDDEN) for n, i in enumerate(group)
        ]
        step_scores = [jnp.where(causal, x * SCALE2, HIDDEN) for x in step_scores]
        top = [
            jnp.maximum(jnp.max(x, axis=1, keepdims=True), jnp.max(y, axis=1, keepdims=True))
            for x, y in zip(scores, step_scores)
        ]
        weights = [jnp.exp2(x - m) for x, m in zip(scores, top)]
        step_weights = [jnp.exp2(x - m) for x, m in zip(step_scores, top)]
        total = [
            jnp.sum(x, axis=1, keepdims=True) + jnp.sum(y, axis=1, keepdims=True)
            for x, y in zip(weights, step_weights)
        ]
        for n, i in enumerate(group):
            numer = dot(weights[n].astype(BF16), values[i])
            numer = numer + dot(step_weights[n].astype(BF16), sv_ref[i])
            value = numer / total[n]
            stat = split_stat(top[n] + jnp.log2(total[n]))
            for c in range(2):
                one, two = value[c * 8 : c * 8 + 8], stat[c * 8 : c * 8 + 8]
                tiles[c, i] = jnp.where(lower, one, pltpu.roll(two, 4, 0))
                tiles[2 + c, i] = jnp.where(lower, pltpu.roll(one, 4, 0), two)

    def piece(to_xh, to_core):
        return tiles[2 * to_xh + to_core].reshape(slots * 8, D).astype(BF16)

    keep_ref[...] = piece(xh, core)
    core_ref[...] = jnp.concatenate([piece(xh, 1 - core), piece(1 - xh, 1 - core)], axis=0)
    xh_ref[...] = piece(1 - xh, core)


def suffix_attention(lengths, q_step, step_k, step_values, suffix_k, suffix_values):
    slots, span, _ = suffix_k.shape
    rows = 16
    piece = jax.ShapeDtypeStruct((slots * 8, D), BF16)
    blocks = span // BLOCK
    return pl.pallas_call(
        suffix_kernel,
        in_specs=[HBM_SPEC] * 6,
        out_specs=[VMEM_SPEC] * 3,
        out_shape=[piece, jax.ShapeDtypeStruct((slots * 16, D), BF16), piece],
        scratch_shapes=[
            pltpu.SMEM(lengths.shape, jnp.int32),
            pltpu.VMEM(q_step.shape, BF16),
            pltpu.VMEM(step_k.shape, BF16),
            pltpu.VMEM(step_values.shape, BF16),
            pltpu.VMEM((2, slots, 8, D), F32),
            pltpu.VMEM((slots, span, D), BF16),
            pltpu.VMEM((slots, span, D), BF16),
            pltpu.VMEM((4, slots, 8, D), F32),
            pltpu.SemaphoreType.DMA((4,)),
            pltpu.SemaphoreType.DMA((2, slots, blocks)),
        ],
        cost_estimate=pl.CostEstimate(
            flops=4 * slots * rows * span * D * 64,
            bytes_accessed=4 * slots * span * D,
            transcendentals=slots * rows * span,
        ),
        compiler_params=PARAMS,
        name="suffix_attention",
    )(
        in_hbm(lengths),
        in_hbm(q_step),
        in_hbm(step_k),
        in_hbm(step_values),
        in_hbm(suffix_k),
        in_hbm(suffix_values),
    )


def prefix_kernel(q_ref, k_own, k_other, v_own, v_other, out_ref):
    indices = q_ref.shape[0]
    q_both = q_ref[:, 0].astype(F32) + q_ref[:, 1].astype(F32)
    q = [q_both[:, u * 8 : u * 8 + 8].reshape(indices * 8, D).astype(BF16) for u in range(2)]
    scores = [[dot_t(q[u], k[u]) * SCALE2 for k in (k_own, k_other)] for u in range(2)]
    top = [
        jnp.maximum(jnp.max(one, axis=1, keepdims=True), jnp.max(two, axis=1, keepdims=True))
        for one, two in scores
    ]
    weights = [[jnp.exp2(part - top[u]) for part in scores[u]] for u in range(2)]
    total = [sum(jnp.sum(part, axis=1, keepdims=True) for part in weights[u]) for u in range(2)]
    numer = [
        sum(dot(part.astype(BF16), v[u]) for part, v in zip(weights[u], (v_own, v_other)))
        for u in range(2)
    ]
    pair = [
        (
            (numer[u] / total[u]).reshape(indices, 8, D),
            split_stat(top[u] + jnp.log2(total[u])).reshape(indices, 8, D),
        )
        for u in range(2)
    ]
    lower = lower_rows((indices, 8, D))
    for j in range(2):
        halves = []
        for part in range(2):
            one, two = pair[0][part], pair[1][part]
            if j == 0:
                halves.append(jnp.where(lower, one, pltpu.roll(two, 4, 1)))
            else:
                halves.append(jnp.where(lower, pltpu.roll(one, 4, 1), two))
        out_ref[:, j] = jnp.concatenate(halves, axis=1).astype(BF16)


def prefix_attention(q_rows, k_own, k_other, v_own, v_other):
    return pl.pallas_call(
        prefix_kernel,
        in_specs=[VMEM_SPEC] * 5,
        out_specs=VMEM_SPEC,
        out_shape=jax.ShapeDtypeStruct(q_rows.shape, BF16),
        compiler_params=PARAMS,
        name="prefix_attention",
    )(q_rows, k_own, k_other, v_own, v_other)


def low_copies(me_ref, w_hbm, low_ref, sem, which):
    blocks, depth, width = low_ref.shape
    return [
        pltpu.make_async_copy(
            w_hbm.at[pl.ds(depth, depth), block_columns(me_ref, b, which, width)],
            low_ref.at[b],
            sem.at[b],
        )
        for b in range(blocks)
    ]


def stage_kernel(w_hbm, after_ref, upper_ref, low_ref, mine_hbm, mine_ref, *sems):
    me_ref = here()
    upper_sem, low_sem, mine_sem, out_sem = sems
    core = me_ref[1]
    chunk = upper_ref.shape[0] // CHUNKS
    mine = low_copies(me_ref, w_hbm, mine_ref, mine_sem, core)
    copies = low_copies(me_ref, w_hbm, low_ref, low_sem, 1 - core)
    for j in range(CHUNKS):
        part = pl.ds(j * chunk, chunk)
        copies.append(pltpu.make_async_copy(w_hbm.at[part], upper_ref.at[part], upper_sem.at[j]))
    for copy in mine + copies:
        copy.start()
    out = [
        pltpu.make_async_copy(mine_ref.at[b], mine_hbm.at[b], out_sem.at[b])
        for b in range(len(mine))
    ]
    for arrived, copy in zip(mine, out):
        arrived.wait()
        copy.start()
    for copy in copies + out:
        copy.wait()


def stage_weight(weight, after, blocks):
    depth, width = weight.shape
    low = (blocks, depth // 2, width // (2 * blocks))
    return pl.pallas_call(
        stage_kernel,
        in_specs=[HBM_SPEC, pl.BlockSpec(memory_space=pl.ANY)],
        out_specs=[VMEM_SPEC, VMEM_SPEC, HBM_SPEC],
        out_shape=[
            jax.ShapeDtypeStruct((depth // 2, width), BF16),
            jax.ShapeDtypeStruct(low, BF16),
            pltpu.HBM(low, BF16),
        ],
        scratch_shapes=[
            pltpu.VMEM(low, BF16),
            pltpu.SemaphoreType.DMA((CHUNKS,)),
            pltpu.SemaphoreType.DMA((blocks,)),
            pltpu.SemaphoreType.DMA((blocks,)),
            pltpu.SemaphoreType.DMA((blocks,)),
        ],
        cost_estimate=pl.CostEstimate(
            flops=0, bytes_accessed=5 * depth * width, transcendentals=0
        ),
        compiler_params=PARAMS,
        name="stage_weight",
    )(in_hbm(weight), after)


def block_columns(me_ref, step, which, width):
    ahead = (me_ref[2] + step // 2) % 4
    xh = me_ref[0] if step % 2 == 0 else 1 - me_ref[0]
    block = 4 * ahead + 2 * xh + which
    return pl.ds(pl.multiple_of(block * width, width), width)


def collect_kernel(
    place_ref, col_ref, keep_ref, near_ref, far_ref, value_ref, level_ref, pick_ref, own
):
    xh, core, _ = here()
    owners = value_ref.shape[0]
    count = keep_ref.shape[0] // 8
    pieces = ((keep_ref, 0, xh, core), (near_ref, 0, xh, 1 - core))
    pieces += ((far_ref, 0, 1 - xh, core), (far_ref, count, 1 - xh, 1 - core))
    for ref, start, from_xh, from_core in pieces:
        value = ref[start * 8 : (start + count) * 8, :].astype(F32)
        for i in range(count):
            slot = (2 * from_xh + from_core) * count + i
            own[place_ref[0, slot]] = value[i * 8 : (i + 1) * 8]
    lower = lower_rows((owners, 8, D))
    both = own[...].reshape(owners, 2, 8, D)
    one, two = both[:, 0], both[:, 1]
    value_ref[...] = jnp.where(lower, one, pltpu.roll(two, 4, 1))
    level = join_stat(jnp.where(lower, pltpu.roll(one, 4, 1), two))
    level_ref[...] = jnp.broadcast_to(level, level_ref.shape)
    lane = lax.broadcasted_iota(jnp.int32, pick_ref.shape[1:], 1)
    for h in range(2):
        pick_ref[h] = jnp.where(lane == col_ref[...] + 2 * h, 1.0, 0.0).astype(BF16)


def collect_suffix(placement, columns, pieces, owners):
    part = jax.ShapeDtypeStruct((owners, 8, D), F32)
    return pl.pallas_call(
        collect_kernel,
        in_specs=[SMEM_SPEC] + [VMEM_SPEC] * 4,
        out_specs=[VMEM_SPEC] * 3,
        out_shape=[
            part,
            part,
            jax.ShapeDtypeStruct((2, columns.shape[0], owners * 8), BF16),
        ],
        scratch_shapes=[pltpu.VMEM((placement.shape[1], 8, D), F32)],
        cost_estimate=pl.CostEstimate(
            flops=0, bytes_accessed=1024 * 1024, transcendentals=0
        ),
        compiler_params=PARAMS,
        name="collect_suffix",
    )(placement, columns, *pieces)


def merge_kernel(
    parts_ref, value_ref, level_ref, pick_ref, upper_ref, low_ref, out_ref, att_ref
):
    me_ref = here()
    core = me_ref[1]
    blocks, out_rows, width = out_ref.shape
    owners = parts_ref.shape[0]
    values = [value_ref[...]]
    levels = [level_ref[...]]
    for c in range(parts_ref.shape[1]):
        block = parts_ref[:, c].astype(F32)
        values.append(block[:, 0:8])
        levels.append(jnp.broadcast_to(join_stat(block[:, 8:16]), level_ref.shape))
    top = levels[0]
    for level in levels[1:]:
        top = jnp.maximum(top, level)
    total = jnp.zeros_like(top)
    numer = jnp.zeros_like(values[0])
    for value, level in zip(values, levels):
        weight = jnp.exp2(level - top)
        total = total + weight
        numer = numer + value * weight
    merged = (numer / total).astype(BF16).reshape(owners * 8, D)
    for h in range(2):
        att_ref[:, h * D : (h + 1) * D] = dot(pick_ref[h], merged).astype(BF16)
    half = low_ref.shape[1]
    for b in range(blocks):
        columns = block_columns(me_ref, b, 1 - core, width)
        value = dot(att_ref[:, 0:half], upper_ref[:, columns])
        out_ref[b] = (value + dot(att_ref[:, half:], low_ref[b])).astype(BF16)


def merge_and_project(out_rows, parts, suffix, upper, low):
    blocks, half, width = low.shape
    return pl.pallas_call(
        merge_kernel,
        in_specs=[VMEM_SPEC] * 6,
        out_specs=[VMEM_SPEC, VMEM_SPEC],
        out_shape=[
            jax.ShapeDtypeStruct((blocks, out_rows, width), BF16),
            jax.ShapeDtypeStruct((out_rows, 2 * half), BF16),
        ],
        compiler_params=PARAMS,
        name="merge_and_project",
    )(parts, *suffix, upper, low)


def project_kernel(att_ref, upper_ref, low_hbm, out_ref, low_ref, sem):
    me_ref = here()
    blocks, half, width = low_ref.shape
    copies = [
        pltpu.make_async_copy(low_hbm.at[b], low_ref.at[b], sem.at[b]) for b in range(blocks)
    ]
    for copy in copies:
        copy.start()
    for b in range(blocks):
        columns = block_columns(me_ref, b, me_ref[1], width)
        out_ref[b] = dot(att_ref[:, 0:half], upper_ref[:, columns])
    for copy in copies:
        copy.wait()
    for b in range(blocks):
        out_ref[b] += dot(att_ref[:, half:], low_ref[b])


def project(attention, upper, low):
    blocks, half, width = low.shape
    out_rows = attention.shape[0]
    return pl.pallas_call(
        project_kernel,
        in_specs=[VMEM_SPEC, VMEM_SPEC, HBM_SPEC],
        out_specs=VMEM_SPEC,
        out_shape=jax.ShapeDtypeStruct((blocks, out_rows, width), F32),
        scratch_shapes=[pltpu.VMEM(low.shape, BF16), pltpu.SemaphoreType.DMA((blocks,))],
        cost_estimate=pl.CostEstimate(
            flops=4 * out_rows * half * width * blocks * 8,
            bytes_accessed=4 * half * width * blocks,
            transcendentals=0,
        ),
        compiler_params=PARAMS,
        name="project",
    )(attention, upper, in_hbm(low))


def add_kernel(one_ref, two_ref, keep_ref, *out_refs):
    keep_ref[...] = one_ref[0:2] + two_ref[0:2].astype(F32)
    for b, out_ref in enumerate(out_refs, 1):
        value = one_ref[2 * b : 2 * b + 2] + two_ref[2 * b : 2 * b + 2].astype(F32)
        out_ref[...] = value.astype(BF16)


def add_halves(one, two):
    steps = one.shape[0] // 2
    shape = (2,) + one.shape[1:]
    return pl.pallas_call(
        add_kernel,
        in_specs=[VMEM_SPEC] * 2,
        out_specs=[VMEM_SPEC] * steps,
        out_shape=[jax.ShapeDtypeStruct(shape, F32)]
        + [jax.ShapeDtypeStruct(shape, BF16)] * (steps - 1),
        compiler_params=PARAMS,
        name="add_halves",
    )(one, two)


def tensor_kernel(keep_ref, *rest):
    in_refs, stay_ref, away_ref = rest[:-2], rest[-2], rest[-1]
    for away, out_ref in ((0, stay_ref), (1, away_ref)):
        total = keep_ref[away]
        for ref in in_refs:
            total = total + ref[away].astype(F32)
        out_ref[...] = total.astype(out_ref.dtype)


def sum_tensor(keep, shares):
    shape = keep.shape[1:]
    return pl.pallas_call(
        tensor_kernel,
        in_specs=[VMEM_SPEC] * (1 + len(shares)),
        out_specs=[VMEM_SPEC] * 2,
        out_shape=[jax.ShapeDtypeStruct(shape, F32), jax.ShapeDtypeStruct(shape, BF16)],
        compiler_params=PARAMS,
        name="sum_tensor",
    )(keep, *shares)


def sum_kernel(one_ref, two_ref, out_ref):
    total = one_ref[...] + two_ref[...].astype(F32)
    out_ref[...] = total.astype(BF16).reshape(out_ref.shape)


def sum_shares(one, two, tokens):
    rows, width = one.shape
    return pl.pallas_call(
        sum_kernel,
        in_specs=[VMEM_SPEC] * 2,
        out_specs=VMEM_SPEC,
        out_shape=jax.ShapeDtypeStruct((rows // tokens, tokens, width), BF16),
        compiler_params=PARAMS,
        name="sum_shares",
    )(one, two)


def swap(value, axes):
    size = 2 ** len(axes)
    return lax.ppermute(value, axes, [(i, size - 1 - i) for i in range(size)])


def body(
    q_step,
    step_k,
    step_values,
    prefix_k,
    prefix_v,
    suffix_k,
    suffix_values,
    lengths,
    placement,
    output_weight,
):
    tokens = q_step.shape[1]
    indices = lax.axis_size("prompt")
    blocks = lax.axis_size("tensor") * 2
    place = placement[0]
    slots = place.shape[0]
    other = swap(q_step, ("core",))
    own, place_here, pick = own_rows(placement, q_step)
    routed = route(pick, own, other, indices)
    routed, prefix_k, prefix_v = lax.optimization_barrier((routed, prefix_k, prefix_v))
    k_other = swap(prefix_k, ("core",))
    v_other = swap(prefix_v, ("core",))
    arrived = lax.all_to_all(
        routed.reshape(indices * 2, 16, D), ("prompt", "xh"), split_axis=0, concat_axis=0, tiled=True
    )
    keep, to_core, to_xh = suffix_attention(
        lengths, q_step, step_k, step_values, suffix_k, suffix_values
    )
    near = swap(to_core, ("core",))
    parts = prefix_attention(
        arrived.reshape(indices, 2, 16, D), prefix_k, k_other, prefix_v, v_other
    )
    near, parts = lax.optimization_barrier((near, parts))
    far = swap(jnp.concatenate([to_xh, near[near.shape[0] // 2 :]], axis=0), ("xh",))
    returned = lax.all_to_all(
        parts.reshape(indices * 2, 16, D), ("prompt", "xh"), split_axis=0, concat_axis=0, tiled=True
    )
    upper, low_away, low_mine = stage_weight(output_weight, parts, blocks)
    columns = (place[:, None] * 4 + jnp.arange(tokens, dtype=jnp.int32)[None, :]).reshape(
        slots * tokens, 1
    )
    away, attention = merge_and_project(
        slots * tokens,
        returned.reshape(indices, 2, 16, D),
        collect_suffix(place_here, columns, (keep, near, far), indices),
        upper,
        low_away,
    )
    away = swap(away, ("core",))
    stay = project(attention, upper, low_mine)
    keep_t, *shares = add_halves(stay, away)
    steps = blocks // 2
    shares = [
        lax.ppermute(shares[b - 1], "tensor", [(i, (i + b) % steps) for i in range(steps)])
        for b in (2, 1, 3)
    ]
    one, two = sum_tensor(keep_t, shares)
    return sum_shares(one, swap(two, ("xh",)), tokens)


def solution(mesh):
    sizes = mesh.shape
    fine = Mesh(
        mesh.devices.reshape(sizes["tensor"], sizes["prompt"], 2, sizes["cand"] // 2),
        ("tensor", "prompt", "xh", "core"),
    )
    slot = ("prompt", "xh", "core")
    cand = ("xh", "core")
    return jax.shard_map(
        body,
        mesh=fine,
        in_specs=(
            P(slot, None, "tensor"),
            P(slot, None, "tensor"),
            P(slot, None, "tensor"),
            P("prompt", cand, "tensor"),
            P("prompt", cand, "tensor"),
            P(slot, None, "tensor"),
            P(slot, None, "tensor"),
            P(slot),
            P("prompt", None),
            P(("tensor",) + cand, None),
        ),
        out_specs=P("prompt", None, ("tensor",) + cand),
        check_vma=False,
    )
```
